32 devices in a mesh: replica: 8 (over y, x, core), group: 4 (over z).
Axes of the slice: x: 2, y: 2, z: 4, core: 2. Of those that a mesh axis runs over, the one named last changes fastest.
Arguments:
- images: bfloat16 [160, 197, 512], P(('replica', 'group')), may hold values from -6 to 6
- attn_norm_gain: bfloat16 [512], P('group'), may hold values from 0.5 to 1.5
- attn_norm_bias: bfloat16 [512], P('group'), may hold values from -1.1953125 to 1.1953125
- qkv_weight: bfloat16 [512, 1536], P('group'), may hold values from -0.25 to 0.25
- query_value_bias: bfloat16 [1024], P('group'), may hold values from -1.1953125 to 1.1953125
- proj_weight: bfloat16 [512, 512], P('group'), may hold values from -2 to 2
- proj_bias: bfloat16 [512], P('group'), may hold values from -1.1953125 to 1.1953125
- moe_norm_gain: bfloat16 [512], P('group'), may hold values from 0.5 to 1.5
- moe_norm_bias: bfloat16 [512], P('group'), may hold values from -1.1953125 to 1.1953125
- router_weight: bfloat16 [512, 4], P('group'), may hold values from -0.1875 to 0.1875
- expert_inner: bfloat16 [4, 512, 2048], P('group'), may hold values from -0.25 to 0.25
- expert_inner_bias: bfloat16 [4, 2048], P('group'), may hold values from -0.8984375 to 0.8984375
- expert_outer: bfloat16 [4, 2048, 512], P('group'), may hold values from -0.5 to 0.5
- expert_outer_bias: bfloat16 [4, 512], P('group'), may hold values from -1.796875 to 1.796875
- live_count: int32 [32], P(('replica', 'group')), may hold values from 3 to 5, as said below
- routes: int32 [160, 197, 2], P(('replica', 'group')), may hold values from 0 to 3, as said below
- slot_ids: int32 [160, 197, 2], P(('replica', 'group')), may hold values from -1 to 639, as said below
- cotangent: bfloat16 [160, 197, 512], P(('replica', 'group')), may hold values from -6 to 6
Outputs:
- block_out: bfloat16 [160, 197, 512], P(('replica', 'group'))
- input_grad: float32 [160, 197, 512], P(('replica', 'group'))
- grad_attn_norm_gain: float32 [512], P('group')
- grad_attn_norm_bias: float32 [512], P('group')
- grad_qkv_weight: float32 [512, 1536], P('group')
- grad_query_value_bias: float32 [1024], P('group')
- grad_proj_weight: float32 [512, 512], P('group')
- grad_proj_bias: float32 [512], P('group')
- grad_moe_norm_gain: float32 [512], P('group')
- grad_moe_norm_bias: float32 [512], P('group')
- grad_router_weight: float32 [512, 4], P('group')
- grad_expert_inner: float32 [4, 512, 2048], P('group')
- grad_expert_inner_bias: float32 [4, 2048], P('group')
- grad_expert_outer: float32 [4, 2048, 512], P('group')
- grad_expert_outer_bias: float32 [4, 512], P('group')
The draws below stay inside these ranges and needn't reach their ends.
Inputs may be any that keep to these rules, and one draw needn't show every extreme that they name: Each device holds 5 image slots; the first live_count of them are images, the others padding whose outputs are zero; some device is full in every draw. `routes`: every token names two different experts. `slot_ids`: on each device and for each expert, the routes of live tokens to that expert take the slots 0, 1, 2, ... in order of token and then of choice; -1 marks a route of a padding image or one after the expert's 640 slots on that device are full.
All inputs are finite; a program needn't handle non-finite values.
Results may differ from the reference program's by a relative error of at most 0.017.
Values may be sent and summed in bfloat16 or wider, within the bound.
No kernel may reach another device: no remote copies, remote signals or barrier semaphores. Data moves between devices by JAX's collectives and lax.ppermute only.
A program may use at most 256 MiB of HBM per device.

```python
import math
import jax
import jax.numpy as jnp
from jax import lax

D = 512
HEADS = 8
F = 2048
E = 4
S = 197
IMG_DEV = 5
CAP = 640
IMAGES = 160
N_REPLICA = 8
N_GROUP = 4


def routing_tables(key):
    device_total = IMAGES // IMG_DEV
    row_count = IMG_DEV * S
    subkeys = jax.random.split(key, 6)
    counts = jax.random.randint(subkeys[0], (device_total,), IMG_DEV // 2 + 1, IMG_DEV + 1)
    fullest = jax.random.randint(subkeys[1], (), 0, device_total)
    counts = jnp.where(jnp.arange(device_total) == fullest, IMG_DEV, counts).astype(jnp.int32)
    favored = jax.random.randint(subkeys[2], (device_total, 1), 0, E)
    leaning = jax.random.randint(subkeys[3], (device_total, row_count), 0, 100) < 45
    firsts = jnp.where(leaning, favored, jax.random.randint(subkeys[4], (device_total, row_count), 0, E))
    seconds = (firsts + jax.random.randint(subkeys[5], (device_total, row_count), 1, E)) % E
    paired = jnp.stack([firsts, seconds], axis=-1)
    live_rows = (jnp.arange(row_count) // S)[None, :] < counts[:, None]
    matches = ((paired[..., None] == jnp.arange(E)) & live_rows[:, :, None, None]).astype(jnp.int32)
    running = jnp.cumsum(matches.reshape(device_total, row_count * 2, E), axis=1).reshape(device_total, row_count, 2, E) - 1
    ranking = jnp.sum(running * matches, axis=-1)
    keeping = live_rows[:, :, None] & (ranking < CAP)
    placed = jnp.where(keeping, ranking, -1)
    return (counts, paired.reshape(IMAGES, S, 2).astype(jnp.int32), placed.reshape(IMAGES, S, 2).astype(jnp.int32))


def draw_live_count(key, part):
    tables = routing_tables(key)
    return tables[0]


def draw_routes(key, part):
    tables = routing_tables(key)
    return tables[1]


def draw_slot_ids(key, part):
    tables = routing_tables(key)
    return tables[2]


def spiked(drawn, rng, source, target, parts, factor):
    def block_of(position):
        return (jnp.arange(drawn.shape[position]) // (drawn.shape[position] // parts)).reshape((-1,) + (1,) * (drawn.ndim - 1 - position))

    one_side = jax.random.permutation(rng, parts)[block_of(target)]
    other_side = (block_of(target) + parts // 2) % parts
    return jnp.where((block_of(source) == one_side) | (block_of(source) == other_side), factor * drawn, drawn)


def steps_of(stream_key, dims, cuts, low, top_value):
    gain = 1.0
    for dim, blocks in cuts:
        steps = jax.random.uniform(jax.random.fold_in(jax.random.fold_in(stream_key, 6), dim), (blocks,), jnp.float32, low / len(cuts), top_value / len(cuts))
        gain = gain * jnp.repeat(jnp.exp(steps), dims[dim] // blocks).reshape((-1,) + (1,) * (len(dims) - 1 - dim))
    return gain


def noise(rng, dims, scale, bound, cuts=(), dtype=jnp.bfloat16):
    drawn = jax.random.normal(rng, dims, jnp.float32) * scale
    if len(cuts) > 0:
        drawn = steps_of(rng, dims, cuts, -0.22, 0.18) * drawn
    return jnp.clip(drawn, min=-bound, max=bound).astype(dtype)


def gaussian_with(own_key, dims, width, most, pieces, heavy, dtype=jnp.bfloat16):
    drawn = width * jax.random.normal(own_key, dims, jnp.float32)
    if pieces:
        drawn = drawn * steps_of(own_key, dims, pieces, -0.22, 0.18)
    return jnp.clip(spiked(drawn, jax.random.fold_in(own_key, 3), *heavy), -most, most).astype(dtype)


def setup_inputs(seed: int = 0) -> dict:
    splits = jax.random.split(jax.random.key(seed), 19)
    images = noise(splits[0], (IMAGES, S, D), 1.0, 6.0, ((0, 32),))
    attn_norm_gain = jnp.clip(1.0 + 0.1 * jax.random.normal(splits[1], (D,), jnp.float32), 0.5, 1.5).astype(jnp.bfloat16)
    attn_norm_bias = noise(splits[2], (D,), 0.2, 1.1953125, ((0, 4),))
    qkv_weight = noise(splits[3], (D, 3 * D), D ** -0.5, 0.25, ((0, 4),))
    query_value_bias = noise(splits[4], (2 * D,), 0.2, 1.1953125, ((0, 4),))
    proj_weight = noise(splits[5], (D, D), (D // 64) ** -0.5, 2.0, ((0, 4),))
    proj_bias = noise(splits[6], (D,), 0.2, 1.1953125, ((0, 4),))
    moe_norm_gain = jnp.clip(1.0 + 0.1 * jax.random.normal(splits[7], (D,), jnp.float32), 0.5, 1.5).astype(jnp.bfloat16)
    moe_norm_bias = noise(splits[8], (D,), 0.2, 1.1953125, ((0, 4),))
    router_weight = noise(splits[9], (D, E), (2 * D) ** -0.5, 0.1875, ((0, 4),))
    expert_inner = noise(splits[10], (E, D, F), D ** -0.5, 0.25, ((0, 4),))
    expert_inner_bias = noise(splits[11], (E, F), 0.15, 0.8984375, ((0, 4),))
    expert_outer = noise(splits[12], (E, F, D), (F // 16) ** -0.5, 0.5, ((0, 4),))
    expert_outer_bias = noise(splits[13], (E, D), 0.3, 1.796875, ((0, 4),))
    live_count = draw_live_count(jax.random.fold_in(splits[18], 71), 0)
    routes = draw_routes(jax.random.fold_in(splits[18], 71), 0)
    slot_ids = draw_slot_ids(jax.random.fold_in(splits[18], 71), 0)
    cotangent = gaussian_with(splits[17], (IMAGES, S, D), 1.0, 6.0, ((0, 32),), (0, 2, 32, 2.75))
    return dict(images=images, attn_norm_gain=attn_norm_gain, attn_norm_bias=attn_norm_bias, qkv_weight=qkv_weight, query_value_bias=query_value_bias, proj_weight=proj_weight, proj_bias=proj_bias, moe_norm_gain=moe_norm_gain, moe_norm_bias=moe_norm_bias, router_weight=router_weight, expert_inner=expert_inner, expert_inner_bias=expert_inner_bias, expert_outer=expert_outer, expert_outer_bias=expert_outer_bias, live_count=live_count, routes=routes, slot_ids=slot_ids, cotangent=cotangent)


@jax.custom_vjp
def low(v):
    return lax.optimization_barrier(v.astype(jnp.bfloat16)).astype(jnp.float32)

@jax.custom_vjp
def low_back(v):
    return v

def low_keep(v):
    return (low(v), None)

def low_pass(kept, grad):
    return (grad,)

def back_keep(v):
    return (v, None)

def back_low(kept, grad):
    return (low(grad),)
low.defvjp(low_keep, low_pass)
low_back.defvjp(back_keep, back_low)
NORM_EPS = 1e-06
HIGHEST = lax.Precision.HIGHEST

def layer_norm(values, gain_vector, shift_vector):
    center = values - lax.optimization_barrier(jnp.mean(values, axis=-1, keepdims=True))
    spread = lax.optimization_barrier(jnp.mean(center * center, axis=-1, keepdims=True))
    return center * lax.rsqrt(spread + NORM_EPS) * gain_vector + shift_vector

def device_block(params, inputs, live_images, route_ids, slot_index):
    norm1_gain, norm1_shift, qkv_matrix, pair_shift, proj_matrix, proj_shift, norm2_gain, norm2_shift, router_matrix, inner_matrix, inner_shift, outer_matrix, outer_shift = params
    image_count, length, model_width = inputs.shape
    row_count = image_count * length
    head_size = model_width // HEADS
    expert_count = router_matrix.shape[1]
    slot_total = expert_count * CAP
    score_scale = 1.0 / math.sqrt(head_size)
    token_rows = inputs.reshape(row_count, model_width)
    live_rows = (jnp.arange(row_count) // length < live_images).astype(jnp.float32)[:, None]
    normed = low(layer_norm(token_rows, norm1_gain, norm1_shift))
    projected = jnp.dot(normed, qkv_matrix, precision=HIGHEST)
    queries = low(low_back(projected[:, :model_width] + pair_shift[:model_width]))
    keys_all = low(low_back(projected[:, model_width:2 * model_width]))
    values_all = low(low_back(projected[:, 2 * model_width:] + pair_shift[model_width:]))

    def by_head(matrix):
        return matrix.reshape(image_count, length, HEADS, head_size)
    scores = jnp.einsum('bqhc,bkhc->bhqk', by_head(queries), by_head(keys_all), precision=HIGHEST)
    scores = low_back(scores * score_scale)
    attn_weights = low(jax.nn.softmax(scores, axis=-1))
    attended = jnp.einsum('bhqk,bkhc->bqhc', attn_weights, by_head(values_all), precision=HIGHEST)
    attended = low(low_back(attended.reshape(row_count, model_width)))
    branch = low_back(jnp.dot(attended, proj_matrix, precision=HIGHEST) + proj_shift)
    residual = token_rows + branch
    normed2 = low(layer_norm(residual, norm2_gain, norm2_shift))
    logits = low_back(jnp.dot(normed2, router_matrix, precision=HIGHEST))
    router_probs = jax.nn.softmax(logits, axis=-1)
    route_flat = route_ids.reshape(row_count, 2)
    slot_flat = slot_index.reshape(row_count, 2)
    routed = slot_flat >= 0
    chosen = ((route_flat[:, :, None] == jnp.arange(expert_count)[None, None, :]) & routed[:, :, None]).astype(jnp.float32)
    gate_values = lax.optimization_barrier(jnp.sum(router_probs[:, None, :] * chosen, axis=-1))
    target = jnp.where(routed, route_flat * CAP + slot_flat, slot_total).reshape(-1).astype(jnp.int32)
    fetch_index = jnp.minimum(target, slot_total - 1).astype(jnp.int32)
    buffer = jnp.zeros((slot_total, model_width), jnp.float32).at[target].set(jnp.repeat(normed2, 2, axis=0), mode='drop')
    buffer = buffer.reshape(expert_count, CAP, model_width)
    hidden = jnp.einsum('ecd,edf->ecf', buffer, inner_matrix, precision=HIGHEST) + inner_shift[:, None, :]
    hidden = low_back(hidden)
    active = low(jax.nn.gelu(hidden, approximate=False))
    expert_rows = jnp.einsum('ecf,efd->ecd', active, outer_matrix, precision=HIGHEST) + outer_shift[:, None, :]
    expert_rows = low_back(expert_rows)
    picked = jnp.take(expert_rows.reshape(slot_total, model_width), fetch_index, axis=0).reshape(row_count, 2, model_width)
    mixture = lax.optimization_barrier(jnp.sum(gate_values[:, :, None] * picked, axis=1))
    return ((residual + mixture) * live_rows).reshape(image_count, length, model_width)

def reference(images, attn_norm_gain, attn_norm_bias, qkv_weight, query_value_bias, proj_weight, proj_bias, moe_norm_gain, moe_norm_bias, router_weight, expert_inner, expert_inner_bias, expert_outer, expert_outer_bias, live_count, routes, slot_ids, cotangent):
    params = tuple((entry.astype(jnp.float32) for entry in (attn_norm_gain, attn_norm_bias, qkv_weight, query_value_bias, proj_weight, proj_bias, moe_norm_gain, moe_norm_bias, router_weight, expert_inner, expert_inner_bias, expert_outer, expert_outer_bias)))
    device_total = N_REPLICA * N_GROUP
    stacked = images.astype(jnp.float32).reshape(device_total, IMG_DEV, S, D)
    route_stack = routes.reshape(device_total, IMG_DEV, S, 2)
    slot_stack = slot_ids.reshape(device_total, IMG_DEV, S, 2)
    block_step = jax.checkpoint(device_block)

    def forward(weights, inputs):

        def one_device(item):
            return block_step(weights, item[0], item[1], item[2], item[3])
        return lax.map(one_device, (inputs, live_count, route_stack, slot_stack))
    outputs, pullback = jax.vjp(forward, params, stacked)
    grads, input_grad = pullback(cotangent.astype(jnp.float32).reshape(outputs.shape))
    return (outputs.reshape(IMAGES, S, D).astype(jnp.bfloat16), input_grad.reshape(IMAGES, S, D), grads[0], grads[1], grads[2], grads[3], grads[4], grads[5], grads[6], grads[7], grads[8], grads[9], grads[10], grads[11], grads[12])
```

```python
import functools
import math

import jax
import jax.numpy as jnp
from jax import lax
from jax.experimental import pallas as pl
from jax.experimental.pallas import tpu as pltpu
from jax.sharding import PartitionSpec as P

HEADS = 8
CAP = 640
NORM_EPS = 1e-06
F32 = jnp.float32
BF16 = jnp.bfloat16
PAD = 256
PIECES = 8
SPLIT_A = (2, 4, 1)
SPLIT_B = (4, 2, 1)
SMALL = 128
MIB = 1 << 20


def offset_of(position, order):
    total = 0
    for k, bit in enumerate(order):
        total = total + ((position >> k) & 1) * bit
    return total


def dot_nn(a, b):
    return lax.dot_general(a, b, (((1,), (0,)), ((), ())), preferred_element_type=F32)


def dot_nt(a, b):
    return lax.dot_general(a, b, (((1,), (1,)), ((), ())), preferred_element_type=F32)


def dot_tn(a, b):
    return lax.dot_general(a, b, (((0,), (0,)), ((), ())), preferred_element_type=F32)


def norm_parts(values):
    center = values - jnp.mean(values, axis=-1, keepdims=True)
    spread = jnp.mean(center * center, axis=-1, keepdims=True)
    rstd = lax.rsqrt(spread + NORM_EPS)
    return center * rstd, rstd


def gelu_parts(v):
    size = jnp.abs(v)
    density = jnp.exp(v * v * (-0.5)) * 0.3989422804014327
    t = 1.0 / (1.0 + 0.2316418882 * size)
    series = t * (
        0.319381530 + t * (-0.356563782 + t * (1.781477937 + t * (-1.821255978 + t * 1.330274429)))
    )
    tail = density * series
    phi = jnp.where(v < 0, tail, 1.0 - tail)
    return v * phi, phi + v * density


def forward_kernel(
    place, images, cot, a_lo, a_hi, b_lo, b_hi,
    qkv_out, att_out, res_out, tok_out, gates_out, full_out, small_out,
):
    model = images.shape[2]
    length = images.shape[1]
    depth = a_lo.shape[2]
    parts = a_lo.shape[1]
    split = a_lo.shape[3]

    @pl.when(pl.program_id(0) == 0)
    def _():
        z, r = place[0], place[1]
        for pos in range(PIECES):
            for d in range(parts):
                owner = lax.rem(z + parts - d, parts) * PIECES
                for lo, hi, order, start in ((a_lo, a_hi, SPLIT_A, 0), (b_lo, b_hi, SPLIT_B, split)):
                    block = (lo if pos < PIECES // 2 else hi)[pos % (PIECES // 2), d]
                    row = pl.multiple_of((owner + jnp.bitwise_xor(r, offset_of(pos, order))) * depth, depth)
                    full_out[pl.ds(row, depth), start : start + block.shape[1]] = block
        small_out[...] = full_out[:, 4 * model :].astype(F32).T

    def vector(row):
        return small_out[row : row + 1, :]

    x = images[0].astype(F32)
    xhat, _ = norm_parts(x)
    normed = (xhat * vector(4) + vector(5)).astype(BF16)
    projected = dot_nn(normed, full_out[:, : 3 * model])
    bias_parts = []
    for part in range(parts):
        lanes = slice(part * 128, part * 128 + 128)
        bias_parts += [small_out[9:10, lanes], small_out[10:11, lanes]]
    pair = jnp.concatenate(bias_parts, axis=1)
    q = (projected[:, :model] + pair[:, :model]).astype(BF16)
    k = projected[:, model : 2 * model].astype(BF16)
    v = (projected[:, 2 * model :] + pair[:, model:]).astype(BF16)
    qkv_out[0, :, :model] = q
    qkv_out[0, :, model : 2 * model] = k
    qkv_out[0, :, 2 * model :] = v
    head = model // HEADS
    first = lax.broadcasted_iota(jnp.int32, (1, 2 * head), 1) < head
    scale = 1.0 / math.sqrt(head)
    attended = []
    for two in range(HEADS // 2):
        lanes = slice(two * 2 * head, (two + 1) * 2 * head)
        q2, k2, v2 = q[:, lanes], k[:, lanes], v[:, lanes]
        total = None
        for mask in (first, jnp.logical_not(first)):
            scores = dot_nt(jnp.where(mask, q2, jnp.zeros_like(q2)), k2) * scale
            e = jnp.exp(scores - jnp.max(scores, axis=-1, keepdims=True))
            probs = (e * (1.0 / jnp.sum(e, axis=-1, keepdims=True))).astype(BF16)
            part = dot_nn(probs, jnp.where(mask, v2, jnp.zeros_like(v2)))
            total = part if total is None else total + part
        attended.append(total.astype(BF16))
    attended = jnp.concatenate(attended, axis=1)
    att_out[0] = attended
    residual = x + (dot_nn(attended, full_out[:, 3 * model : 4 * model]) + vector(6))
    res_out[0] = residual
    xhat2, _ = norm_parts(residual)
    normed2 = (xhat2 * vector(7) + vector(8)).astype(BF16)
    tail = length // 64 * 64
    tok_out[tail:, :] = jnp.zeros((PAD - tail, 2 * model), BF16)
    tok_out[:length, :model] = normed2
    tok_out[:length, model:] = cot[0]
    logits = dot_nt(small_out[0:8, :].astype(BF16), tok_out[:, :model])
    experts = lax.broadcasted_iota(jnp.int32, logits.shape, 0) < parts
    logits = jnp.where(experts, logits, -jnp.inf)
    e = jnp.exp(logits - jnp.max(logits, axis=0, keepdims=True))
    gates_out[0] = e / jnp.sum(e, axis=0, keepdims=True)


def forward_call(place, images, cot, a_lo, a_hi, b_lo, b_hi):
    count, length, model = images.shape
    whole = lambda a: pl.BlockSpec(a.shape, lambda i, *_: (0,) * a.ndim)
    image = lambda *dims: pl.BlockSpec((1,) + dims, lambda i, *_: (i, 0, 0))
    outs = (
        jax.ShapeDtypeStruct((count, length, 3 * model), BF16),
        jax.ShapeDtypeStruct((count, length, model), BF16),
        jax.ShapeDtypeStruct((count, length, model), F32),
        jax.ShapeDtypeStruct((count * PAD, 2 * model), BF16),
        jax.ShapeDtypeStruct((count, 8, PAD), F32),
        jax.ShapeDtypeStruct((model, 4 * model + SMALL), BF16),
        jax.ShapeDtypeStruct((SMALL, model), F32),
    )
    return pl.pallas_call(
        forward_kernel,
        out_shape=outs,
        grid_spec=pltpu.PrefetchScalarGridSpec(
            num_scalar_prefetch=1,
            grid=(count,),
            in_specs=[image(length, model), image(length, model)] + [whole(a) for a in (a_lo, a_hi, b_lo, b_hi)],
            out_specs=[
                image(length, 3 * model), image(length, model), image(length, model),
                pl.BlockSpec((PAD, 2 * model), lambda i, *_: (i, 0)),
                image(8, PAD), whole(outs[5]), whole(outs[6]),
            ],
        ),
        compiler_params=pltpu.CompilerParams(vmem_limit_bytes=40 * MIB),
        cost_estimate=pl.CostEstimate(flops=14 * 10**9, bytes_accessed=12 * MIB, transcendentals=0),
        name="attention_forward",
    )(place, images, cot, a_lo, a_hi, b_lo, b_hi)


def expert_kernel(
    place, tok, slots, gates, small, ia_lo, ia_hi, ib_lo, ib_hi,
    a_keep, a_send, b_keep, b_send, rows_out, back_out, bias_out,
    onehot, buffer, grad_slots, rows, back, *, turn,
):
    i = pl.program_id(0)
    count = slots.shape[0]
    model = tok.shape[1] // 2
    half = PIECES // 2
    piece = place[4 + 4 * PIECES + i]

    @pl.when(i == 0)
    def _():
        e = place[2]
        where = lax.broadcasted_iota(jnp.int32, (CAP, PAD), 0)
        gate = jnp.zeros((CAP, 128), F32)
        for b in range(count):
            mask = where == slots[b, turn : turn + 1, :]
            onehot[:, b * PAD : (b + 1) * PAD] = mask.astype(F32).astype(BF16)
            weighted = jnp.where(mask, gates[b, pl.ds(e, 1), :], 0.0)
            gate = gate + weighted[:, :128] + weighted[:, 128:]
        gate = jnp.sum(gate, axis=1, keepdims=True)
        buffer[...] = dot_nn(onehot[...], tok[:, :model]).astype(BF16)
        grads = (dot_nn(onehot[...], tok[:, model:]) * gate).astype(BF16)
        grad_slots[...] = grads
        sums = jnp.sum(grads.astype(F32), axis=0, keepdims=True)
        for c in range(4):
            bias_out[16 + c : 17 + c, :] = sums[:, c * 128 : (c + 1) * 128]
        bias_out[20:32, :] = jnp.zeros((12, 128), F32)
        outer_bias = jnp.concatenate([small[28 + c : 29 + c, :] for c in range(4)], axis=1)
        rows[...] = jnp.broadcast_to(outer_bias, rows.shape)
        back[...] = jnp.zeros_like(back)

    early = i < half
    wa = jnp.where(early, ia_lo[...], ia_hi[...])
    wb = jnp.where(early, ib_lo[...], ib_hi[...])
    buf = buffer[...]
    gs = grad_slots[...]
    bias = jnp.concatenate([small[pl.ds(12 + 2 * piece, 1), :], small[pl.ds(13 + 2 * piece, 1), :]], axis=1)
    hidden = dot_nt(buf, wa) + bias
    active, slope = gelu_parts(hidden)
    active = active.astype(BF16)
    rows[...] += dot_nn(active, wb)
    grad_hidden = dot_nt(gs, wb) * slope
    grad_low = grad_hidden.astype(BF16)
    sums = jnp.sum(grad_low.astype(F32), axis=0, keepdims=True)
    bias_out[pl.ds(2 * piece, 1), :] = sums[:, :128]
    bias_out[pl.ds(2 * piece + 1, 1), :] = sums[:, 128:]
    grad_a = dot_tn(grad_low, buf).astype(BF16)
    grad_b = dot_tn(active, gs).astype(BF16)
    back[...] += dot_nn(grad_low, wa)

    @pl.when(early)
    def _():
        a_keep[...] = grad_a
        b_keep[...] = grad_b

    @pl.when(jnp.logical_not(early))
    def _():
        a_send[...] = grad_a
        b_send[...] = grad_b

    @pl.when(i == PIECES - 1)
    def _():
        rows_out[...] = rows[...].astype(BF16)
        back_out[...] = back[...].astype(BF16)


def expert_call(turn, place, tok, slots, gates, small, weights):
    model = tok.shape[1] // 2
    count = slots.shape[0]
    depth = PIECES * 256
    half = depth // 2
    whole = lambda a: pl.BlockSpec(a.shape, lambda i, *_: (0,) * a.ndim)
    table = lambda k: pl.BlockSpec((256, model), lambda i, s: (s[4 + k * PIECES + i], 0))
    out_half = lambda f: pl.BlockSpec((256, model), lambda i, s: (f(i), 0))
    swap = lambda i: ((i & 1) << 1) | ((i >> 1) & 1)
    outs = tuple(jax.ShapeDtypeStruct((half, model), BF16) for _ in range(4)) + (
        jax.ShapeDtypeStruct((CAP, model), BF16),
        jax.ShapeDtypeStruct((CAP, model), BF16),
        jax.ShapeDtypeStruct((32, 128), F32),
    )
    keep_a = lambda i: jnp.minimum(i, 3)
    send_a = lambda i: jnp.maximum(i - 4, 0)
    keep_b = lambda i: jnp.where(i < 4, swap(i), 3)
    send_b = lambda i: jnp.where(i < 4, 0, swap(i - 4))
    return pl.pallas_call(
        functools.partial(expert_kernel, turn=turn),
        out_shape=outs,
        grid_spec=pltpu.PrefetchScalarGridSpec(
            num_scalar_prefetch=1,
            grid=(PIECES,),
            in_specs=[
                whole(tok), whole(slots), whole(gates),
                pl.BlockSpec((SMALL, 128), lambda i, s: (0, s[2])),
                table(0), table(1), table(2), table(3),
            ],
            out_specs=[
                out_half(keep_a), out_half(send_a), out_half(keep_b), out_half(send_b),
                whole(outs[4]), whole(outs[5]), whole(outs[6]),
            ],
            scratch_shapes=[
                pltpu.VMEM((CAP, count * PAD), BF16),
                pltpu.VMEM((CAP, model), BF16),
                pltpu.VMEM((CAP, model), BF16),
                pltpu.VMEM((CAP, model), F32),
                pltpu.VMEM((CAP, model), F32),
            ],
        ),
        compiler_params=pltpu.CompilerParams(vmem_limit_bytes=40 * MIB),
        cost_estimate=pl.CostEstimate(flops=14 * 10**9, bytes_accessed=14 * MIB, transcendentals=0),
        name="expert",
    )(place, tok, slots, gates, small, *weights)


def backward_kernel(place, *refs, turns):
    images, cot, qkv, att, res, tok, slots, full, small = refs[:9]
    rows = refs[9 : 9 + turns]
    back = refs[9 + turns : 9 + 2 * turns]
    biases = refs[9 + 2 * turns : 9 + 3 * turns]
    block_out, input_grad, a_keep, a_send, b_keep, b_send = refs[9 + 3 * turns : 15 + 3 * turns]
    acc_qkv, acc_proj, acc_router, acc_small = refs[15 + 3 * turns :]
    b = pl.program_id(0)
    model = images.shape[2]
    length = images.shape[1]
    parts = turns

    @pl.when(b == 0)
    def _():
        acc_qkv[...] = jnp.zeros_like(acc_qkv)
        acc_proj[...] = jnp.zeros_like(acc_proj)
        acc_router[...] = jnp.zeros_like(acc_router)
        acc_small[...] = jnp.zeros_like(acc_small)

    def vector(row):
        return small[row : row + 1, :]

    def add_row(row, values):
        acc_small[row : row + 1, :] += jnp.sum(values, axis=0, keepdims=True)

    live = (b < place[3]).astype(F32)
    x = images[0].astype(F32)
    xhat1, rstd1 = norm_parts(x)
    residual = res[0]
    xhat2, rstd2 = norm_parts(residual)
    normed2 = tok[:length, :model]
    grad_out = cot[0].astype(F32) * live

    logits = dot_nn(normed2, full[:, 4 * model :])
    lane = lax.broadcasted_iota(jnp.int32, logits.shape, 1)
    logits = jnp.where(lane < parts, logits, -jnp.inf)
    e = jnp.exp(logits - jnp.max(logits, axis=-1, keepdims=True))
    probs = e / jnp.sum(e, axis=-1, keepdims=True)

    seat = lax.broadcasted_iota(jnp.int32, (length, CAP), 1)
    mixture = jnp.zeros((length, model), F32)
    grad_n2 = jnp.zeros((length, model), F32)
    grad_probs = jnp.zeros_like(probs)
    for j in range(turns):
        expert = lax.rem(place[0] + parts - j, parts)
        mask = (slots[0][:, j : j + 1] == seat).astype(F32).astype(BF16)
        picked = dot_nn(mask, rows[j][...])
        gate = jnp.sum(jnp.where(lane == expert, probs, 0.0), axis=-1, keepdims=True)
        mixture = mixture + gate * picked
        grad_gate = jnp.sum(grad_out * picked, axis=-1, keepdims=True)
        grad_probs = jnp.where(lane == expert, grad_gate, grad_probs)
        grad_n2 = grad_n2 + dot_nn(mask, back[j][...])
    block_out[0] = ((residual + mixture) * live).astype(BF16)
    grad_logits = probs * (grad_probs - jnp.sum(probs * grad_probs, axis=-1, keepdims=True))
    grad_logits = grad_logits.astype(BF16)
    grad_n2 = grad_n2 + dot_nt(grad_logits, full[:, 4 * model :])
    acc_router[...] += dot_tn(normed2, grad_logits)

    add_row(7, grad_n2 * xhat2)
    add_row(8, grad_n2)
    inner = grad_n2 * vector(7)
    grad_res = grad_out + rstd2 * (
        inner
        - jnp.mean(inner, axis=-1, keepdims=True)
        - xhat2 * jnp.mean(inner * xhat2, axis=-1, keepdims=True)
    )
    branch = grad_res.astype(BF16)
    add_row(6, branch.astype(F32))
    attended = att[0]
    acc_proj[...] += dot_tn(attended, branch)
    grad_att = dot_nt(branch, full[:, 3 * model : 4 * model]).astype(BF16)

    head = model // HEADS
    first = lax.broadcasted_iota(jnp.int32, (1, 2 * head), 1) < head
    scale = 1.0 / math.sqrt(head)
    grads = [[], [], []]
    for two in range(HEADS // 2):
        lanes = slice(two * 2 * head, (two + 1) * 2 * head)
        q2 = qkv[0, :, two * 2 * head : (two + 1) * 2 * head]
        k2 = qkv[0, :, model + two * 2 * head : model + (two + 1) * 2 * head]
        v2 = qkv[0, :, 2 * model + two * 2 * head : 2 * model + (two + 1) * 2 * head]
        g2 = grad_att[:, lanes]
        totals = [None, None, None]
        for mask in (first, jnp.logical_not(first)):
            only = lambda t: jnp.where(mask, t, jnp.zeros_like(t))
            q1, g1 = only(q2), only(g2)
            scores = dot_nt(q1, k2) * scale
            e = jnp.exp(scores - jnp.max(scores, axis=-1, keepdims=True))
            weights = e * (1.0 / jnp.sum(e, axis=-1, keepdims=True))
            grad_weights = dot_nt(g1, v2)
            grad_scores = weights * (
                grad_weights - jnp.sum(grad_weights * weights, axis=-1, keepdims=True)
            )
            grad_scores = grad_scores.astype(BF16)
            new = (
                dot_nn(grad_scores, only(k2)),
                dot_tn(grad_scores, q1),
                dot_tn(weights.astype(BF16), g1),
            )
            totals = [n if t is None else t + n for t, n in zip(totals, new)]
        grads[0].append((totals[0] * scale).astype(BF16))
        grads[1].append((totals[1] * scale).astype(BF16))
        grads[2].append(totals[2].astype(BF16))
    grad_projected = jnp.concatenate(grads[0] + grads[1] + grads[2], axis=1)
    normed = (xhat1 * vector(4) + vector(5)).astype(BF16)
    acc_qkv[...] += dot_tn(normed, grad_projected)
    grad_normed = dot_nt(grad_projected, full[:, : 3 * model])
    for row, start in ((9, 0), (10, 2 * model)):
        sums = jnp.sum(grad_projected[:, start : start + model].astype(F32), axis=0, keepdims=True)
        acc_small[row + 23 : row + 24, :] += sums
    add_row(4, grad_normed * xhat1)
    add_row(5, grad_normed)
    inner = grad_normed * vector(4)
    input_grad[0] = grad_res + rstd1 * (
        inner
        - jnp.mean(inner, axis=-1, keepdims=True)
        - xhat1 * jnp.mean(inner * xhat1, axis=-1, keepdims=True)
    )

    @pl.when(b == pl.num_programs(0) - 1)
    def _():
        for part in range(parts):
            for k in range(2):
                start = (part * 2 + k) * 128
                source = 32 + start // model
                acc_small[9 + k : 10 + k, part * 128 : part * 128 + 128] = acc_small[
                    source : source + 1, start % model : start % model + 128
                ]
        acc_small[32:34, :] = jnp.zeros((2, model), F32)
        for j in range(turns):
            expert = lax.rem(place[0] + parts - j, parts)
            acc_small[12:32, pl.ds(pl.multiple_of(expert * 128, 128), 128)] = biases[j][0:20, :]
        acc_router[...] = acc_router[...] + acc_small[...].T
        depth = a_keep.shape[2]
        split = a_keep.shape[3]
        for pos in range(PIECES):
            for d in range(parts):
                owner = lax.rem(place[0] + parts - d, parts) * PIECES
                where = pos % (PIECES // 2)
                row = pl.multiple_of((owner + jnp.bitwise_xor(place[1], offset_of(pos, SPLIT_A))) * depth, depth)
                out = a_keep if pos < PIECES // 2 else a_send
                out[where, d] = acc_qkv[pl.ds(row, depth), :split].astype(BF16)
                row = pl.multiple_of((owner + jnp.bitwise_xor(place[1], offset_of(pos, SPLIT_B))) * depth, depth)
                out = b_keep if pos < PIECES // 2 else b_send
                rest = 3 * model - split
                out[where, d, :, :rest] = acc_qkv[pl.ds(row, depth), split:].astype(BF16)
                out[where, d, :, rest : rest + model] = acc_proj[pl.ds(row, depth), :].astype(BF16)
                out[where, d, :, rest + model :] = acc_router[pl.ds(row, depth), :].astype(BF16)


def backward_call(place, images, cot, qkv, att, res, tok, slots, full, small, rows, back, biases):
    count, length, model = images.shape
    turns = len(rows)
    depth = model // (turns * PIECES)
    whole = lambda a: pl.BlockSpec(a.shape, lambda i, *_: (0,) * a.ndim)
    image = lambda *dims: pl.BlockSpec((1,) + dims, lambda i, *_: (i, 0, 0))
    outs = (
        jax.ShapeDtypeStruct((count, length, model), BF16),
        jax.ShapeDtypeStruct((count, length, model), F32),
    ) + tuple(
        jax.ShapeDtypeStruct((PIECES // 2, turns, depth, w), BF16)
        for w in (2 * model, 2 * model, 2 * model + SMALL, 2 * model + SMALL)
    )
    return pl.pallas_call(
        functools.partial(backward_kernel, turns=turns),
        out_shape=outs,
        grid_spec=pltpu.PrefetchScalarGridSpec(
            num_scalar_prefetch=1,
            grid=(count,),
            in_specs=[
                image(length, model), image(length, model), image(length, 3 * model),
                image(length, model), image(length, model),
                pl.BlockSpec((PAD, 2 * model), lambda i, *_: (i, 0)),
                image(length, slots.shape[2]), whole(full), whole(small),
            ] + [whole(a) for a in (*rows, *back, *biases)],
            out_specs=[image(length, model), image(length, model)] + [whole(o) for o in outs[2:]],
            scratch_shapes=[
                pltpu.VMEM((model, 3 * model), F32),
                pltpu.VMEM((model, model), F32),
                pltpu.VMEM((model, SMALL), F32),
                pltpu.VMEM((SMALL, model), F32),
            ],
        ),
        compiler_params=pltpu.CompilerParams(vmem_limit_bytes=48 * MIB),
        cost_estimate=pl.CostEstimate(flops=35 * 10**9, bytes_accessed=16 * MIB, transcendentals=0),
        name="attention_backward",
    )(place, images, cot, qkv, att, res, tok, slots, full, small, *rows, *back, *biases)


def finish_kernel(place, a_lo, a_hi, b_lo, b_hi, inner_out, outer_out):
    early = pl.program_id(0) < PIECES // 2
    inner_out[0] = jnp.where(early, a_lo[...], a_hi[...]).astype(F32).T
    outer_out[0] = jnp.where(early, b_lo[...], b_hi[...]).astype(F32)


def finish_call(place, a_lo, a_hi, b_lo, b_hi):
    model = a_lo.shape[1]
    depth = PIECES * 256
    swap = lambda i: ((i & 1) << 1) | ((i >> 1) & 1)
    block = lambda f: pl.BlockSpec((256, model), lambda i, s: (f(i), 0))
    piece = lambda i, s: s[4 + 4 * PIECES + i]
    return pl.pallas_call(
        finish_kernel,
        out_shape=(
            jax.ShapeDtypeStruct((1, model, depth), F32),
            jax.ShapeDtypeStruct((1, depth, model), F32),
        ),
        grid_spec=pltpu.PrefetchScalarGridSpec(
            num_scalar_prefetch=1,
            grid=(PIECES,),
            in_specs=[
                block(lambda i: jnp.minimum(i, 3)),
                block(lambda i: jnp.maximum(i - 4, 0)),
                block(lambda i: jnp.where(i < 4, swap(i), 3)),
                block(lambda i: jnp.where(i < 4, 0, swap(i - 4))),
            ],
            out_specs=[
                pl.BlockSpec((1, model, 256), lambda i, s: (0, 0, piece(i, s))),
                pl.BlockSpec((1, 256, model), lambda i, s: (0, piece(i, s), 0)),
            ],
        ),
        cost_estimate=pl.CostEstimate(flops=6 * 10**9, bytes_accessed=12 * MIB, transcendentals=0),
        name="finish_experts",
    )(place, a_lo, a_hi, b_lo, b_hi)


def finish_dense_kernel(place, a_lo, a_hi, b_lo, b_hi, qkv_out, proj_out, small_out, turned_out):
    model = proj_out.shape[1]
    depth = a_lo.shape[1]
    split = a_lo.shape[2]
    for pos in range(PIECES):
        where = pos % (PIECES // 2)
        row = pl.multiple_of(jnp.bitwise_xor(place[1], offset_of(pos, SPLIT_A)) * depth, depth)
        block = (a_lo if pos < PIECES // 2 else a_hi)[where].astype(F32)
        qkv_out[pl.ds(row, depth), :split] = block
        row = pl.multiple_of(jnp.bitwise_xor(place[1], offset_of(pos, SPLIT_B)) * depth, depth)
        block = (b_lo if pos < PIECES // 2 else b_hi)[where].astype(F32)
        rest = 3 * model - split
        qkv_out[pl.ds(row, depth), split:] = block[:, :rest]
        proj_out[pl.ds(row, depth), :] = block[:, rest : rest + model]
        small_out[pl.ds(row, depth), :] = block[:, rest + model :]
    turned_out[...] = small_out[...].T


def finish_dense_call(place, a_lo, a_hi, b_lo, b_hi, model):
    rows = a_lo.shape[1] * PIECES
    return pl.pallas_call(
        finish_dense_kernel,
        out_shape=(
            jax.ShapeDtypeStruct((rows, 3 * model), F32),
            jax.ShapeDtypeStruct((rows, model), F32),
            jax.ShapeDtypeStruct((rows, SMALL), F32),
            jax.ShapeDtypeStruct((SMALL, rows), F32),
        ),
        in_specs=[pl.BlockSpec(memory_space=pltpu.SMEM)] + [pl.BlockSpec(memory_space=pltpu.VMEM)] * 4,
        cost_estimate=pl.CostEstimate(flops=2 * 10**9, bytes_accessed=2 * MIB, transcendentals=0),
        name="finish_dense",
    )(place, a_lo, a_hi, b_lo, b_hi)


def local(
    images, attn_norm_gain, attn_norm_bias, qkv_weight, query_value_bias, proj_weight, proj_bias,
    moe_norm_gain, moe_norm_bias, router_weight, expert_inner, expert_inner_bias, expert_outer,
    expert_outer_bias, live_count, routes, slot_ids, cotangent, *, n_replica, n_group,
):
    count, length, model = images.shape
    shard = qkv_weight.shape[0]
    hidden = expert_inner.shape[2]
    depth = shard // PIECES
    block = hidden // PIECES
    z = lax.axis_index("group").astype(jnp.int32)
    replica = lax.axis_index("replica").astype(jnp.int32)
    r = replica & (PIECES - 1)

    def across(value, bit):
        return lax.ppermute(value, "replica", [(i, i ^ bit) for i in range(n_replica)])

    def along(value, shift):
        return lax.ppermute(value, "group", [(i, (i + shift) % n_group) for i in range(n_group)])

    def add(one, other):
        return (one.astype(F32) + other.astype(F32)).astype(BF16)

    def collect(value, order):
        for bit in order[:-1]:
            value = jnp.concatenate([value, across(value, bit)], axis=0)
        return value, across(value, order[-1])

    def reduce(keep, send, order):
        value = add(keep, across(send, order[-1]))
        for bit in order[-2::-1]:
            half = value.shape[0] // 2
            value = add(value[:half], across(value[half:], bit))
        bit = PIECES
        while bit < n_replica:
            value = add(value, across(value, bit))
            bit *= 2
        return value

    column = lambda vector: vector.reshape(-1, shard).T
    table = jnp.concatenate(
        [qkv_weight, proj_weight, router_weight]
        + [column(v) for v in (attn_norm_gain, attn_norm_bias, proj_bias, moe_norm_gain, moe_norm_bias, query_value_bias)]
        + [jnp.zeros((shard, 1), BF16), column(expert_inner_bias), column(expert_outer_bias)]
        + [jnp.zeros((shard, SMALL - 32), BF16)],
        axis=1,
    )
    mine = lax.dynamic_slice_in_dim(table, r * depth, depth, 0)
    split = 2 * model
    dense = []
    for part, order in ((mine[:, :split], SPLIT_A), (mine[:, split:], SPLIT_B)):
        stack = jnp.stack([part] + [along(part, d) for d in range(1, n_group)])
        dense += collect(stack[None], order)

    inner_turned = expert_inner[0].T
    outer_here = expert_outer[0]
    piece_a = lax.dynamic_slice_in_dim(inner_turned, r * block, block, 0)
    piece_b = lax.dynamic_slice_in_dim(outer_here, r * block, block, 0)
    weights = [(inner_turned, inner_turned, outer_here, outer_here)]
    for d in range(1, n_group):
        weights.append(collect(along(piece_a, d), SPLIT_A) + collect(along(piece_b, d), SPLIT_B))

    steps = jnp.arange(PIECES, dtype=jnp.int32)
    swap = ((steps & 1) << 1) | ((steps >> 1) & 1)
    pieces = r ^ offset_of(steps, SPLIT_A)
    halves = [
        jnp.minimum(steps, 3), jnp.maximum(steps - 4, 0),
        jnp.where(steps < 4, swap, 3), jnp.where(steps < 4, 0, swap),
    ]
    own = [
        pieces[jnp.minimum(steps, 3)], pieces[jnp.maximum(steps, 4)],
        pieces[jnp.minimum(steps, 3)], pieces[jnp.maximum(steps, 4)],
    ]

    def place_of(turn):
        expert = (z + n_group - turn) % n_group
        head = jnp.stack([z, r, expert, live_count[0].astype(jnp.int32)])
        return jnp.concatenate([head] + (own if turn == 0 else halves) + [pieces]).astype(jnp.int32)

    experts = (z + n_group - jnp.arange(n_group, dtype=jnp.int32)) % n_group
    chosen = routes[:, None] == experts[None, :, None, None]
    seats = jnp.max(jnp.where(chosen, slot_ids[:, None], -1), axis=-1)
    slots_lane = jnp.pad(seats, ((0, 0), (0, 8 - n_group), (0, PAD - length)), constant_values=-1)
    slots_row = jnp.pad(seats.transpose(0, 2, 1), ((0, 0), (0, 0), (0, 8 - n_group)), constant_values=-1)

    place = place_of(0)
    qkv, att, res, tok, gates, full, small = forward_call(place, images, cotangent, *dense)
    rows, back, biases, shards_a, shards_b = [], [], [], [], []
    for turn in range(n_group):
        out = expert_call(turn, place_of(turn), tok, slots_lane, gates, small, weights[turn])
        rows.append(out[4])
        back.append(out[5])
        biases.append(out[6])
        sum_a = reduce(out[0], out[1], SPLIT_A)
        sum_b = reduce(out[2], out[3], SPLIT_B)
        shards_a.append(along(sum_a, -turn) if turn else sum_a)
        shards_b.append(along(sum_b, -turn) if turn else sum_b)

    block_out, input_grad, *dense_grads = backward_call(
        place, images, cotangent, qkv, att, res, tok, slots_row, full, small, rows, back, biases
    )

    def total(values):
        return sum(v.astype(F32) for v in values).astype(BF16)

    halves_a = collect(total(shards_a), SPLIT_A)
    halves_b = collect(total(shards_b), SPLIT_B)
    dense_halves = []
    for keep, send, order in ((dense_grads[0], dense_grads[1], SPLIT_A), (dense_grads[2], dense_grads[3], SPLIT_B)):
        value = reduce(keep, send, order)[0]
        value = total([value[0]] + [along(value[d], -d) for d in range(1, n_group)])
        dense_halves += collect(value[None], order)
    grad_qkv, grad_proj, grad_small, turned = finish_dense_call(place, *dense_halves, model)
    grad_inner, grad_outer = finish_call(place, *halves_a, *halves_b)
    return (
        block_out,
        input_grad,
        turned[4],
        turned[5],
        grad_qkv,
        turned[9:11].reshape(-1),
        grad_proj,
        turned[6],
        turned[7],
        turned[8],
        grad_small[:, :n_group],
        grad_inner,
        turned[12:28].reshape(1, -1),
        grad_outer,
        turned[28:32].reshape(1, -1),
    )


def solution(mesh):
    both = ("replica", "group")
    in_specs = (
        P(both, None, None), P("group"), P("group"), P("group", None), P("group"), P("group", None),
        P("group"), P("group"), P("group"), P("group", None), P("group", None, None), P("group", None),
        P("group", None, None), P("group", None), P(both), P(both, None, None), P(both, None, None),
        P(both, None, None),
    )
    out_specs = (
        P(both, None, None), P(both, None, None), P("group"), P("group"), P("group", None), P("group"),
        P("group", None), P("group"), P("group"), P("group"), P("group", None), P("group", None, None),
        P("group", None), P("group", None, None), P("group", None),
    )
    body = functools.partial(local, n_replica=mesh.shape["replica"], n_group=mesh.shape["group"])
    return jax.shard_map(body, mesh=mesh, in_specs=in_specs, out_specs=out_specs, check_vma=False)
```

```python
import functools
import math

import jax
import jax.numpy as jnp
from jax import lax
from jax.experimental import pallas as pl
from jax.experimental.pallas import tpu as pltpu
from jax.sharding import PartitionSpec as P

HEADS = 8
CAP = 640
NORM_EPS = 1e-06
F32 = jnp.float32
BF16 = jnp.bfloat16
PAD = 256
PIECES = 8
BITS = (2, 4, 1)
WIDE = 512
SMALL = 128
MIB = 1 << 20


def offset_of(position):
    total = 0
    for k, bit in enumerate(BITS):
        total = total + ((position >> k) & 1) * bit
    return total


def dot_nn(a, b):
    return lax.dot_general(a, b, (((1,), (0,)), ((), ())), preferred_element_type=F32)


def dot_nt(a, b):
    return lax.dot_general(a, b, (((1,), (1,)), ((), ())), preferred_element_type=F32)


def dot_tn(a, b):
    return lax.dot_general(a, b, (((0,), (0,)), ((), ())), preferred_element_type=F32)


def norm_parts(values):
    center = values - jnp.mean(values, axis=-1, keepdims=True)
    spread = jnp.mean(center * center, axis=-1, keepdims=True)
    rstd = lax.rsqrt(spread + NORM_EPS)
    return center * rstd, rstd


def gelu_parts(v):
    size = jnp.abs(v)
    density = jnp.exp(v * v * (-0.5)) * 0.3989422804014327
    t = 1.0 / (1.0 + 0.2316418882 * size)
    series = t * (
        0.319381530 + t * (-0.356563782 + t * (1.781477937 + t * (-1.821255978 + t * 1.330274429)))
    )
    tail = density * series
    phi = jnp.where(v < 0, tail, 1.0 - tail)
    return v * phi, phi + v * density


def params(megabytes=60):
    return pltpu.CompilerParams(vmem_limit_bytes=megabytes * MIB)


def cost(microseconds, megabytes):
    return pl.CostEstimate(flops=int(microseconds * 1.1e9), bytes_accessed=int(megabytes * MIB), transcendentals=0)


def padded(length):
    return -(-length // 16) * 16


def pack_kernel(place, qkv, proj, router, *refs):
    *vectors, out, lines, turned = refs
    depth = out.shape[0]
    row = pl.multiple_of(place[1] * depth, depth)
    width = qkv.shape[1] + proj.shape[1]
    lines[...] = jnp.zeros_like(lines)
    lines[: router.shape[0], :] = router[...].astype(F32)
    at = 4
    for vector in vectors:
        values = vector[...].astype(F32).reshape(1, -1)
        for c in range(values.shape[1] // 128):
            lines[at : at + 1, :] = values[:, c * 128 : (c + 1) * 128]
            at += 1
        if at == 11:
            at = 12
    turned[...] = lines[...].T
    out[:, : qkv.shape[1]] = qkv[pl.ds(row, depth), :]
    out[:, qkv.shape[1] : width] = proj[pl.ds(row, depth), :]
    out[:, width:] = turned[pl.ds(row, depth), :].astype(BF16)


def pack_call(place, qkv, proj, router, vectors):
    shard = qkv.shape[0]
    vmem = pl.BlockSpec(memory_space=pltpu.VMEM)
    return pl.pallas_call(
        pack_kernel,
        out_shape=jax.ShapeDtypeStruct((shard // PIECES, qkv.shape[1] + proj.shape[1] + SMALL), BF16),
        in_specs=[pl.BlockSpec(memory_space=pltpu.SMEM)] + [vmem] * (3 + len(vectors)),
        out_specs=vmem,
        scratch_shapes=[pltpu.VMEM((SMALL, shard), F32), pltpu.VMEM((shard, SMALL), F32)],
        cost_estimate=cost(2, 1),
        name="pack_dense",
    )(place, qkv, proj, router.T, *vectors)


def cut_kernel(place, inner, outer, out):
    out[0] = inner[0].T
    out[1] = outer[0]


def cut_call(place, inner, outer):
    _, model, hidden = inner.shape
    block = hidden // PIECES
    return pl.pallas_call(
        cut_kernel,
        out_shape=jax.ShapeDtypeStruct((2, block, model), BF16),
        grid_spec=pltpu.PrefetchScalarGridSpec(
            num_scalar_prefetch=1,
            grid=(1,),
            in_specs=[
                pl.BlockSpec((1, model, block), lambda i, s: (0, 0, s[1])),
                pl.BlockSpec((1, block, model), lambda i, s: (0, s[1], 0)),
            ],
            out_specs=pl.BlockSpec((2, block, model), lambda i, s: (0, 0, 0)),
        ),
        compiler_params=params(),
        cost_estimate=cost(2, 1),
        name="cut_own",
    )(place, inner, outer)


def forward_kernel(
    place, images, cot, *refs,
):
    dense = refs[:PIECES]
    qkv_out, att_out, res_out, lse_out, tok_out, gates_out, full_out, small_out, rows = refs[PIECES:]
    model = images.shape[2]
    length = images.shape[1]
    size = rows.shape[0]
    parts, depth = dense[0].shape[:2]

    @pl.when(pl.program_id(0) == 0)
    def _():
        z, r = place[0], place[1]
        for pos in range(PIECES):
            for d in range(parts):
                owner = lax.rem(z + parts - d, parts) * PIECES
                row = pl.multiple_of((owner + jnp.bitwise_xor(r, offset_of(pos))) * depth, depth)
                full_out[pl.ds(row, depth), :] = dense[pos][d]
        small_out[...] = full_out[:, 4 * model :].astype(F32).T
        rows[...] = jnp.zeros_like(rows)

    def vector(row):
        return small_out[row : row + 1, :]

    rows[:length, :] = images[0].astype(F32)
    x = rows[...]
    xhat, _ = norm_parts(x)
    normed = (xhat * vector(4) + vector(5)).astype(BF16)
    projected = dot_nn(normed, full_out[:, : 3 * model])
    bias_parts = []
    for part in range(parts):
        lanes = slice(part * 128, part * 128 + 128)
        bias_parts += [small_out[9:10, lanes], small_out[10:11, lanes]]
    pair = jnp.concatenate(bias_parts, axis=1)
    qkv_out[0, :, :model] = (projected[:, :model] + pair[:, :model]).astype(BF16)
    qkv_out[0, :, model : 2 * model] = projected[:, model : 2 * model].astype(BF16)
    qkv_out[0, :, 2 * model :] = (projected[:, 2 * model :] + pair[:, model:]).astype(BF16)
    qkv_out[0, length:, :] = jnp.zeros((size - length, 3 * model), BF16)

    head = model // HEADS
    first = lax.broadcasted_iota(jnp.int32, (1, 2 * head), 1) < head
    real = lax.broadcasted_iota(jnp.int32, (1, size), 1) < length
    column = lax.broadcasted_iota(jnp.int32, (size, 128), 1)
    scale = 1.0 / math.sqrt(head)
    lse = jnp.zeros((size, 128), F32)
    attended = []
    for two in range(HEADS // 2):
        lanes = lambda start: slice(start + two * 2 * head, start + (two + 1) * 2 * head)
        q2, k2, v2 = (qkv_out[0, :, lanes(s * model)] for s in range(3))
        zero = jnp.zeros_like(q2)
        stack = jnp.concatenate([jnp.where(first, q2, zero), jnp.where(first, zero, q2)], axis=0)
        scores = jnp.where(real, dot_nt(stack, k2) * scale, -1e30)
        peak = jnp.max(scores, axis=-1, keepdims=True)
        e = jnp.exp(scores - peak)
        total = jnp.sum(e, axis=-1, keepdims=True)
        probs = (e * (1.0 / total)).astype(BF16)
        both = dot_nn(probs, v2)
        attended.append(jnp.where(first, both[:size], both[size:]).astype(BF16))
        logs = peak + jnp.log(total)
        lse = jnp.where(column == 2 * two, logs[:size], lse)
        lse = jnp.where(column == 2 * two + 1, logs[size:], lse)
    lse_out[0] = lse
    attended = jnp.concatenate(attended, axis=1)
    att_out[0] = attended
    residual = x + (dot_nn(attended, full_out[:, 3 * model : 4 * model]) + vector(6))
    res_out[0] = residual
    xhat2, _ = norm_parts(residual)
    normed2 = (xhat2 * vector(7) + vector(8)).astype(BF16)
    tail = length // 16 * 16
    tok_out[tail:, :] = jnp.zeros((PAD - tail, 2 * model), BF16)
    tok_out[:size, :model] = normed2
    tok_out[:length, model:] = cot[0]
    logits = dot_nt(small_out[0:8, :].astype(BF16), tok_out[:, :model])
    experts = lax.broadcasted_iota(jnp.int32, logits.shape, 0) < parts
    logits = jnp.where(experts, logits, -jnp.inf)
    e = jnp.exp(logits - jnp.max(logits, axis=0, keepdims=True))
    gates_out[0] = e / jnp.sum(e, axis=0, keepdims=True)


def whole(a):
    return pl.BlockSpec(a.shape, lambda i, *_: (0,) * len(a.shape))


def image(*dims):
    return pl.BlockSpec((1,) + dims, lambda i, *_: (i, 0, 0))


def forward_call(place, images, cot, dense):
    count, length, model = images.shape
    size = padded(length)
    outs = (
        jax.ShapeDtypeStruct((count, size, 3 * model), BF16),
        jax.ShapeDtypeStruct((count, size, model), BF16),
        jax.ShapeDtypeStruct((count, size, model), F32),
        jax.ShapeDtypeStruct((count, size, 128), F32),
        jax.ShapeDtypeStruct((count * PAD, 2 * model), BF16),
        jax.ShapeDtypeStruct((count, 8, PAD), F32),
        jax.ShapeDtypeStruct((model, 4 * model + SMALL), BF16),
        jax.ShapeDtypeStruct((SMALL, model), F32),
    )
    return pl.pallas_call(
        forward_kernel,
        out_shape=outs,
        grid_spec=pltpu.PrefetchScalarGridSpec(
            num_scalar_prefetch=1,
            grid=(count,),
            in_specs=[image(length, model), image(length, model)] + [whole(d) for d in dense],
            out_specs=[
                image(size, 3 * model), image(size, model), image(size, model), image(size, 128),
                pl.BlockSpec((PAD, 2 * model), lambda i, *_: (i, 0)),
                image(8, PAD), whole(outs[6]), whole(outs[7]),
            ],
            scratch_shapes=[pltpu.VMEM((size, model), F32)],
        ),
        compiler_params=params(),
        cost_estimate=cost(12, 12),
        name="attention_forward",
    )(place, images, cot, *dense)


def expert_kernel(place, slots, gates, small, tok, *refs, turn, sources, count_in):
    arrays = refs[:count_in]
    keep, send, pair_out, bias_out = refs[count_in : count_in + 4]
    tokens, onehot, buffer, grad_slots, rows, back, mine, inners, outers, staged, token_sem, in_sems, out_sems = (
        refs[count_in + 4 :]
    )
    local = sources is None
    count = slots.shape[0]
    model = buffer.shape[1]
    block = outers.shape[1]
    per = staged.shape[1]
    steps = staged.shape[0]

    token_copy = pltpu.make_async_copy(tok, tokens, token_sem)
    token_copy.start()
    loads = []
    for pos in range(PIECES):
        for side, matrices in enumerate((inners, outers)):
            if local:
                start = pl.multiple_of(jnp.bitwise_xor(place[1], offset_of(pos)) * block, block)
                source = arrays[1].at[0, pl.ds(start, block)] if side else arrays[0].at[0, :, pl.ds(start, block)]
            else:
                which, at = sources(pos, side)
                source = arrays[which].at[at]
            loads.append(pltpu.make_async_copy(source, matrices.at[pos], in_sems.at[pos, side]))

    expert = lax.rem(place[0] + place[3] - turn, place[3])
    lanes = pl.ds(pl.multiple_of(expert * 128, 128), 128)
    mine[...] = small[:, lanes]
    where = lax.broadcasted_iota(jnp.int32, (CAP, PAD), 0)
    gate = jnp.zeros((CAP, 128), F32)
    for b in range(count):
        mask = where == slots[b, turn : turn + 1, :]
        onehot[:, b * PAD : (b + 1) * PAD] = mask.astype(F32).astype(BF16)
        weighted = jnp.where(mask, gates[b, pl.ds(expert, 1), :], 0.0)
        gate = gate + weighted[:, :128] + weighted[:, 128:]
    gate = jnp.sum(gate, axis=1, keepdims=True)
    outer_bias = jnp.concatenate([mine[28 + c : 29 + c, :] for c in range(model // 128)], axis=1)
    token_copy.wait()
    for copy in loads:
        copy.start()
    buffer[...] = dot_nn(onehot[...], tokens[:, :model]).astype(BF16)
    grads = (dot_nn(onehot[...], tokens[:, model:]) * gate).astype(BF16)
    grad_slots[...] = grads
    sums = jnp.sum(grads.astype(F32), axis=0, keepdims=True)
    for c in range(model // 128):
        bias_out[16 + c : 17 + c, :] = sums[:, c * 128 : (c + 1) * 128]
    bias_out[20:32, :] = jnp.zeros((12, 128), F32)

    def first_products(i):
        for copy in loads[2 * i * per : 2 * (i + 1) * per]:
            copy.wait()
        buf, gs = buffer[...], grad_slots[...]
        here = slice(i * per, (i + 1) * per)
        lines = [
            jnp.bitwise_xor(place[1], offset_of(pos)) * (block // 128) + c
            for pos in range(here.start, here.stop)
            for c in range(block // 128)
        ]
        bias = jnp.concatenate([mine[pl.ds(12 + line, 1), :] for line in lines], axis=1)
        if local:
            hidden = jnp.concatenate([dot_nn(buf, inners[pos]) for pos in range(here.start, here.stop)], axis=1)
        else:
            hidden = dot_nt(buf, inners[here].reshape(per * block, model))
        return hidden + bias, dot_nt(gs, outers[here].reshape(per * block, model)), lines

    stores = []
    for i in range(steps):
        hidden, grad_active, lines = first_products(i)
        here = slice(i * per, (i + 1) * per)
        active, slope = gelu_parts(hidden)
        active = active.astype(BF16)
        grad_low = (grad_active * slope).astype(BF16)
        sums = jnp.sum(grad_low.astype(F32), axis=0, keepdims=True)
        for k, line in enumerate(lines):
            bias_out[pl.ds(line, 1), :] = sums[:, k * 128 : (k + 1) * 128]
        staged[i, :, 0] = dot_tn(grad_low, buffer[...]).astype(BF16).reshape(per, block, model)
        staged[i, :, 1] = dot_tn(active, grad_slots[...]).astype(BF16).reshape(per, block, model)
        out = keep if i < steps // 2 else send
        stores.append(pltpu.make_async_copy(staged.at[i], out.at[:, i % (steps // 2)], out_sems.at[i]))
        stores[-1].start()
        new_rows = dot_nn(active, outers[here].reshape(per * block, model))
        if local:
            new_back = sum(
                dot_nt(grad_low[:, j * block : (j + 1) * block], inners[i * per + j]) for j in range(per)
            )
        else:
            new_back = dot_nn(grad_low, inners[here].reshape(per * block, model))
        rows[...] = new_rows + (outer_bias if i == 0 else rows[...])
        back[...] = new_back if i == 0 else new_back + back[...]
    pair_out[:, :model] = rows[...].astype(BF16)
    pair_out[:, model:] = back[...].astype(BF16)
    for copy in stores:
        copy.wait()


def expert_call(turn, place, tok, slots, gates, small, weights):
    arrays, sources = weights
    model = tok.shape[1] // 2
    count = slots.shape[0]
    block = arrays[1].shape[1] // PIECES if sources is None else arrays[0].shape[-2]
    per = WIDE // block
    steps = PIECES // per
    vmem = pl.BlockSpec(memory_space=pltpu.VMEM)
    anywhere = pl.BlockSpec(memory_space=pl.ANY)
    half = jax.ShapeDtypeStruct((2, 2, 2, block, model), BF16)
    return pl.pallas_call(
        functools.partial(expert_kernel, turn=turn, sources=sources, count_in=len(arrays)),
        out_shape=(
            half,
            half,
            jax.ShapeDtypeStruct((CAP, 2 * model), BF16),
            jax.ShapeDtypeStruct((32, 128), F32),
        ),
        in_specs=[pl.BlockSpec(memory_space=pltpu.SMEM), vmem, vmem, vmem, anywhere] + [anywhere] * len(arrays),
        out_specs=[anywhere, anywhere, vmem, vmem],
        scratch_shapes=[
            pltpu.VMEM(tok.shape, BF16),
            pltpu.VMEM((CAP, count * PAD), BF16),
            pltpu.VMEM((CAP, model), BF16),
            pltpu.VMEM((CAP, model), BF16),
            pltpu.VMEM((CAP, model), F32),
            pltpu.VMEM((CAP, model), F32),
            pltpu.VMEM((SMALL, 128), F32),
            pltpu.VMEM((PIECES, model, block) if sources is None else (PIECES, block, model), BF16),
            pltpu.VMEM((PIECES, block, model), BF16),
            pltpu.VMEM((steps, per, 2, block, model), BF16),
            pltpu.SemaphoreType.DMA(()),
            pltpu.SemaphoreType.DMA((PIECES, 2)),
            pltpu.SemaphoreType.DMA((steps,)),
        ],
        compiler_params=params(),
        cost_estimate=cost(18, 14),
        name="expert",
    )(place, slots, gates, small, tok, *arrays)


def norm_back(inner, xhat, rstd):
    return rstd * (
        inner - jnp.mean(inner, axis=-1, keepdims=True) - xhat * jnp.mean(inner * xhat, axis=-1, keepdims=True)
    )


def combine_kernel(place, *refs, turns, lo, carried, last):
    cot, att, res, tok, slots, full, small = refs[:7]
    pairs = refs[7 : 7 + turns]
    biases = refs[7 + turns : 7 + 2 * turns]
    before = refs[7 + 2 * turns : 7 + 2 * turns + 6 * carried]
    *outs, cots = refs[7 + 2 * turns + 6 * carried :]
    block_out, gres_out, gatt_out, acc_proj, acc_router, acc_small = outs[:6]
    b = pl.program_id(0)
    length, model = cot.shape[1:]
    size = cots.shape[0]
    parts = turns

    @pl.when(b == 0)
    def _():
        cots[...] = jnp.zeros_like(cots)
        for k, acc in enumerate((acc_proj, acc_router, acc_small)):
            acc[...] = before[3 + k][...] if carried else jnp.zeros_like(acc)

    def vector(row):
        return small[row : row + 1, :]

    def add_row(row, values):
        acc_small[row : row + 1, :] += jnp.sum(values, axis=0, keepdims=True)

    live = (lo + b < place[2]).astype(F32)
    cots[:length, :] = cot[0].astype(F32) * live
    grad_out = cots[...]
    residual = res[0]
    xhat2, rstd2 = norm_parts(residual)
    normed2 = tok[:size, :model]
    router = full[:, 4 * model :]

    logits = dot_nn(normed2, router)
    lane = lax.broadcasted_iota(jnp.int32, logits.shape, 1)
    logits = jnp.where(lane < parts, logits, -jnp.inf)
    e = jnp.exp(logits - jnp.max(logits, axis=-1, keepdims=True))
    probs = e / jnp.sum(e, axis=-1, keepdims=True)

    seat = lax.broadcasted_iota(jnp.int32, (size, CAP), 1)
    mixture = None
    grad_n2 = None
    grad_probs = jnp.zeros_like(probs)
    for j in range(turns):
        expert = lax.rem(place[0] + parts - j, parts)
        mask = (slots[0][:, j : j + 1] == seat).astype(F32).astype(BF16)
        both = dot_nn(mask, pairs[j][...])
        picked = both[:, :model]
        gate = jnp.sum(jnp.where(lane == expert, probs, 0.0), axis=-1, keepdims=True)
        mixture = gate * picked if mixture is None else mixture + gate * picked
        grad_gate = jnp.sum(grad_out * picked, axis=-1, keepdims=True)
        grad_probs = jnp.where(lane == expert, grad_gate, grad_probs)
        grad_n2 = both[:, model:] if grad_n2 is None else grad_n2 + both[:, model:]
    block_out[0] = ((residual + mixture) * live).astype(BF16)[:length]
    grad_logits = probs * (grad_probs - jnp.sum(probs * grad_probs, axis=-1, keepdims=True))
    grad_logits = grad_logits.astype(BF16)
    grad_n2 = grad_n2 + dot_nt(grad_logits, router)
    acc_router[...] += dot_tn(normed2, grad_logits)

    add_row(7, grad_n2 * xhat2)
    add_row(8, grad_n2)
    grad_res = grad_out + norm_back(grad_n2 * vector(7), xhat2, rstd2)
    gres_out[0] = grad_res
    branch = grad_res.astype(BF16)
    add_row(6, branch.astype(F32))
    acc_proj[...] += dot_tn(att[0], branch)
    gatt_out[0] = dot_nt(branch, full[:, 3 * model : 4 * model]).astype(BF16)

    if not last:
        return

    @pl.when(b == pl.num_programs(0) - 1)
    def _():
        late_out = outs[-1]
        for j in range(turns):
            expert = lax.rem(place[0] + parts - j, parts)
            acc_small[12:32, pl.ds(pl.multiple_of(expert * 128, 128), 128)] = biases[j][0:20, :]
        late_out[:, :model] = acc_proj[...].astype(BF16)
        late_out[:, model:] = (acc_router[...] + acc_small[...].T).astype(BF16)


def part_of(lo, *dims):
    return pl.BlockSpec((1,) + dims, lambda i, *_: (lo + i, 0, 0))


def combine_call(lo, hi, before, place, cot, att, res, tok, slots, full, small, pairs, biases):
    count, length, model = cot.shape
    size = att.shape[1]
    turns = len(pairs)
    last = hi == count
    outs = (
        jax.ShapeDtypeStruct((count, length, model), BF16),
        jax.ShapeDtypeStruct((count, size, model), F32),
        jax.ShapeDtypeStruct((count, size, model), BF16),
        jax.ShapeDtypeStruct((model, model), F32),
        jax.ShapeDtypeStruct((model, SMALL), F32),
        jax.ShapeDtypeStruct((SMALL, model), F32),
    ) + ((jax.ShapeDtypeStruct((model, model + SMALL), BF16),) if last else ())
    image = functools.partial(part_of, lo)
    inputs = (cot, att, res, tok, slots, full, small, *pairs, *biases)
    return pl.pallas_call(
        functools.partial(combine_kernel, turns=turns, lo=lo, carried=len(before) > 0, last=last),
        out_shape=outs,
        grid_spec=pltpu.PrefetchScalarGridSpec(
            num_scalar_prefetch=1,
            grid=(hi - lo,),
            in_specs=[
                image(length, model), image(size, model), image(size, model),
                pl.BlockSpec((PAD, 2 * model), lambda i, *_: (lo + i, 0)),
                image(size, slots.shape[2]),
            ] + [whole(a) for a in inputs[5:]] + [pl.BlockSpec(memory_space=pl.ANY)] * min(3, len(before))
            + [whole(a) for a in before[3:]],
            out_specs=[image(length, model), image(size, model), image(size, model)] + [whole(o) for o in outs[3:]],
            scratch_shapes=[pltpu.VMEM((size, model), F32)],
        ),
        input_output_aliases={1 + len(inputs) + k: k for k in range(len(before))},
        compiler_params=params(),
        cost_estimate=cost(4 * (hi - lo), 14),
        name="combine",
    )(place, *inputs, *before)


def backward_kernel(place, images, qkv, lse, gres, gatt, full, small, late, *refs, parts, carried, last):
    before = refs[: 3 * carried]
    *outs, rows = refs[3 * carried :]
    input_grad, acc_qkv, acc_small = outs[:3]
    b = pl.program_id(0)
    length, model = images.shape[1:]
    size = rows.shape[0]

    @pl.when(b == 0)
    def _():
        rows[...] = jnp.zeros_like(rows)
        for k, acc in enumerate((acc_qkv, acc_small)):
            acc[...] = before[1 + k][...] if carried else jnp.zeros_like(acc)

    def vector(row):
        return small[row : row + 1, :]

    def add_row(row, values):
        acc_small[row : row + 1, :] += jnp.sum(values, axis=0, keepdims=True)

    head = model // HEADS
    first = lax.broadcasted_iota(jnp.int32, (1, 2 * head), 1) < head
    real = lax.broadcasted_iota(jnp.int32, (1, size), 1) < length
    scale = 1.0 / math.sqrt(head)
    grads = [[], [], []]
    for two in range(HEADS // 2):
        lanes = lambda start: slice(start + two * 2 * head, start + (two + 1) * 2 * head)
        q2, k2, v2 = (qkv[0, :, lanes(s * model)] for s in range(3))
        g2 = gatt[0, :, lanes(0)]
        zero = jnp.zeros_like(q2)
        stack = lambda t: jnp.concatenate([jnp.where(first, t, zero), jnp.where(first, zero, t)], axis=0)
        merge = lambda t: jnp.where(first, t[:size], t[size:])
        qs, gs = stack(q2), stack(g2)
        logs = jnp.concatenate([lse[0, :, 2 * two : 2 * two + 1], lse[0, :, 2 * two + 1 : 2 * two + 2]], axis=0)
        weights = jnp.where(real, jnp.exp(dot_nt(qs, k2) * scale - logs), 0.0)
        grad_weights = dot_nt(gs, v2)
        grad_scores = weights * (grad_weights - jnp.sum(grad_weights * weights, axis=-1, keepdims=True))
        grad_scores = grad_scores.astype(BF16)
        grads[0].append((merge(dot_nn(grad_scores, k2)) * scale).astype(BF16))
        grads[1].append((dot_tn(grad_scores, qs) * scale).astype(BF16))
        grads[2].append(dot_tn(weights.astype(BF16), gs).astype(BF16))
    grad_projected = jnp.concatenate(grads[0] + grads[1] + grads[2], axis=1)
    rows[:length, :] = images[0].astype(F32)
    xhat1, rstd1 = norm_parts(rows[...])
    normed = (xhat1 * vector(4) + vector(5)).astype(BF16)
    acc_qkv[:, : 3 * model] += dot_tn(normed, grad_projected)
    grad_normed = dot_nt(grad_projected, full[:, : 3 * model])
    add_row(4, grad_normed * xhat1)
    add_row(5, grad_normed)
    add_row(32, grad_projected[:, :model].astype(F32))
    add_row(33, grad_projected[:, 2 * model :].astype(F32))
    input_grad[0] = (gres[0] + norm_back(grad_normed * vector(4), xhat1, rstd1))[:length]

    if not last:
        return

    @pl.when(b == pl.num_programs(0) - 1)
    def _():
        keep, send = outs[-2:]
        for part in range(parts):
            for k in range(2):
                start = (part * 2 + k) * 128
                source = 32 + start // model
                acc_small[9 + k : 10 + k, part * 128 : part * 128 + 128] = acc_small[
                    source : source + 1, start % model : start % model + 128
                ]
        acc_small[32:34, :] = jnp.zeros((2, model), F32)
        acc_qkv[:, 3 * model :] = acc_small[...].T + late[:, model:].astype(F32)
        depth = keep.shape[2]
        for pos in range(PIECES):
            for d in range(parts):
                owner = lax.rem(place[0] + parts - d, parts) * PIECES
                row = pl.multiple_of((owner + jnp.bitwise_xor(place[1], offset_of(pos))) * depth, depth)
                out = keep if pos < PIECES // 2 else send
                spot = pos % (PIECES // 2)
                out[spot, d, :, : 3 * model] = acc_qkv[pl.ds(row, depth), : 3 * model].astype(BF16)
                out[spot, d, :, 3 * model : 4 * model] = late[pl.ds(row, depth), :model]
                out[spot, d, :, 4 * model :] = acc_qkv[pl.ds(row, depth), 3 * model :].astype(BF16)


def backward_call(lo, hi, before, place, images, qkv, lse, gres, gatt, full, small, late, turns):
    count, length, model = images.shape
    size = qkv.shape[1]
    depth = model // (turns * PIECES)
    last = hi == count
    half = jax.ShapeDtypeStruct((PIECES // 2, turns, depth, 4 * model + SMALL), BF16)
    outs = (
        jax.ShapeDtypeStruct((count, length, model), F32),
        jax.ShapeDtypeStruct((model, 3 * model + SMALL), F32),
        jax.ShapeDtypeStruct((SMALL, model), F32),
    ) + ((half, half) if last else ())
    image = functools.partial(part_of, lo)
    inputs = (images, qkv, lse, gres, gatt, full, small, late)
    return pl.pallas_call(
        functools.partial(backward_kernel, parts=turns, carried=len(before) > 0, last=last),
        out_shape=outs,
        grid_spec=pltpu.PrefetchScalarGridSpec(
            num_scalar_prefetch=1,
            grid=(hi - lo,),
            in_specs=[
                image(length, model), image(size, 3 * model), image(size, 128), image(size, model),
                image(size, model), whole(full), whole(small), whole(late),
            ] + [pl.BlockSpec(memory_space=pl.ANY)] * min(1, len(before)) + [whole(a) for a in before[1:]],
            out_specs=[image(length, model)] + [whole(o) for o in outs[1:]],
            scratch_shapes=[pltpu.VMEM((size, model), F32)],
        ),
        input_output_aliases={1 + len(inputs) + k: k for k in range(len(before))},
        compiler_params=params(),
        cost_estimate=cost(4 * (hi - lo), 14),
        name="attention_backward",
    )(place, *inputs, *before)


def finish_kernel(place, *refs):
    pieces = refs[: PIECES // 2]
    inner_out, outer_out = refs[-2:]
    for k, piece in enumerate(pieces):

        @pl.when(pl.program_id(0) == k)
        def _():
            inner_out[0] = piece[0].astype(F32).T
            outer_out[0] = piece[1].astype(F32)


def finish_call(half, place, pieces, outs=()):
    _, block, model = pieces[0].shape
    piece = lambda i, s: jnp.bitwise_xor(s[1], offset_of(i + 4 * half))
    return pl.pallas_call(
        finish_kernel,
        out_shape=(
            jax.ShapeDtypeStruct((1, model, PIECES * block), F32),
            jax.ShapeDtypeStruct((1, PIECES * block, model), F32),
        ),
        grid_spec=pltpu.PrefetchScalarGridSpec(
            num_scalar_prefetch=1,
            grid=(PIECES // 2,),
            in_specs=[whole(p) for p in pieces] + [pl.BlockSpec(memory_space=pl.ANY)] * len(outs),
            out_specs=[
                pl.BlockSpec((1, model, block), lambda i, s: (0, 0, piece(i, s))),
                pl.BlockSpec((1, block, model), lambda i, s: (0, piece(i, s), 0)),
            ],
        ),
        input_output_aliases={1 + len(pieces) + k: k for k in range(len(outs))},
        compiler_params=params(),
        cost_estimate=cost(4, 6),
        name="finish_experts",
    )(place, *pieces, *outs)


def finish_dense_kernel(place, *refs):
    pieces = refs[:PIECES]
    qkv_out, proj_out, router_out, inner_out, outer_out, rest_out, table = refs[PIECES:]
    model = proj_out.shape[1]
    depth = pieces[0].shape[0]
    for pos in range(PIECES):
        row = pl.multiple_of(jnp.bitwise_xor(place[1], offset_of(pos)) * depth, depth)
        block = pieces[pos][...].astype(F32)
        qkv_out[pl.ds(row, depth), :] = block[:, : 3 * model]
        proj_out[pl.ds(row, depth), :] = block[:, 3 * model : 4 * model]
        table[pl.ds(row, depth), :] = block[:, 4 * model :]
    table[...] = table[...].T
    router_out[...] = table[: router_out.shape[0], :]
    rest_out[...] = table[4 : 4 + rest_out.shape[0], :]
    for c in range(inner_out.shape[1] // 128):
        inner_out[:, c * 128 : (c + 1) * 128] = table[12 + c : 13 + c, :]
    for c in range(outer_out.shape[1] // 128):
        outer_out[:, c * 128 : (c + 1) * 128] = table[28 + c : 29 + c, :]


def finish_dense_call(place, pieces, model, parts, hidden):
    rows = pieces[0].shape[0] * PIECES
    vmem = pl.BlockSpec(memory_space=pltpu.VMEM)
    return pl.pallas_call(
        finish_dense_kernel,
        out_shape=(
            jax.ShapeDtypeStruct((rows, 3 * model), F32),
            jax.ShapeDtypeStruct((rows, model), F32),
            jax.ShapeDtypeStruct((parts, rows), F32),
            jax.ShapeDtypeStruct((1, hidden), F32),
            jax.ShapeDtypeStruct((1, model), F32),
            jax.ShapeDtypeStruct((8, rows), F32),
        ),
        in_specs=[pl.BlockSpec(memory_space=pltpu.SMEM)] + [vmem] * PIECES,
        scratch_shapes=[pltpu.VMEM((rows, SMALL), F32)],
        cost_estimate=cost(2, 2),
        name="finish_dense",
    )(place, *pieces)


def join(*values):
    return lax.optimization_barrier(values)


def local(
    images, attn_norm_gain, attn_norm_bias, qkv_weight, query_value_bias, proj_weight, proj_bias,
    moe_norm_gain, moe_norm_bias, router_weight, expert_inner, expert_inner_bias, expert_outer,
    expert_outer_bias, live_count, routes, slot_ids, cotangent, *, n_replica, n_group,
):
    count, length, model = images.shape
    shard = qkv_weight.shape[0]
    hidden = expert_inner.shape[2]
    size = padded(length)
    z = lax.axis_index("group").astype(jnp.int32)
    r = lax.axis_index("replica").astype(jnp.int32) & (PIECES - 1)
    place = jnp.stack([z, r, live_count[0].astype(jnp.int32), jnp.int32(n_group)])

    def across(value, bit):
        return lax.ppermute(value, "replica", [(i, i ^ bit) for i in range(n_replica)])

    def along(value, shift):
        return lax.ppermute(value, "group", [(i, (i + shift) % n_group) for i in range(n_group)])

    def plus(*values):
        return sum(v.astype(F32) for v in values).astype(BF16)

    def both(value, bit):
        return jnp.concatenate([value, across(value, bit)], axis=0)

    def spread(value):
        return [value] + [across(value, offset_of(pos)) for pos in range(1, PIECES // 2)]

    def rest_of_replicas(value):
        bit = PIECES
        while bit < n_replica:
            value = plus(value, across(value, bit))
            bit *= 2
        return value

    shifts = list(range(1, n_group))

    vectors = (attn_norm_gain, attn_norm_bias, proj_bias, moe_norm_gain, moe_norm_bias, query_value_bias)
    mine = pack_call(place, qkv_weight, proj_weight, router_weight, vectors + (expert_inner_bias, expert_outer_bias))
    dense_z = {d: along(mine, d) for d in shifts}

    piece = cut_call(place, expert_inner, expert_outer)
    piece, dense_z = join(piece, dense_z)
    expert_z = {1: along(piece, 1)}
    dense = spread(jnp.stack([mine] + [dense_z[d] for d in range(1, n_group)]))
    dense = dense + [across(v, 1) for v in dense]

    experts = (z + n_group - jnp.arange(n_group, dtype=jnp.int32)) % n_group
    chosen = routes[:, None] == experts[None, :, None, None]
    seats = jnp.max(jnp.where(chosen, slot_ids[:, None], -1), axis=-1)
    slots_lane = jnp.pad(seats, ((0, 0), (0, 8 - n_group), (0, PAD - length)), constant_values=-1)
    slots_row = jnp.pad(
        seats.transpose(0, 2, 1), ((0, 0), (0, size - length), (0, 8 - n_group)), constant_values=-1
    )

    def first_stage(k, got):
        if k == 1:
            return both(got[0][None], 2), both(got[1][None], 4)
        return (both(got[None], 2),)

    def second_stage(k, arrays):
        if k == 1:
            return across(arrays[0], 4), across(arrays[1], 2)
        return (across(arrays[0], 4),)

    def third_stage(arrays):
        return tuple(across(a, 1) for a in arrays)

    def sources(pos, side):
        return pos // 2, (pos % 2, side)

    def sources_first(pos, side):
        x, y, core = pos & 1, pos >> 1 & 1, pos >> 2
        other, at = (x, y) if side else (y, x)
        return 4 * core + 2 * other + side, at

    outs, folds, shards = {}, {}, {}

    at_once = (2, 3)

    def fold_core(k):
        folds[k] = (outs[k][0], across(outs[k][1], 1))

    def fold_one(k):
        keep, core = folds[k]
        if k in at_once:
            quarters = [plus(keep[x, y], core[x, y]) for x, y in ((1, 0), (0, 1), (1, 1))]
            folds[k] = (keep, core) + tuple(across(q, bits) for q, bits in zip(quarters, (2, 4, 6)))
        else:
            folds[k] = (keep, core, across(plus(keep[1], core[1]), 2))

    def fold_two(k):
        keep, core, x = folds[k]
        folds[k] = (keep, core, x, across(plus(keep[0, 1], core[0, 1], x[1]), 4))

    def fold_z(k):
        keep, core, *got = folds[k]
        if k not in at_once:
            got[0] = got[0][0]
        value = rest_of_replicas(plus(keep[0, 0], core[0, 0], *got))
        shards[k] = along(value, -k) if k else value

    one, two, cores = {}, {}, {}
    one[1] = first_stage(1, expert_z[1])
    piece, expert_z[1] = join(piece, expert_z[1])
    expert_z[2] = along(piece, 2)
    one[1], images, dense = join(one[1], images, dense)
    two[1] = second_stage(1, one[1])
    cores[1] = third_stage(one[1])
    qkv, att, res, lse, tok, gates, full, small = forward_call(place, images, cotangent, dense)
    tok, gates, small, piece, one, two, cores, expert_z = join(tok, gates, small, piece, one, two, cores, expert_z)
    tables = (slots_lane, gates, small)

    weights = one[1] + two[1] + cores[1] + third_stage(two[1])
    one[2] = first_stage(2, expert_z[2])
    expert_z[3] = along(piece, 3)
    outs[0] = expert_call(0, place, tok, *tables, ((expert_inner, expert_outer), None))
    outs, tok, weights, one, expert_z = join(outs, tok, weights, one, expert_z)

    two[2] = second_stage(2, one[2])
    cores[2] = third_stage(one[2])
    one[3] = first_stage(3, expert_z[3])
    fold_core(0)
    outs[1] = expert_call(1, place, tok, *tables, (weights, sources_first))
    outs, tok, one, two, cores, folds = join(outs, tok, one, two, cores, folds)

    weights = one[2] + two[2] + cores[2] + third_stage(two[2])
    two[3] = second_stage(3, one[3])
    cores[3] = third_stage(one[3])
    fold_one(0)
    fold_core(1)
    outs[2] = expert_call(2, place, tok, *tables, (weights, sources))
    outs, tok, one, two, cores, folds = join(outs, tok, one, two, cores, folds)

    weights = one[3] + two[3] + cores[3] + third_stage(two[3])
    fold_two(0)
    fold_one(1)
    fold_core(2)
    outs[3] = expert_call(3, place, tok, *tables, (weights, sources))
    outs, folds = join(outs, folds)

    fold_z(0)
    fold_two(1)
    fold_one(2)
    fold_core(3)
    pairs = [outs[k][2] for k in range(n_group)]
    biases = [outs[k][3] for k in range(n_group)]
    block_out, gres, gatt, *_, late = combine_call(
        0, count, (), place, cotangent, att, res, tok, slots_row, full, small, pairs, biases
    )
    gres, gatt, late, folds, shards = join(gres, gatt, late, folds, shards)

    fold_z(1)
    fold_z(2)
    fold_one(3)
    input_grad, *_, keep, send = backward_call(0, count, (), place, images, qkv, lse, gres, gatt, full, small, late, n_group)
    keep, send, folds, shards = join(keep, send, folds, shards)
    fold_z(3)

    value = plus(keep, across(send, 1))
    value = plus(value[0], *(across(value[pos], offset_of(pos)) for pos in range(1, PIECES // 2)))
    value = rest_of_replicas(value)
    value, total = join(value, plus(*shards.values()))
    own_half = spread(total)
    value = plus(*([value[0]] + [along(value[d], -d) for d in range(1, n_group)]))
    value, own_half = join(value, own_half)
    value = spread(value)
    value = value + [across(v, 1) for v in value]
    grad_qkv, grad_proj, grad_router, grad_inner_bias, grad_outer_bias, rest = finish_dense_call(
        place, value, model, n_group, hidden
    )

    other_half = [across(v, 1) for v in own_half]
    grads = finish_call(0, place, own_half)
    grad_inner, grad_outer = finish_call(1, place, other_half, grads)
    return (
        block_out, input_grad, rest[0], rest[1], grad_qkv, rest[5:7].reshape(-1), grad_proj, rest[2], rest[3],
        rest[4], grad_router.T, grad_inner, grad_inner_bias, grad_outer, grad_outer_bias,
    )


def solution(mesh):
    both = ("replica", "group")
    in_specs = (
        P(both, None, None), P("group"), P("group"), P("group", None), P("group"), P("group", None),
        P("group"), P("group"), P("group"), P("group", None), P("group", None, None), P("group", None),
        P("group", None, None), P("group", None), P(both), P(both, None, None), P(both, None, None),
        P(both, None, None),
    )
    out_specs = (
        P(both, None, None), P(both, None, None), P("group"), P("group"), P("group", None), P("group"),
        P("group", None), P("group"), P("group"), P("group"), P("group", None), P("group", None, None),
        P("group", None), P("group", None, None), P("group", None),
    )
    body = functools.partial(local, n_replica=mesh.shape["replica"], n_group=mesh.shape["group"])
    return jax.shard_map(body, mesh=mesh, in_specs=in_specs, out_specs=out_specs, check_vma=False)
```

```python
import functools
import math

import jax
import jax.numpy as jnp
from jax import lax
from jax.experimental import pallas as pl
from jax.experimental.pallas import tpu as pltpu
from jax.sharding import PartitionSpec as P

HEADS = 8
CAP = 640
NORM_EPS = 1e-06
F32 = jnp.float32
BF16 = jnp.bfloat16
PAD = 256
PIECES = 8
BITS = (2, 4, 1)
WIDE = 512
SMALL = 128
MIB = 1 << 20


def offset_of(position):
    total = 0
    for k, bit in enumerate(BITS):
        total = total + ((position >> k) & 1) * bit
    return total


def dot_nn(a, b):
    return lax.dot_general(a, b, (((1,), (0,)), ((), ())), preferred_element_type=F32)


def dot_nt(a, b):
    return lax.dot_general(a, b, (((1,), (1,)), ((), ())), preferred_element_type=F32)


def dot_tn(a, b):
    return lax.dot_general(a, b, (((0,), (0,)), ((), ())), preferred_element_type=F32)


def norm_parts(values):
    center = values - jnp.mean(values, axis=-1, keepdims=True)
    spread = jnp.mean(center * center, axis=-1, keepdims=True)
    rstd = lax.rsqrt(spread + NORM_EPS)
    return center * rstd, rstd


def gelu_parts(v):
    size = jnp.abs(v)
    density = jnp.exp(v * v * (-0.5)) * 0.3989422804014327
    t = 1.0 / (1.0 + 0.2316418882 * size)
    series = t * (
        0.319381530 + t * (-0.356563782 + t * (1.781477937 + t * (-1.821255978 + t * 1.330274429)))
    )
    tail = density * series
    phi = jnp.where(v < 0, tail, 1.0 - tail)
    return v * phi, phi + v * density


def params(megabytes=62):
    return pltpu.CompilerParams(vmem_limit_bytes=megabytes * MIB)


def cost(microseconds, megabytes):
    return pl.CostEstimate(flops=int(microseconds * 1.1e9), bytes_accessed=int(megabytes * MIB), transcendentals=0)


def padded(length):
    return -(-length // 16) * 16


def pack_kernel(place, qkv, proj, router, *refs):
    *vectors, out, table, lines, turned = refs
    depth = out.shape[0]
    row = pl.multiple_of(place[1] * depth, depth)
    width = qkv.shape[1] + proj.shape[1]
    lines[...] = jnp.zeros_like(lines)
    lines[: router.shape[0], :] = router[...].astype(F32)
    at = 4
    for vector in vectors:
        values = vector[...].astype(F32).reshape(1, -1)
        for c in range(values.shape[1] // 128):
            lines[at : at + 1, :] = values[:, c * 128 : (c + 1) * 128]
            at += 1
        if at == 11:
            at = 12
    turned[...] = lines[...].T
    out[:, : qkv.shape[1]] = qkv[pl.ds(row, depth), :]
    out[:, qkv.shape[1] : width] = proj[pl.ds(row, depth), :]
    out[:, width:] = turned[pl.ds(row, depth), :].astype(BF16)
    table[:, : qkv.shape[1]] = qkv[...]
    table[:, qkv.shape[1] : width] = proj[...]
    table[:, width:] = turned[...].astype(BF16)


def pack_call(place, qkv, proj, router, vectors):
    shard = qkv.shape[0]
    vmem = pl.BlockSpec(memory_space=pltpu.VMEM)
    return pl.pallas_call(
        pack_kernel,
        out_shape=tuple(
            jax.ShapeDtypeStruct((rows, qkv.shape[1] + proj.shape[1] + SMALL), BF16) for rows in (shard // PIECES, shard)
        ),
        in_specs=[pl.BlockSpec(memory_space=pltpu.SMEM)] + [vmem] * (3 + len(vectors)),
        out_specs=(vmem, vmem),
        scratch_shapes=[pltpu.VMEM((SMALL, shard), F32), pltpu.VMEM((shard, SMALL), F32)],
        cost_estimate=cost(2, 1),
        name="pack_dense",
    )(place, qkv, proj, router.T, *vectors)


def cut_kernel(place, inner, outer, out):
    out[0] = inner[0].T
    out[1] = outer[0]


def cut_call(place, inner, outer):
    _, model, hidden = inner.shape
    block = hidden // PIECES
    return pl.pallas_call(
        cut_kernel,
        out_shape=jax.ShapeDtypeStruct((2, block, model), BF16),
        grid_spec=pltpu.PrefetchScalarGridSpec(
            num_scalar_prefetch=1,
            grid=(1,),
            in_specs=[
                pl.BlockSpec((1, model, block), lambda i, s: (0, 0, s[1])),
                pl.BlockSpec((1, block, model), lambda i, s: (0, s[1], 0)),
            ],
            out_specs=pl.BlockSpec((2, block, model), lambda i, s: (0, 0, 0)),
        ),
        compiler_params=params(),
        cost_estimate=cost(2, 1),
        name="cut_own",
    )(place, inner, outer)


def forward_kernel(
    place, images, cot, *refs,
):
    dense = refs[:PIECES]
    own, qkv_out, att_out, res_out, lse_out, tok_out, gates_out, full_out, small_out, rows = refs[PIECES:]
    model = images.shape[2]
    length = images.shape[1]
    size = rows.shape[0]
    parts = dense[0].shape[0] + 1
    depth = dense[0].shape[1]

    @pl.when(pl.program_id(0) == 0)
    def _():
        z, r = place[0], place[1]
        for pos in range(PIECES):
            for d in range(1, parts):
                owner = lax.rem(z + parts - d, parts) * PIECES
                row = pl.multiple_of((owner + jnp.bitwise_xor(r, offset_of(pos))) * depth, depth)
                full_out[pl.ds(row, depth), :] = dense[pos][d - 1]
        full_out[pl.ds(pl.multiple_of(z * PIECES * depth, depth), PIECES * depth), :] = own[...]
        small_out[...] = full_out[:, 4 * model :].astype(F32).T
        rows[...] = jnp.zeros_like(rows)

    def vector(row):
        return small_out[row : row + 1, :]

    rows[:length, :] = images[0].astype(F32)
    x = rows[...]
    xhat, _ = norm_parts(x)
    normed = (xhat * vector(4) + vector(5)).astype(BF16)
    projected = dot_nn(normed, full_out[:, : 3 * model])
    bias_parts = []
    for part in range(parts):
        lanes = slice(part * 128, part * 128 + 128)
        bias_parts += [small_out[9:10, lanes], small_out[10:11, lanes]]
    pair = jnp.concatenate(bias_parts, axis=1)
    qkv_out[0, :, :model] = (projected[:, :model] + pair[:, :model]).astype(BF16)
    qkv_out[0, :, model : 2 * model] = projected[:, model : 2 * model].astype(BF16)
    qkv_out[0, :, 2 * model :] = (projected[:, 2 * model :] + pair[:, model:]).astype(BF16)
    qkv_out[0, length:, :] = jnp.zeros((size - length, 3 * model), BF16)

    head = model // HEADS
    first = lax.broadcasted_iota(jnp.int32, (1, 2 * head), 1) < head
    real = lax.broadcasted_iota(jnp.int32, (1, size), 1) < length
    column = lax.broadcasted_iota(jnp.int32, (size, 128), 1)
    scale = 1.0 / math.sqrt(head)
    lse = jnp.zeros((size, 128), F32)
    attended = []
    for two in range(HEADS // 2):
        lanes = lambda start: slice(start + two * 2 * head, start + (two + 1) * 2 * head)
        q2, k2, v2 = (qkv_out[0, :, lanes(s * model)] for s in range(3))
        zero = jnp.zeros_like(q2)
        stack = jnp.concatenate([jnp.where(first, q2, zero), jnp.where(first, zero, q2)], axis=0)
        scores = jnp.where(real, dot_nt(stack, k2) * scale, -1e30)
        peak = jnp.max(scores, axis=-1, keepdims=True)
        e = jnp.exp(scores - peak)
        total = jnp.sum(e, axis=-1, keepdims=True)
        probs = (e * (1.0 / total)).astype(BF16)
        both = dot_nn(probs, v2)
        attended.append(jnp.where(first, both[:size], both[size:]).astype(BF16))
        logs = peak + jnp.log(total)
        lse = jnp.where(column == 2 * two, logs[:size], lse)
        lse = jnp.where(column == 2 * two + 1, logs[size:], lse)
    lse_out[0] = lse
    attended = jnp.concatenate(attended, axis=1)
    att_out[0] = attended
    residual = x + (dot_nn(attended, full_out[:, 3 * model : 4 * model]) + vector(6))
    res_out[0] = residual
    xhat2, _ = norm_parts(residual)
    normed2 = (xhat2 * vector(7) + vector(8)).astype(BF16)
    tail = length // 16 * 16
    tok_out[tail:, :] = jnp.zeros((PAD - tail, 2 * model), BF16)
    tok_out[:size, :model] = normed2
    tok_out[:length, model:] = cot[0]
    logits = dot_nt(small_out[0:8, :].astype(BF16), tok_out[:, :model])
    experts = lax.broadcasted_iota(jnp.int32, logits.shape, 0) < parts
    logits = jnp.where(experts, logits, -jnp.inf)
    e = jnp.exp(logits - jnp.max(logits, axis=0, keepdims=True))
    gates_out[0] = e / jnp.sum(e, axis=0, keepdims=True)


def whole(a):
    return pl.BlockSpec(a.shape, lambda i, *_: (0,) * len(a.shape))


def image(*dims):
    return pl.BlockSpec((1,) + dims, lambda i, *_: (i, 0, 0))


def forward_call(place, images, cot, dense, own):
    count, length, model = images.shape
    size = padded(length)
    outs = (
        jax.ShapeDtypeStruct((count, size, 3 * model), BF16),
        jax.ShapeDtypeStruct((count, size, model), BF16),
        jax.ShapeDtypeStruct((count, size, model), F32),
        jax.ShapeDtypeStruct((count, size, 128), F32),
        jax.ShapeDtypeStruct((count * PAD, 2 * model), BF16),
        jax.ShapeDtypeStruct((count, 8, PAD), F32),
        jax.ShapeDtypeStruct((model, 4 * model + SMALL), BF16),
        jax.ShapeDtypeStruct((SMALL, model), F32),
    )
    return pl.pallas_call(
        forward_kernel,
        out_shape=outs,
        grid_spec=pltpu.PrefetchScalarGridSpec(
            num_scalar_prefetch=1,
            grid=(count,),
            in_specs=[image(length, model), image(length, model)] + [whole(d) for d in (*dense, own)],
            out_specs=[
                image(size, 3 * model), image(size, model), image(size, model), image(size, 128),
                pl.BlockSpec((PAD, 2 * model), lambda i, *_: (i, 0)),
                image(8, PAD), whole(outs[6]), whole(outs[7]),
            ],
            scratch_shapes=[pltpu.VMEM((size, model), F32)],
        ),
        compiler_params=params(),
        cost_estimate=cost(12, 12),
        name="attention_forward",
    )(place, images, cot, *dense, own)


def blend_loads(jobs, arrays, loaded, sems):
    copies = []
    for _, terms in jobs:
        for which, index in terms:
            spot = len(copies)
            source = arrays[which].at[index] if index else arrays[which]
            copies.append(pltpu.make_async_copy(source, loaded.at[spot], sems.at[spot]))
    return copies


def blend_stores(jobs, outs, loaded, summed, sems):
    copies, spot, sums = [], 0, 0
    for out, (kind, terms) in zip(outs, jobs):
        if kind == "collect":
            pairs = [(loaded.at[spot + k], out.at[k]) for k in range(len(terms))]
        else:
            pairs = [(summed.at[sums], out)]
            sums += 1
        spot += len(terms)
        copies.append([pltpu.make_async_copy(a, b, sems.at[sum(map(len, copies)) + k]) for k, (a, b) in enumerate(pairs)])
    return copies


def blend_work(jobs, loads, stores, loaded, summed):
    spot = sums = 0
    for (kind, terms), copies in zip(jobs, stores):
        total = None
        for k in range(len(terms)):
            loads[spot].wait()
            if kind == "collect":
                copies[k].start()
            else:
                value = loaded[spot].astype(F32)
                total = value if total is None else total + value
            spot += 1
        if kind == "sum":
            summed[sums] = total.astype(BF16)
            copies[0].start()
            sums += 1


def blend_kernel(*refs, jobs, count_in):
    arrays = refs[:count_in]
    outs = refs[count_in : count_in + len(jobs)]
    loaded, summed, in_sems, out_sems = refs[count_in + len(jobs) :]
    loads = blend_loads(jobs, arrays, loaded, in_sems)
    for copy in loads:
        copy.start()
    stores = blend_stores(jobs, outs, loaded, summed, out_sems)
    blend_work(jobs, loads, stores, loaded, summed)
    for copies in stores:
        for copy in copies:
            copy.wait()


def blend_plan(jobs):
    arrays, plan, shapes = [], [], []
    for kind, terms in jobs:
        listed = []
        for array, index in terms:
            known = [k for k, a in enumerate(arrays) if a is array]
            if not known:
                arrays.append(array)
                known = [len(arrays) - 1]
            listed.append((known[0], index))
        unit = terms[0][0].shape[len(terms[0][1]) :]
        shapes.append(jax.ShapeDtypeStruct(((len(terms),) if kind == "collect" else ()) + unit, BF16))
        plan.append((kind, tuple(listed)))
    units = sum(len(terms) for _, terms in plan)
    sums = sum(kind == "sum" for kind, _ in plan)
    stores = sums + sum(len(terms) for kind, terms in plan if kind == "collect")
    scratch = [
        pltpu.VMEM((units,) + unit, BF16),
        pltpu.VMEM((max(sums, 1),) + unit, BF16),
        pltpu.SemaphoreType.DMA((units,)),
        pltpu.SemaphoreType.DMA((stores,)),
    ]
    return arrays, tuple(plan), shapes, scratch


def blend_call(*jobs):
    arrays, plan, shapes, scratch = blend_plan(jobs)
    anywhere = pl.BlockSpec(memory_space=pl.ANY)
    return pl.pallas_call(
        functools.partial(blend_kernel, jobs=plan, count_in=len(arrays)),
        out_shape=tuple(shapes),
        in_specs=[anywhere] * len(arrays),
        out_specs=(anywhere,) * len(shapes),
        scratch_shapes=scratch,
        compiler_params=params(),
        cost_estimate=cost(3, 3),
        name="blend",
    )(*arrays)


def expert_kernel(place, slots, gates, small, tok, *refs, turn, sources, count_in):
    arrays = refs[:count_in]
    keep, send, pair_out, bias_out = refs[count_in : count_in + 4]
    tokens, onehot, buffer, grad_slots, rows, back, mine, inners, outers, staged, token_sem, in_sems, out_sems = (
        refs[count_in + 4 :]
    )
    local = sources is None
    count = slots.shape[0]
    model = buffer.shape[1]
    block = outers.shape[1]
    per = staged.shape[1]
    steps = staged.shape[0]

    token_copy = pltpu.make_async_copy(tok, tokens, token_sem)
    token_copy.start()
    loads = []
    for pos in range(PIECES):
        for side, matrices in enumerate((inners, outers)):
            if local:
                start = pl.multiple_of(jnp.bitwise_xor(place[1], offset_of(pos)) * block, block)
                source = arrays[1].at[0, pl.ds(start, block)] if side else arrays[0].at[0, :, pl.ds(start, block)]
            else:
                which, at = sources(pos, side)
                source = arrays[which].at[at]
            loads.append(pltpu.make_async_copy(source, matrices.at[pos], in_sems.at[pos, side]))

    expert = lax.rem(place[0] + place[3] - turn, place[3])
    lanes = pl.ds(pl.multiple_of(expert * 128, 128), 128)
    mine[...] = small[:, lanes]
    where = lax.broadcasted_iota(jnp.int32, (CAP, PAD), 0)
    gate = jnp.zeros((CAP, 128), F32)
    for b in range(count):
        mask = where == slots[b, turn : turn + 1, :]
        onehot[:, b * PAD : (b + 1) * PAD] = mask.astype(F32).astype(BF16)
        weighted = jnp.where(mask, gates[b, pl.ds(expert, 1), :], 0.0)
        gate = gate + weighted[:, :128] + weighted[:, 128:]
    gate = jnp.sum(gate, axis=1, keepdims=True)
    outer_bias = jnp.concatenate([mine[28 + c : 29 + c, :] for c in range(model // 128)], axis=1)
    token_copy.wait()
    for copy in loads:
        copy.start()
    buffer[...] = dot_nn(onehot[...], tokens[:, :model]).astype(BF16)
    grads = (dot_nn(onehot[...], tokens[:, model:]) * gate).astype(BF16)
    grad_slots[...] = grads
    sums = jnp.sum(grads.astype(F32), axis=0, keepdims=True)
    for c in range(model // 128):
        bias_out[16 + c : 17 + c, :] = sums[:, c * 128 : (c + 1) * 128]
    bias_out[20:32, :] = jnp.zeros((12, 128), F32)

    def first_products(i):
        for copy in loads[2 * i * per : 2 * (i + 1) * per]:
            copy.wait()
        buf, gs = buffer[...], grad_slots[...]
        here = slice(i * per, (i + 1) * per)
        lines = [
            jnp.bitwise_xor(place[1], offset_of(pos)) * (block // 128) + c
            for pos in range(here.start, here.stop)
            for c in range(block // 128)
        ]
        bias = jnp.concatenate([mine[pl.ds(12 + line, 1), :] for line in lines], axis=1)
        if local:
            hidden = jnp.concatenate([dot_nn(buf, inners[pos]) for pos in range(here.start, here.stop)], axis=1)
        else:
            hidden = dot_nt(buf, inners[here].reshape(per * block, model))
        return hidden + bias, dot_nt(gs, outers[here].reshape(per * block, model)), lines

    stores = []
    for i in range(steps):
        hidden, grad_active, lines = first_products(i)
        here = slice(i * per, (i + 1) * per)
        active, slope = gelu_parts(hidden)
        active = active.astype(BF16)
        grad_low = (grad_active * slope).astype(BF16)
        sums = jnp.sum(grad_low.astype(F32), axis=0, keepdims=True)
        for k, line in enumerate(lines):
            bias_out[pl.ds(line, 1), :] = sums[:, k * 128 : (k + 1) * 128]
        staged[i, :, 0] = dot_tn(grad_low, buffer[...]).astype(BF16).reshape(per, block, model)
        staged[i, :, 1] = dot_tn(active, grad_slots[...]).astype(BF16).reshape(per, block, model)
        out = keep if i < steps // 2 else send
        stores.append(pltpu.make_async_copy(staged.at[i], out.at[:, i % (steps // 2)], out_sems.at[i]))
        stores[-1].start()
        new_rows = dot_nn(active, outers[here].reshape(per * block, model))
        if local:
            new_back = sum(
                dot_nt(grad_low[:, j * block : (j + 1) * block], inners[i * per + j]) for j in range(per)
            )
        else:
            new_back = dot_nn(grad_low, inners[here].reshape(per * block, model))
        rows[...] = new_rows + (outer_bias if i == 0 else rows[...])
        back[...] = new_back if i == 0 else new_back + back[...]
    pair_out[:, :model] = rows[...].astype(BF16)
    pair_out[:, model:] = back[...].astype(BF16)
    for copy in stores:
        copy.wait()


def expert_call(turn, place, tok, slots, gates, small, weights):
    arrays, sources = weights
    model = tok.shape[1] // 2
    count = slots.shape[0]
    block = arrays[1].shape[1] // PIECES if sources is None else arrays[0].shape[-2]
    per = WIDE // block
    steps = PIECES // per
    vmem = pl.BlockSpec(memory_space=pltpu.VMEM)
    anywhere = pl.BlockSpec(memory_space=pl.ANY)
    half = jax.ShapeDtypeStruct((2, 2, 2, block, model), BF16)
    return pl.pallas_call(
        functools.partial(expert_kernel, turn=turn, sources=sources, count_in=len(arrays)),
        out_shape=(
            half,
            half,
            jax.ShapeDtypeStruct((CAP, 2 * model), BF16),
            jax.ShapeDtypeStruct((32, 128), F32),
        ),
        in_specs=[pl.BlockSpec(memory_space=pltpu.SMEM), vmem, vmem, vmem, anywhere] + [anywhere] * len(arrays),
        out_specs=[anywhere, anywhere, vmem, vmem],
        scratch_shapes=[
            pltpu.VMEM(tok.shape, BF16),
            pltpu.VMEM((CAP, count * PAD), BF16),
            pltpu.VMEM((CAP, model), BF16),
            pltpu.VMEM((CAP, model), BF16),
            pltpu.VMEM((CAP, model), F32),
            pltpu.VMEM((CAP, model), F32),
            pltpu.VMEM((SMALL, 128), F32),
            pltpu.VMEM((PIECES, model, block) if sources is None else (PIECES, block, model), BF16),
            pltpu.VMEM((PIECES, block, model), BF16),
            pltpu.VMEM((steps, per, 2, block, model), BF16),
            pltpu.SemaphoreType.DMA(()),
            pltpu.SemaphoreType.DMA((PIECES, 2)),
            pltpu.SemaphoreType.DMA((steps,)),
        ],
        compiler_params=params(),
        cost_estimate=cost(18, 14),
        name="expert",
    )(place, slots, gates, small, tok, *arrays)


def norm_back(inner, xhat, rstd):
    return rstd * (
        inner - jnp.mean(inner, axis=-1, keepdims=True) - xhat * jnp.mean(inner * xhat, axis=-1, keepdims=True)
    )


def combine_kernel(place, *refs, turns, jobs, count_in):
    cot, att, res, tok, slots, full, small = refs[:7]
    pairs = refs[7 : 7 + turns]
    biases = refs[7 + turns : 7 + 2 * turns]
    arrays = refs[7 + 2 * turns : 7 + 2 * turns + count_in]
    block_out, gres_out, gatt_out, late_out, *side_outs = refs[7 + 2 * turns + count_in : -8]
    cots, acc_proj, acc_router, acc_small, loaded, summed, in_sems, out_sems = refs[-8:]
    b = pl.program_id(0)
    loads = blend_loads(jobs, arrays, loaded, in_sems)
    stores = blend_stores(jobs, side_outs, loaded, summed, out_sems)

    @pl.when(b == 0)
    def _():
        for copy in loads:
            copy.start()

    @pl.when(b == 1)
    def _():
        blend_work(jobs, loads, stores, loaded, summed)

    length, model = cot.shape[1:]
    size = cots.shape[0]
    parts = turns

    @pl.when(b == 0)
    def _():
        cots[...] = jnp.zeros_like(cots)
        for acc in (acc_proj, acc_router, acc_small):
            acc[...] = jnp.zeros_like(acc)

    def vector(row):
        return small[row : row + 1, :]

    def add_row(row, values):
        acc_small[row : row + 1, :] += jnp.sum(values, axis=0, keepdims=True)

    live = (b < place[2]).astype(F32)
    cots[:length, :] = cot[0].astype(F32) * live
    grad_out = cots[...]
    residual = res[0]
    xhat2, rstd2 = norm_parts(residual)
    normed2 = tok[:size, :model]
    router = full[:, 4 * model :]

    logits = dot_nn(normed2, router)
    lane = lax.broadcasted_iota(jnp.int32, logits.shape, 1)
    logits = jnp.where(lane < parts, logits, -jnp.inf)
    e = jnp.exp(logits - jnp.max(logits, axis=-1, keepdims=True))
    probs = e / jnp.sum(e, axis=-1, keepdims=True)

    seat = lax.broadcasted_iota(jnp.int32, (size, CAP), 1)
    mixture = None
    grad_n2 = None
    grad_probs = jnp.zeros_like(probs)
    for j in range(turns):
        expert = lax.rem(place[0] + parts - j, parts)
        mask = (slots[0][:, j : j + 1] == seat).astype(F32).astype(BF16)
        both = dot_nn(mask, pairs[j][...])
        picked = both[:, :model]
        gate = jnp.sum(jnp.where(lane == expert, probs, 0.0), axis=-1, keepdims=True)
        mixture = gate * picked if mixture is None else mixture + gate * picked
        grad_gate = jnp.sum(grad_out * picked, axis=-1, keepdims=True)
        grad_probs = jnp.where(lane == expert, grad_gate, grad_probs)
        grad_n2 = both[:, model:] if grad_n2 is None else grad_n2 + both[:, model:]
    block_out[0] = ((residual + mixture) * live).astype(BF16)[:length]
    grad_logits = probs * (grad_probs - jnp.sum(probs * grad_probs, axis=-1, keepdims=True))
    grad_logits = grad_logits.astype(BF16)
    grad_n2 = grad_n2 + dot_nt(grad_logits, router)
    acc_router[...] += dot_tn(normed2, grad_logits)

    add_row(7, grad_n2 * xhat2)
    add_row(8, grad_n2)
    grad_res = grad_out + norm_back(grad_n2 * vector(7), xhat2, rstd2)
    gres_out[0] = grad_res
    branch = grad_res.astype(BF16)
    add_row(6, branch.astype(F32))
    acc_proj[...] += dot_tn(att[0], branch)
    gatt_out[0] = dot_nt(branch, full[:, 3 * model : 4 * model]).astype(BF16)

    @pl.when(b == pl.num_programs(0) - 1)
    def _():
        for copies in stores:
            for copy in copies:
                copy.wait()
        for j in range(turns):
            expert = lax.rem(place[0] + parts - j, parts)
            acc_small[12:32, pl.ds(pl.multiple_of(expert * 128, 128), 128)] = biases[j][0:20, :]
        late_out[:, :model] = acc_proj[...].astype(BF16)
        late_out[:, model:] = (acc_router[...] + acc_small[...].T).astype(BF16)


def combine_call(jobs, place, cot, att, res, tok, slots, full, small, pairs, biases):
    count, length, model = cot.shape
    size = att.shape[1]
    turns = len(pairs)
    arrays, plan, shapes, scratch = blend_plan(jobs)
    anywhere = pl.BlockSpec(memory_space=pl.ANY)
    outs = (
        jax.ShapeDtypeStruct((count, length, model), BF16),
        jax.ShapeDtypeStruct((count, size, model), F32),
        jax.ShapeDtypeStruct((count, size, model), BF16),
        jax.ShapeDtypeStruct((model, model + SMALL), BF16),
    )
    return pl.pallas_call(
        functools.partial(combine_kernel, turns=turns, jobs=plan, count_in=len(arrays)),
        out_shape=outs + tuple(shapes),
        grid_spec=pltpu.PrefetchScalarGridSpec(
            num_scalar_prefetch=1,
            grid=(count,),
            in_specs=[
                image(length, model), image(size, model), image(size, model),
                pl.BlockSpec((PAD, 2 * model), lambda i, *_: (i, 0)),
                image(size, slots.shape[2]), whole(full), whole(small),
            ] + [whole(a) for a in (*pairs, *biases)] + [anywhere] * len(arrays),
            out_specs=[image(length, model), image(size, model), image(size, model), whole(outs[3])] + [anywhere] * len(shapes),
            scratch_shapes=[
                pltpu.VMEM((size, model), F32),
                pltpu.VMEM((model, model), F32),
                pltpu.VMEM((model, SMALL), F32),
                pltpu.VMEM((SMALL, model), F32),
            ] + scratch,
        ),
        compiler_params=params(),
        cost_estimate=cost(18, 14),
        name="combine",
    )(place, cot, att, res, tok, slots, full, small, *pairs, *biases, *arrays)


def backward_kernel(
    place, images, qkv, lse, gres, gatt, full, small, late, input_grad, keep, send, rows, acc_qkv, acc_small,
):
    parts = keep.shape[1]
    b = pl.program_id(0)
    length, model = images.shape[1:]
    size = rows.shape[0]

    @pl.when(b == 0)
    def _():
        rows[...] = jnp.zeros_like(rows)
        acc_qkv[...] = jnp.zeros_like(acc_qkv)
        acc_small[...] = jnp.zeros_like(acc_small)

    def vector(row):
        return small[row : row + 1, :]

    def add_row(row, values):
        acc_small[row : row + 1, :] += jnp.sum(values, axis=0, keepdims=True)

    head = model // HEADS
    first = lax.broadcasted_iota(jnp.int32, (1, 2 * head), 1) < head
    real = lax.broadcasted_iota(jnp.int32, (1, size), 1) < length
    scale = 1.0 / math.sqrt(head)
    grads = [[], [], []]
    for two in range(HEADS // 2):
        lanes = lambda start: slice(start + two * 2 * head, start + (two + 1) * 2 * head)
        q2, k2, v2 = (qkv[0, :, lanes(s * model)] for s in range(3))
        g2 = gatt[0, :, lanes(0)]
        zero = jnp.zeros_like(q2)
        stack = lambda t: jnp.concatenate([jnp.where(first, t, zero), jnp.where(first, zero, t)], axis=0)
        merge = lambda t: jnp.where(first, t[:size], t[size:])
        qs, gs = stack(q2), stack(g2)
        logs = jnp.concatenate([lse[0, :, 2 * two : 2 * two + 1], lse[0, :, 2 * two + 1 : 2 * two + 2]], axis=0)
        weights = jnp.where(real, jnp.exp(dot_nt(qs, k2) * scale - logs), 0.0)
        grad_weights = dot_nt(gs, v2)
        grad_scores = weights * (grad_weights - jnp.sum(grad_weights * weights, axis=-1, keepdims=True))
        grad_scores = grad_scores.astype(BF16)
        grads[0].append((merge(dot_nn(grad_scores, k2)) * scale).astype(BF16))
        grads[1].append((dot_tn(grad_scores, qs) * scale).astype(BF16))
        grads[2].append(dot_tn(weights.astype(BF16), gs).astype(BF16))
    grad_projected = jnp.concatenate(grads[0] + grads[1] + grads[2], axis=1)
    rows[:length, :] = images[0].astype(F32)
    xhat1, rstd1 = norm_parts(rows[...])
    normed = (xhat1 * vector(4) + vector(5)).astype(BF16)
    acc_qkv[:, : 3 * model] += dot_tn(normed, grad_projected)
    grad_normed = dot_nt(grad_projected, full[:, : 3 * model])
    add_row(4, grad_normed * xhat1)
    add_row(5, grad_normed)
    add_row(32, grad_projected[:, :model].astype(F32))
    add_row(33, grad_projected[:, 2 * model :].astype(F32))
    input_grad[0] = (gres[0] + norm_back(grad_normed * vector(4), xhat1, rstd1))[:length]

    @pl.when(b == pl.num_programs(0) - 1)
    def _():
        for part in range(parts):
            for k in range(2):
                start = (part * 2 + k) * 128
                source = 32 + start // model
                acc_small[9 + k : 10 + k, part * 128 : part * 128 + 128] = acc_small[
                    source : source + 1, start % model : start % model + 128
                ]
        acc_small[32:34, :] = jnp.zeros((2, model), F32)
        acc_qkv[:, 3 * model :] = acc_small[...].T + late[:, model:].astype(F32)
        depth = keep.shape[2]
        for pos in range(PIECES):
            for d in range(parts):
                owner = lax.rem(place[0] + parts - d, parts) * PIECES
                row = pl.multiple_of((owner + jnp.bitwise_xor(place[1], offset_of(pos))) * depth, depth)
                out = keep if pos < PIECES // 2 else send
                spot = pos % (PIECES // 2)
                out[spot, d, :, : 3 * model] = acc_qkv[pl.ds(row, depth), : 3 * model].astype(BF16)
                out[spot, d, :, 3 * model : 4 * model] = late[pl.ds(row, depth), :model]
                out[spot, d, :, 4 * model :] = acc_qkv[pl.ds(row, depth), 3 * model :].astype(BF16)


def backward_call(place, images, qkv, lse, gres, gatt, full, small, late, parts):
    count, length, model = images.shape
    size = qkv.shape[1]
    half = jax.ShapeDtypeStruct((PIECES // 2, parts, model // (parts * PIECES), 4 * model + SMALL), BF16)
    outs = (jax.ShapeDtypeStruct((count, length, model), F32), half, half)
    return pl.pallas_call(
        backward_kernel,
        out_shape=outs,
        grid_spec=pltpu.PrefetchScalarGridSpec(
            num_scalar_prefetch=1,
            grid=(count,),
            in_specs=[
                image(length, model), image(size, 3 * model), image(size, 128), image(size, model),
                image(size, model), whole(full), whole(small), whole(late),
            ],
            out_specs=[image(length, model), whole(half), whole(half)],
            scratch_shapes=[
                pltpu.VMEM((size, model), F32),
                pltpu.VMEM((model, 3 * model + SMALL), F32),
                pltpu.VMEM((SMALL, model), F32),
            ],
        ),
        compiler_params=params(),
        cost_estimate=cost(22, 14),
        name="attention_backward",
    )(place, images, qkv, lse, gres, gatt, full, small, late)


def finish_kernel(place, *refs, half):
    pieces = refs[: PIECES // 2]
    inner_out, outer_out, loaded, inner, outer, in_sems, out_sems = refs[-7:]
    block = outer.shape[1]
    loads = [pltpu.make_async_copy(p, loaded.at[k], in_sems.at[k]) for k, p in enumerate(pieces)]
    for copy in loads:
        copy.start()
    stores = []
    for k, copy in enumerate(loads):
        copy.wait()
        piece = jnp.bitwise_xor(place[1], offset_of(k + half * PIECES // 2))
        spot = pl.ds(pl.multiple_of(piece * block, block), block)
        inner[k] = loaded[k, 0].astype(F32).T
        outer[k] = loaded[k, 1].astype(F32)
        for side, (source, target) in enumerate(((inner.at[k], inner_out.at[0, :, spot]), (outer.at[k], outer_out.at[0, spot]))):
            stores.append(pltpu.make_async_copy(source, target, out_sems.at[k, side]))
            stores[-1].start()
    for copy in stores:
        copy.wait()


def finish_call(half, place, pieces, outs=()):
    _, block, model = pieces[0].shape
    count = len(pieces)
    anywhere = pl.BlockSpec(memory_space=pl.ANY)
    return pl.pallas_call(
        functools.partial(finish_kernel, half=half),
        out_shape=(
            jax.ShapeDtypeStruct((1, model, PIECES * block), F32),
            jax.ShapeDtypeStruct((1, PIECES * block, model), F32),
        ),
        in_specs=[pl.BlockSpec(memory_space=pltpu.SMEM)] + [anywhere] * (count + len(outs)),
        out_specs=(anywhere, anywhere),
        scratch_shapes=[
            pltpu.VMEM((count, 2, block, model), BF16),
            pltpu.VMEM((count, model, block), F32),
            pltpu.VMEM((count, block, model), F32),
            pltpu.SemaphoreType.DMA((count,)),
            pltpu.SemaphoreType.DMA((count, 2)),
        ],
        input_output_aliases={1 + count + k: k for k in range(len(outs))},
        compiler_params=params(),
        cost_estimate=cost(4, 6),
        name="finish_experts",
    )(place, *pieces, *outs)


def finish_dense_kernel(place, *refs):
    pieces = refs[:2]
    qkv_out, proj_out, router_out, inner_out, outer_out, *vector_outs, pair_out, table = refs[2:]
    model = proj_out.shape[1]
    depth = pieces[0].shape[1]
    for pos in range(PIECES):
        row = pl.multiple_of(jnp.bitwise_xor(place[1], offset_of(pos)) * depth, depth)
        block = pieces[pos // (PIECES // 2)][pos % (PIECES // 2)].astype(F32)
        qkv_out[pl.ds(row, depth), :] = block[:, : 3 * model]
        proj_out[pl.ds(row, depth), :] = block[:, 3 * model : 4 * model]
        table[pl.ds(row, depth), :] = block[:, 4 * model :]
    table[...] = table[...].T
    router_out[...] = table[: router_out.shape[0], :]
    for k, out in enumerate(vector_outs):
        out[...] = table[4 + k, :]
    for k in range(2):
        pair_out[pl.ds(k * 128, 128)] = table[9 + k, :]
    for c in range(inner_out.shape[1] // 128):
        inner_out[:, c * 128 : (c + 1) * 128] = table[12 + c : 13 + c, :]
    for c in range(outer_out.shape[1] // 128):
        outer_out[:, c * 128 : (c + 1) * 128] = table[28 + c : 29 + c, :]


def finish_dense_call(place, pieces, model, parts, hidden):
    rows = pieces[0].shape[1] * PIECES
    vmem = pl.BlockSpec(memory_space=pltpu.VMEM)
    return pl.pallas_call(
        finish_dense_kernel,
        out_shape=(
            jax.ShapeDtypeStruct((rows, 3 * model), F32),
            jax.ShapeDtypeStruct((rows, model), F32),
            jax.ShapeDtypeStruct((parts, rows), F32),
            jax.ShapeDtypeStruct((1, hidden), F32),
            jax.ShapeDtypeStruct((1, model), F32),
        )
        + tuple(jax.ShapeDtypeStruct((n,), F32) for n in (rows, rows, rows, rows, rows, 2 * rows)),
        in_specs=[pl.BlockSpec(memory_space=pltpu.SMEM)] + [vmem] * 2,
        scratch_shapes=[pltpu.VMEM((rows, SMALL), F32)],
        cost_estimate=cost(2, 2),
        name="finish_dense",
    )(place, *pieces)


def join(*values):
    return lax.optimization_barrier(values)


def local(
    images, attn_norm_gain, attn_norm_bias, qkv_weight, query_value_bias, proj_weight, proj_bias,
    moe_norm_gain, moe_norm_bias, router_weight, expert_inner, expert_inner_bias, expert_outer,
    expert_outer_bias, live_count, routes, slot_ids, cotangent, *, n_replica, n_group,
):
    count, length, model = images.shape
    shard = qkv_weight.shape[0]
    hidden = expert_inner.shape[2]
    size = padded(length)
    z = lax.axis_index("group").astype(jnp.int32)
    r = lax.axis_index("replica").astype(jnp.int32) & (PIECES - 1)
    place = jnp.stack([z, r, live_count[0].astype(jnp.int32), jnp.int32(n_group)])

    def across(value, bit):
        return lax.ppermute(value, "replica", [(i, i ^ bit) for i in range(n_replica)])

    def along(value, shift):
        return lax.ppermute(value, "group", [(i, (i + shift) % n_group) for i in range(n_group)])

    def plus(*values):
        return sum(v.astype(F32) for v in values).astype(BF16)

    def both(value, bit):
        return jnp.concatenate([value, across(value, bit)], axis=0)

    def spread(value):
        return [value] + [across(value, offset_of(pos)) for pos in range(1, PIECES // 2)]

    def rest_of_replicas(value):
        bit = PIECES
        while bit < n_replica:
            value = plus(value, across(value, bit))
            bit *= 2
        return value

    shifts = list(range(1, n_group))

    vectors = (attn_norm_gain, attn_norm_bias, proj_bias, moe_norm_gain, moe_norm_bias, query_value_bias)
    mine, own_table = pack_call(
        place, qkv_weight, proj_weight, router_weight, vectors + (expert_inner_bias, expert_outer_bias)
    )
    dense_z = {d: along(mine, d) for d in shifts}

    piece = cut_call(place, expert_inner, expert_outer)
    piece, dense_z = join(piece, dense_z)
    expert_z = {1: along(piece, 1)}
    dense = spread(jnp.stack([dense_z[d] for d in shifts]))
    dense = dense + [across(v, 1) for v in dense]

    experts = (z + n_group - jnp.arange(n_group, dtype=jnp.int32)) % n_group
    chosen = routes[:, None] == experts[None, :, None, None]
    seats = jnp.max(jnp.where(chosen, slot_ids[:, None], -1), axis=-1)
    slots_lane = jnp.pad(seats, ((0, 0), (0, 8 - n_group), (0, PAD - length)), constant_values=-1)
    slots_row = jnp.pad(
        seats.transpose(0, 2, 1), ((0, 0), (0, size - length), (0, 8 - n_group)), constant_values=-1
    )

    def collected(pieces):
        return ("collect", [(p, ()) for p in pieces])

    def sources(pos, side):
        return pos // (PIECES // 2), (pos % (PIECES // 2), side)

    outs, cores, chips, shards = {}, {}, {}, {}
    places = ((1, 0), (0, 1), (1, 1))

    def quarters(k):
        return [("sum", [(outs[k][0], at), (cores[k], at)]) for at in places]

    def own_quarter(k):
        return ("sum", [(outs[k][0], (0, 0)), (cores[k], (0, 0))] + [(v, ()) for v in chips[k]])

    def send_chips(values):
        return [across(v, offset_of(pos)) for pos, v in zip(range(1, PIECES // 2), values)]

    def send_shard(k, value):
        value = rest_of_replicas(value)
        return along(value, -k) if k else value

    spread_1 = spread(expert_z[1])
    piece, expert_z[1] = join(piece, expert_z[1])
    expert_z[2] = along(piece, 2)
    qkv, att, res, lse, tok, gates, full, small = forward_call(place, images, cotangent, dense, own_table)
    tok, gates, small, piece, spread_1, expert_z = join(tok, gates, small, piece, spread_1, expert_z)
    tables = (slots_lane, gates, small)

    half, = blend_call(collected(spread_1))
    weights = (half, across(half, 1))
    spread_2 = spread(expert_z[2])
    expert_z[3] = along(piece, 3)
    outs[0] = expert_call(0, place, tok, *tables, ((expert_inner, expert_outer), None))
    outs, tok, weights, spread_2, expert_z = join(outs, tok, weights, spread_2, expert_z)

    cores[0] = across(outs[0][1], 1)
    half, = blend_call(collected(spread_2))
    weights_2 = (half, across(half, 1))
    spread_3 = spread(expert_z[3])
    outs[1] = expert_call(1, place, tok, *tables, (weights, sources))
    outs, tok, cores, weights_2, spread_3 = join(outs, tok, cores, weights_2, spread_3)

    cores[1] = across(outs[1][1], 1)
    half, *parts = blend_call(collected(spread_3), *quarters(0))
    weights_3 = (half, across(half, 1))
    chips[0] = send_chips(parts)
    outs[2] = expert_call(2, place, tok, *tables, (weights_2, sources))
    outs, tok, cores, chips, weights_3 = join(outs, tok, cores, chips, weights_3)

    cores[2] = across(outs[2][1], 1)
    chips[1] = send_chips(blend_call(*quarters(1)))
    outs[3] = expert_call(3, place, tok, *tables, (weights_3, sources))
    outs, cores, chips, shards = join(outs, cores, chips, shards)

    cores[3] = across(outs[3][1], 1)
    chips[2] = send_chips(blend_call(*quarters(2)))
    pairs = [outs[k][2] for k in range(n_group)]
    biases = [outs[k][3] for k in range(n_group)]
    block_out, gres, gatt, late, shards[0], shards[1] = combine_call(
        (own_quarter(0), own_quarter(1)), place, cotangent, att, res, tok, slots_row, full, small, pairs, biases
    )
    gres, gatt, late, cores, chips, shards = join(gres, gatt, late, cores, chips, shards)

    *parts, shards[2] = blend_call(*quarters(3), own_quarter(2))
    chips[3] = send_chips(parts)
    passed = along(rest_of_replicas(shards.pop(2)), 1)
    for k in range(2):
        shards[k] = send_shard(k, shards[k])
    input_grad, keep, send = backward_call(place, images, qkv, lse, gres, gatt, full, small, late, n_group)
    keep, send, chips, shards, passed = join(keep, send, chips, shards, passed)
    if n_replica == PIECES:
        value, = blend_call(("sum", own_quarter(3)[1] + [(passed, ())]))
    else:
        value = plus(rest_of_replicas(*blend_call(own_quarter(3))), passed)
    shards[3] = along(value, 1)

    value = plus(keep, across(send, 1))
    value = plus(value[0], *(across(value[pos], offset_of(pos)) for pos in range(1, PIECES // 2)))
    value = rest_of_replicas(value)
    total, = blend_call(("sum", [(v, ()) for v in shards.values()]))
    value, total = join(value, total)
    own_half = spread(total)
    value = plus(*([value[0]] + [along(value[d], -d) for d in range(1, n_group)]))
    value, own_half = join(value, own_half)
    value = spread(value)
    other_half = [across(v, 1) for v in own_half]
    grads = finish_call(0, place, own_half)
    grad_inner, grad_outer = finish_call(1, place, other_half, grads)
    value, grad_inner, grad_outer = join(value, grad_inner, grad_outer)
    value = jnp.stack(value)
    value = (value, across(value, 1))
    grad_qkv, grad_proj, grad_router, grad_inner_bias, grad_outer_bias, *rest = finish_dense_call(
        place, value, model, n_group, hidden
    )
    return (
        block_out, input_grad, rest[0], rest[1], grad_qkv, rest[5], grad_proj, rest[2], rest[3], rest[4],
        grad_router.T, grad_inner, grad_inner_bias, grad_outer, grad_outer_bias,
    )


def solution(mesh):
    both = ("replica", "group")
    in_specs = (
        P(both, None, None), P("group"), P("group"), P("group", None), P("group"), P("group", None),
        P("group"), P("group"), P("group"), P("group", None), P("group", None, None), P("group", None),
        P("group", None, None), P("group", None), P(both), P(both, None, None), P(both, None, None),
        P(both, None, None),
    )
    out_specs = (
        P(both, None, None), P(both, None, None), P("group"), P("group"), P("group", None), P("group"),
        P("group", None), P("group"), P("group"), P("group"), P("group", None), P("group", None, None),
        P("group", None), P("group", None, None), P("group", None),
    )
    body = functools.partial(local, n_replica=mesh.shape["replica"], n_group=mesh.shape["group"])
    return jax.shard_map(body, mesh=mesh, in_specs=in_specs, out_specs=out_specs, check_vma=False)
```

```python
import functools
import math

import jax
import jax.numpy as jnp
from jax import lax
from jax.experimental import pallas as pl
from jax.experimental.pallas import tpu as pltpu
from jax.sharding import PartitionSpec as P

HEADS = 8
CAP = 640
NORM_EPS = 1e-06
F32 = jnp.float32
BF16 = jnp.bfloat16
PAD = 256
PIECES = 8
BITS = (2, 4, 1)
WIDE = 512
SMALL = 128
MIB = 1 << 20


def offset_of(position):
    total = 0
    for k, bit in enumerate(BITS):
        total = total + ((position >> k) & 1) * bit
    return total


def dot_nn(a, b):
    return lax.dot_general(a, b, (((1,), (0,)), ((), ())), preferred_element_type=F32)


def dot_nt(a, b):
    return lax.dot_general(a, b, (((1,), (1,)), ((), ())), preferred_element_type=F32)


def dot_tn(a, b):
    return lax.dot_general(a, b, (((0,), (0,)), ((), ())), preferred_element_type=F32)


def norm_parts(values):
    center = values - jnp.mean(values, axis=-1, keepdims=True)
    spread = jnp.mean(center * center, axis=-1, keepdims=True)
    rstd = lax.rsqrt(spread + NORM_EPS)
    return center * rstd, rstd


def gelu_parts(v):
    size = jnp.abs(v)
    density = jnp.exp(v * v * (-0.5)) * 0.3989422804014327
    t = 1.0 / (1.0 + 0.2316418882 * size)
    series = t * (
        0.319381530 + t * (-0.356563782 + t * (1.781477937 + t * (-1.821255978 + t * 1.330274429)))
    )
    tail = density * series
    phi = jnp.where(v < 0, tail, 1.0 - tail)
    return v * phi, phi + v * density


def params(megabytes=62):
    return pltpu.CompilerParams(vmem_limit_bytes=megabytes * MIB)


def cost(microseconds, megabytes):
    return pl.CostEstimate(flops=int(microseconds * 1.1e9), bytes_accessed=int(megabytes * MIB), transcendentals=0)


def padded(length):
    return -(-length // 16) * 16


def pack_kernel(place, qkv, proj, router, *refs):
    *vectors, out, table, lines, turned = refs
    depth = out.shape[0]
    row = pl.multiple_of(place[1] * depth, depth)
    width = qkv.shape[1] + proj.shape[1]
    lines[...] = jnp.zeros_like(lines)
    lines[: router.shape[0], :] = router[...].astype(F32)
    at = 4
    for vector in vectors:
        values = vector[...].astype(F32).reshape(1, -1)
        for c in range(values.shape[1] // 128):
            lines[at : at + 1, :] = values[:, c * 128 : (c + 1) * 128]
            at += 1
        if at == 11:
            at = 12
    turned[...] = lines[...].T
    out[:, : qkv.shape[1]] = qkv[pl.ds(row, depth), :]
    out[:, qkv.shape[1] : width] = proj[pl.ds(row, depth), :]
    out[:, width:] = turned[pl.ds(row, depth), :].astype(BF16)
    table[:, : qkv.shape[1]] = qkv[...]
    table[:, qkv.shape[1] : width] = proj[...]
    table[:, width:] = turned[...].astype(BF16)


def pack_call(place, qkv, proj, router, vectors):
    shard = qkv.shape[0]
    vmem = pl.BlockSpec(memory_space=pltpu.VMEM)
    return pl.pallas_call(
        pack_kernel,
        out_shape=tuple(
            jax.ShapeDtypeStruct((rows, qkv.shape[1] + proj.shape[1] + SMALL), BF16) for rows in (shard // PIECES, shard)
        ),
        in_specs=[pl.BlockSpec(memory_space=pltpu.SMEM)] + [vmem] * (3 + len(vectors)),
        out_specs=(vmem, vmem),
        scratch_shapes=[pltpu.VMEM((SMALL, shard), F32), pltpu.VMEM((shard, SMALL), F32)],
        cost_estimate=cost(2, 1),
        name="pack_dense",
    )(place, qkv, proj, router.T, *vectors)


def cut_kernel(place, inner, outer, out):
    out[0] = inner[0].T
    out[1] = outer[0]


def cut_call(place, inner, outer):
    _, model, hidden = inner.shape
    block = hidden // PIECES
    return pl.pallas_call(
        cut_kernel,
        out_shape=jax.ShapeDtypeStruct((2, block, model), BF16),
        grid_spec=pltpu.PrefetchScalarGridSpec(
            num_scalar_prefetch=1,
            grid=(1,),
            in_specs=[
                pl.BlockSpec((1, model, block), lambda i, s: (0, 0, s[1])),
                pl.BlockSpec((1, block, model), lambda i, s: (0, s[1], 0)),
            ],
            out_specs=pl.BlockSpec((2, block, model), lambda i, s: (0, 0, 0)),
        ),
        compiler_params=params(),
        cost_estimate=cost(2, 1),
        name="cut_own",
    )(place, inner, outer)


def forward_kernel(
    place, images, cot, *refs,
):
    dense = refs[:PIECES]
    own, qkv_out, att_out, res_out, lse_out, tok_out, gates_out, full_out, small_out, rows = refs[PIECES:]
    model = images.shape[2]
    length = images.shape[1]
    size = rows.shape[0]
    parts = dense[0].shape[0] + 1
    depth = dense[0].shape[1]

    @pl.when(pl.program_id(0) == 0)
    def _():
        z, r = place[0], place[1]
        for pos in range(PIECES):
            for d in range(1, parts):
                owner = lax.rem(z + parts - d, parts) * PIECES
                row = pl.multiple_of((owner + jnp.bitwise_xor(r, offset_of(pos))) * depth, depth)
                full_out[pl.ds(row, depth), :] = dense[pos][d - 1]
        full_out[pl.ds(pl.multiple_of(z * PIECES * depth, depth), PIECES * depth), :] = own[...]
        small_out[...] = full_out[:, 4 * model :].astype(F32).T
        rows[...] = jnp.zeros_like(rows)

    def vector(row):
        return small_out[row : row + 1, :]

    rows[:length, :] = images[0].astype(F32)
    x = rows[...]
    xhat, _ = norm_parts(x)
    normed = (xhat * vector(4) + vector(5)).astype(BF16)
    projected = dot_nn(normed, full_out[:, : 3 * model])
    bias_parts = []
    for part in range(parts):
        lanes = slice(part * 128, part * 128 + 128)
        bias_parts += [small_out[9:10, lanes], small_out[10:11, lanes]]
    pair = jnp.concatenate(bias_parts, axis=1)
    qkv_out[0, :, :model] = (projected[:, :model] + pair[:, :model]).astype(BF16)
    qkv_out[0, :, model : 2 * model] = projected[:, model : 2 * model].astype(BF16)
    qkv_out[0, :, 2 * model :] = (projected[:, 2 * model :] + pair[:, model:]).astype(BF16)
    qkv_out[0, length:, :] = jnp.zeros((size - length, 3 * model), BF16)

    head = model // HEADS
    first = lax.broadcasted_iota(jnp.int32, (1, 2 * head), 1) < head
    real = lax.broadcasted_iota(jnp.int32, (1, size), 1) < length
    column = lax.broadcasted_iota(jnp.int32, (size, 128), 1)
    scale = 1.0 / math.sqrt(head)
    lse = jnp.zeros((size, 128), F32)
    attended = []
    for two in range(HEADS // 2):
        lanes = lambda start: slice(start + two * 2 * head, start + (two + 1) * 2 * head)
        q2, k2, v2 = (qkv_out[0, :, lanes(s * model)] for s in range(3))
        zero = jnp.zeros_like(q2)
        stack = jnp.concatenate([jnp.where(first, q2, zero), jnp.where(first, zero, q2)], axis=0)
        scores = jnp.where(real, dot_nt(stack, k2) * scale, -1e30)
        peak = jnp.max(scores, axis=-1, keepdims=True)
        e = jnp.exp(scores - peak)
        total = jnp.sum(e, axis=-1, keepdims=True)
        probs = (e * (1.0 / total)).astype(BF16)
        both = dot_nn(probs, v2)
        attended.append(jnp.where(first, both[:size], both[size:]).astype(BF16))
        logs = peak + jnp.log(total)
        lse = jnp.where(column == 2 * two, logs[:size], lse)
        lse = jnp.where(column == 2 * two + 1, logs[size:], lse)
    lse_out[0] = lse
    attended = jnp.concatenate(attended, axis=1)
    att_out[0] = attended
    residual = x + (dot_nn(attended, full_out[:, 3 * model : 4 * model]) + vector(6))
    res_out[0] = residual
    xhat2, _ = norm_parts(residual)
    normed2 = (xhat2 * vector(7) + vector(8)).astype(BF16)
    tail = length // 16 * 16
    tok_out[tail:, :] = jnp.zeros((PAD - tail, 2 * model), BF16)
    tok_out[:size, :model] = normed2
    tok_out[:length, model:] = cot[0]
    logits = dot_nt(small_out[0:8, :].astype(BF16), tok_out[:, :model])
    experts = lax.broadcasted_iota(jnp.int32, logits.shape, 0) < parts
    logits = jnp.where(experts, logits, -jnp.inf)
    e = jnp.exp(logits - jnp.max(logits, axis=0, keepdims=True))
    gates_out[0] = e / jnp.sum(e, axis=0, keepdims=True)


def whole(a):
    return pl.BlockSpec(a.shape, lambda i, *_: (0,) * len(a.shape))


def image(*dims):
    return pl.BlockSpec((1,) + dims, lambda i, *_: (i, 0, 0))


def forward_call(place, images, cot, dense, own):
    count, length, model = images.shape
    size = padded(length)
    outs = (
        jax.ShapeDtypeStruct((count, size, 3 * model), BF16),
        jax.ShapeDtypeStruct((count, size, model), BF16),
        jax.ShapeDtypeStruct((count, size, model), F32),
        jax.ShapeDtypeStruct((count, size, 128), F32),
        jax.ShapeDtypeStruct((count * PAD, 2 * model), BF16),
        jax.ShapeDtypeStruct((count, 8, PAD), F32),
        jax.ShapeDtypeStruct((model, 4 * model + SMALL), BF16),
        jax.ShapeDtypeStruct((SMALL, model), F32),
    )
    return pl.pallas_call(
        forward_kernel,
        out_shape=outs,
        grid_spec=pltpu.PrefetchScalarGridSpec(
            num_scalar_prefetch=1,
            grid=(count,),
            in_specs=[image(length, model), image(length, model)] + [whole(d) for d in (*dense, own)],
            out_specs=[
                image(size, 3 * model), image(size, model), image(size, model), image(size, 128),
                pl.BlockSpec((PAD, 2 * model), lambda i, *_: (i, 0)),
                image(8, PAD), whole(outs[6]), whole(outs[7]),
            ],
            scratch_shapes=[pltpu.VMEM((size, model), F32)],
        ),
        compiler_params=params(),
        cost_estimate=cost(12, 12),
        name="attention_forward",
    )(place, images, cot, *dense, own)


def blend_loads(jobs, arrays, loaded, sems):
    copies = []
    for _, terms in jobs:
        for which, index in terms:
            spot = len(copies)
            source = arrays[which].at[index] if index else arrays[which]
            copies.append(pltpu.make_async_copy(source, loaded.at[spot], sems.at[spot]))
    return copies


def blend_stores(jobs, outs, loaded, summed, sems):
    copies, spot, sums = [], 0, 0
    for out, (kind, terms) in zip(outs, jobs):
        if kind == "collect":
            pairs = [(loaded.at[spot + k], out.at[k]) for k in range(len(terms))]
        else:
            pairs = [(summed.at[sums], out)]
            sums += 1
        spot += len(terms)
        copies.append([pltpu.make_async_copy(a, b, sems.at[sum(map(len, copies)) + k]) for k, (a, b) in enumerate(pairs)])
    return copies


def blend_work(jobs, loads, stores, loaded, summed):
    spot = sums = 0
    for (kind, terms), copies in zip(jobs, stores):
        total = None
        for k in range(len(terms)):
            loads[spot].wait()
            if kind == "collect":
                copies[k].start()
            else:
                value = loaded[spot].astype(F32)
                total = value if total is None else total + value
            spot += 1
        if kind == "sum":
            summed[sums] = total.astype(BF16)
            copies[0].start()
            sums += 1


def blend_kernel(*refs, jobs, count_in):
    arrays = refs[:count_in]
    outs = refs[count_in : count_in + len(jobs)]
    loaded, summed, in_sems, out_sems = refs[count_in + len(jobs) :]
    loads = blend_loads(jobs, arrays, loaded, in_sems)
    for copy in loads:
        copy.start()
    stores = blend_stores(jobs, outs, loaded, summed, out_sems)
    blend_work(jobs, loads, stores, loaded, summed)
    for copies in stores:
        for copy in copies:
            copy.wait()


def blend_plan(jobs):
    arrays, plan, shapes = [], [], []
    for kind, terms in jobs:
        listed = []
        for array, index in terms:
            known = [k for k, a in enumerate(arrays) if a is array]
            if not known:
                arrays.append(array)
                known = [len(arrays) - 1]
            listed.append((known[0], index))
        unit = terms[0][0].shape[len(terms[0][1]) :]
        shapes.append(jax.ShapeDtypeStruct(((len(terms),) if kind == "collect" else ()) + unit, BF16))
        plan.append((kind, tuple(listed)))
    units = sum(len(terms) for _, terms in plan)
    sums = sum(kind == "sum" for kind, _ in plan)
    stores = sums + sum(len(terms) for kind, terms in plan if kind == "collect")
    scratch = [
        pltpu.VMEM((units,) + unit, BF16),
        pltpu.VMEM((max(sums, 1),) + unit, BF16),
        pltpu.SemaphoreType.DMA((units,)),
        pltpu.SemaphoreType.DMA((stores,)),
    ]
    return arrays, tuple(plan), shapes, scratch


def blend_call(*jobs):
    arrays, plan, shapes, scratch = blend_plan(jobs)
    anywhere = pl.BlockSpec(memory_space=pl.ANY)
    return pl.pallas_call(
        functools.partial(blend_kernel, jobs=plan, count_in=len(arrays)),
        out_shape=tuple(shapes),
        in_specs=[anywhere] * len(arrays),
        out_specs=(anywhere,) * len(shapes),
        scratch_shapes=scratch,
        compiler_params=params(),
        cost_estimate=cost(3, 3),
        name="blend",
    )(*arrays)


def expert_kernel(place, slots, gates, small, tok, *refs, turn, sources, count_in, count_side):
    arrays = refs[:count_in]
    beside = refs[count_in : count_in + count_side]
    count_in += count_side
    keep, send, pair_out, bias_out = refs[count_in : count_in + 4]
    if count_side:
        collected, passing, side_sems = refs[count_in + 4], refs[-2], refs[-1]
        refs = refs[: count_in + 4] + refs[count_in + 5 : -2]
    tokens, onehot, buffer, grad_slots, rows, back, mine, inners, outers, staged, token_sem, in_sems, out_sems = (
        refs[count_in + 4 :]
    )
    local = sources is None
    count = slots.shape[0]
    model = buffer.shape[1]
    block = outers.shape[1]
    per = staged.shape[1]
    steps = staged.shape[0]

    token_copy = pltpu.make_async_copy(tok, tokens, token_sem)
    token_copy.start()
    loads = []
    for pos in range(PIECES):
        for side, matrices in enumerate((inners, outers)):
            if local:
                start = pl.multiple_of(jnp.bitwise_xor(place[1], offset_of(pos)) * block, block)
                source = arrays[1].at[0, pl.ds(start, block)] if side else arrays[0].at[0, :, pl.ds(start, block)]
            else:
                which, at = sources(pos, side)
                source = arrays[which].at[at]
            loads.append(pltpu.make_async_copy(source, matrices.at[pos], in_sems.at[pos, side]))

    expert = lax.rem(place[0] + place[3] - turn, place[3])
    lanes = pl.ds(pl.multiple_of(expert * 128, 128), 128)
    mine[...] = small[:, lanes]
    where = lax.broadcasted_iota(jnp.int32, (CAP, PAD), 0)
    gate = jnp.zeros((CAP, 128), F32)
    for b in range(count):
        mask = where == slots[b, turn : turn + 1, :]
        onehot[:, b * PAD : (b + 1) * PAD] = mask.astype(F32).astype(BF16)
        weighted = jnp.where(mask, gates[b, pl.ds(expert, 1), :], 0.0)
        gate = gate + weighted[:, :128] + weighted[:, 128:]
    gate = jnp.sum(gate, axis=1, keepdims=True)
    outer_bias = jnp.concatenate([mine[28 + c : 29 + c, :] for c in range(model // 128)], axis=1)
    token_copy.wait()
    for copy in loads:
        copy.start()
    side_loads = [pltpu.make_async_copy(b, passing.at[k], side_sems.at[0, k]) for k, b in enumerate(beside)]
    side_stores = [pltpu.make_async_copy(passing.at[k], collected.at[k], side_sems.at[1, k]) for k in range(count_side)]
    for copy in side_loads:
        copy.start()
    buffer[...] = dot_nn(onehot[...], tokens[:, :model]).astype(BF16)
    grads = (dot_nn(onehot[...], tokens[:, model:]) * gate).astype(BF16)
    grad_slots[...] = grads
    sums = jnp.sum(grads.astype(F32), axis=0, keepdims=True)
    for c in range(model // 128):
        bias_out[16 + c : 17 + c, :] = sums[:, c * 128 : (c + 1) * 128]
    bias_out[20:32, :] = jnp.zeros((12, 128), F32)

    def first_products(i):
        for copy in loads[2 * i * per : 2 * (i + 1) * per]:
            copy.wait()
        buf, gs = buffer[...], grad_slots[...]
        here = slice(i * per, (i + 1) * per)
        lines = [
            jnp.bitwise_xor(place[1], offset_of(pos)) * (block // 128) + c
            for pos in range(here.start, here.stop)
            for c in range(block // 128)
        ]
        bias = jnp.concatenate([mine[pl.ds(12 + line, 1), :] for line in lines], axis=1)
        if local:
            hidden = jnp.concatenate([dot_nn(buf, inners[pos]) for pos in range(here.start, here.stop)], axis=1)
        else:
            hidden = dot_nt(buf, inners[here].reshape(per * block, model))
        return hidden + bias, dot_nt(gs, outers[here].reshape(per * block, model)), lines

    stores = []
    for i in range(steps):
        hidden, grad_active, lines = first_products(i)
        if i == 1:
            for load, store in zip(side_loads, side_stores):
                load.wait()
                store.start()
        here = slice(i * per, (i + 1) * per)
        active, slope = gelu_parts(hidden)
        active = active.astype(BF16)
        grad_low = (grad_active * slope).astype(BF16)
        sums = jnp.sum(grad_low.astype(F32), axis=0, keepdims=True)
        for k, line in enumerate(lines):
            bias_out[pl.ds(line, 1), :] = sums[:, k * 128 : (k + 1) * 128]
        staged[i, :, 0] = dot_tn(grad_low, buffer[...]).astype(BF16).reshape(per, block, model)
        staged[i, :, 1] = dot_tn(active, grad_slots[...]).astype(BF16).reshape(per, block, model)
        out = keep if i < steps // 2 else send
        stores.append(pltpu.make_async_copy(staged.at[i], out.at[:, i % (steps // 2)], out_sems.at[i]))
        stores[-1].start()
        new_rows = dot_nn(active, outers[here].reshape(per * block, model))
        if local:
            new_back = sum(
                dot_nt(grad_low[:, j * block : (j + 1) * block], inners[i * per + j]) for j in range(per)
            )
        else:
            new_back = dot_nn(grad_low, inners[here].reshape(per * block, model))
        rows[...] = new_rows + (outer_bias if i == 0 else rows[...])
        back[...] = new_back if i == 0 else new_back + back[...]
    pair_out[:, :model] = rows[...].astype(BF16)
    pair_out[:, model:] = back[...].astype(BF16)
    for copy in stores + side_stores:
        copy.wait()


def expert_call(turn, place, tok, slots, gates, small, weights, beside=()):
    arrays, sources = weights
    model = tok.shape[1] // 2
    count = slots.shape[0]
    block = arrays[1].shape[1] // PIECES if sources is None else arrays[0].shape[-2]
    per = WIDE // block
    steps = PIECES // per
    vmem = pl.BlockSpec(memory_space=pltpu.VMEM)
    anywhere = pl.BlockSpec(memory_space=pl.ANY)
    half = jax.ShapeDtypeStruct((2, 2, 2, block, model), BF16)
    return pl.pallas_call(
        functools.partial(expert_kernel, turn=turn, sources=sources, count_in=len(arrays), count_side=len(beside)),
        out_shape=(
            half,
            half,
            jax.ShapeDtypeStruct((CAP, 2 * model), BF16),
            jax.ShapeDtypeStruct((32, 128), F32),
        )
        + tuple(jax.ShapeDtypeStruct((len(beside),) + b.shape, BF16) for b in beside[:1]),
        in_specs=[pl.BlockSpec(memory_space=pltpu.SMEM), vmem, vmem, vmem, anywhere]
        + [anywhere] * (len(arrays) + len(beside)),
        out_specs=[anywhere, anywhere, vmem, vmem] + [anywhere] * len(beside[:1]),
        scratch_shapes=[
            pltpu.VMEM(tok.shape, BF16),
            pltpu.VMEM((CAP, count * PAD), BF16),
            pltpu.VMEM((CAP, model), BF16),
            pltpu.VMEM((CAP, model), BF16),
            pltpu.VMEM((CAP, model), F32),
            pltpu.VMEM((CAP, model), F32),
            pltpu.VMEM((SMALL, 128), F32),
            pltpu.VMEM((PIECES, model, block) if sources is None else (PIECES, block, model), BF16),
            pltpu.VMEM((PIECES, block, model), BF16),
            pltpu.VMEM((steps, per, 2, block, model), BF16),
            pltpu.SemaphoreType.DMA(()),
            pltpu.SemaphoreType.DMA((PIECES, 2)),
            pltpu.SemaphoreType.DMA((steps,)),
        ]
        + [pltpu.VMEM((len(beside),) + b.shape, BF16) for b in beside[:1]]
        + [pltpu.SemaphoreType.DMA((2, len(beside))) for _ in beside[:1]],
        compiler_params=params(),
        cost_estimate=cost(18, 14),
        name="expert",
    )(place, slots, gates, small, tok, *arrays, *beside)


def norm_back(inner, xhat, rstd):
    return rstd * (
        inner - jnp.mean(inner, axis=-1, keepdims=True) - xhat * jnp.mean(inner * xhat, axis=-1, keepdims=True)
    )


def combine_kernel(place, *refs, turns, jobs, count_in):
    cot, att, res, tok, slots, full, small = refs[:7]
    pairs = refs[7 : 7 + turns]
    biases = refs[7 + turns : 7 + 2 * turns]
    arrays = refs[7 + 2 * turns : 7 + 2 * turns + count_in]
    block_out, gres_out, gatt_out, late_out, *side_outs = refs[7 + 2 * turns + count_in : -8]
    cots, acc_proj, acc_router, acc_small, loaded, summed, in_sems, out_sems = refs[-8:]
    b = pl.program_id(0)
    loads = blend_loads(jobs, arrays, loaded, in_sems)
    stores = blend_stores(jobs, side_outs, loaded, summed, out_sems)

    @pl.when(b == 0)
    def _():
        for copy in loads:
            copy.start()

    @pl.when(b == 1)
    def _():
        blend_work(jobs, loads, stores, loaded, summed)

    length, model = cot.shape[1:]
    size = cots.shape[0]
    parts = turns

    @pl.when(b == 0)
    def _():
        cots[...] = jnp.zeros_like(cots)
        for acc in (acc_proj, acc_router, acc_small):
            acc[...] = jnp.zeros_like(acc)

    def vector(row):
        return small[row : row + 1, :]

    def add_row(row, values):
        acc_small[row : row + 1, :] += jnp.sum(values, axis=0, keepdims=True)

    live = (b < place[2]).astype(F32)
    cots[:length, :] = cot[0].astype(F32) * live
    grad_out = cots[...]
    residual = res[0]
    xhat2, rstd2 = norm_parts(residual)
    normed2 = tok[:size, :model]
    router = full[:, 4 * model :]

    logits = dot_nn(normed2, router)
    lane = lax.broadcasted_iota(jnp.int32, logits.shape, 1)
    logits = jnp.where(lane < parts, logits, -jnp.inf)
    e = jnp.exp(logits - jnp.max(logits, axis=-1, keepdims=True))
    probs = e / jnp.sum(e, axis=-1, keepdims=True)

    seat = lax.broadcasted_iota(jnp.int32, (size, CAP), 1)
    mixture = None
    grad_n2 = None
    grad_probs = jnp.zeros_like(probs)
    for j in range(turns):
        expert = lax.rem(place[0] + parts - j, parts)
        mask = (slots[0][:, j : j + 1] == seat).astype(F32).astype(BF16)
        both = dot_nn(mask, pairs[j][...])
        picked = both[:, :model]
        gate = jnp.sum(jnp.where(lane == expert, probs, 0.0), axis=-1, keepdims=True)
        mixture = gate * picked if mixture is None else mixture + gate * picked
        grad_gate = jnp.sum(grad_out * picked, axis=-1, keepdims=True)
        grad_probs = jnp.where(lane == expert, grad_gate, grad_probs)
        grad_n2 = both[:, model:] if grad_n2 is None else grad_n2 + both[:, model:]
    block_out[0] = ((residual + mixture) * live).astype(BF16)[:length]
    grad_logits = probs * (grad_probs - jnp.sum(probs * grad_probs, axis=-1, keepdims=True))
    grad_logits = grad_logits.astype(BF16)
    grad_n2 = grad_n2 + dot_nt(grad_logits, router)
    acc_router[...] += dot_tn(normed2, grad_logits)

    add_row(7, grad_n2 * xhat2)
    add_row(8, grad_n2)
    grad_res = grad_out + norm_back(grad_n2 * vector(7), xhat2, rstd2)
    gres_out[0] = grad_res
    branch = grad_res.astype(BF16)
    add_row(6, branch.astype(F32))
    acc_proj[...] += dot_tn(att[0], branch)
    gatt_out[0] = dot_nt(branch, full[:, 3 * model : 4 * model]).astype(BF16)

    @pl.when(b == pl.num_programs(0) - 1)
    def _():
        for copies in stores:
            for copy in copies:
                copy.wait()
        for j in range(turns):
            expert = lax.rem(place[0] + parts - j, parts)
            acc_small[12:32, pl.ds(pl.multiple_of(expert * 128, 128), 128)] = biases[j][0:20, :]
        late_out[:, :model] = acc_proj[...].astype(BF16)
        late_out[:, model:] = (acc_router[...] + acc_small[...].T).astype(BF16)


def combine_call(jobs, place, cot, att, res, tok, slots, full, small, pairs, biases):
    count, length, model = cot.shape
    size = att.shape[1]
    turns = len(pairs)
    arrays, plan, shapes, scratch = blend_plan(jobs)
    anywhere = pl.BlockSpec(memory_space=pl.ANY)
    outs = (
        jax.ShapeDtypeStruct((count, length, model), BF16),
        jax.ShapeDtypeStruct((count, size, model), F32),
        jax.ShapeDtypeStruct((count, size, model), BF16),
        jax.ShapeDtypeStruct((model, model + SMALL), BF16),
    )
    return pl.pallas_call(
        functools.partial(combine_kernel, turns=turns, jobs=plan, count_in=len(arrays)),
        out_shape=outs + tuple(shapes),
        grid_spec=pltpu.PrefetchScalarGridSpec(
            num_scalar_prefetch=1,
            grid=(count,),
            in_specs=[
                image(length, model), image(size, model), image(size, model),
                pl.BlockSpec((PAD, 2 * model), lambda i, *_: (i, 0)),
                image(size, slots.shape[2]), whole(full), whole(small),
            ] + [whole(a) for a in (*pairs, *biases)] + [anywhere] * len(arrays),
            out_specs=[image(length, model), image(size, model), image(size, model), whole(outs[3])] + [anywhere] * len(shapes),
            scratch_shapes=[
                pltpu.VMEM((size, model), F32),
                pltpu.VMEM((model, model), F32),
                pltpu.VMEM((model, SMALL), F32),
                pltpu.VMEM((SMALL, model), F32),
            ] + scratch,
        ),
        compiler_params=params(),
        cost_estimate=cost(18, 14),
        name="combine",
    )(place, cot, att, res, tok, slots, full, small, *pairs, *biases, *arrays)


def backward_kernel(
    place, images, qkv, lse, gres, gatt, full, small, late, input_grad, keep, send, rows, acc_qkv, acc_small,
):
    parts = keep.shape[1]
    b = pl.program_id(0)
    length, model = images.shape[1:]
    size = rows.shape[0]

    @pl.when(b == 0)
    def _():
        rows[...] = jnp.zeros_like(rows)
        acc_qkv[...] = jnp.zeros_like(acc_qkv)
        acc_small[...] = jnp.zeros_like(acc_small)

    def vector(row):
        return small[row : row + 1, :]

    def add_row(row, values):
        acc_small[row : row + 1, :] += jnp.sum(values, axis=0, keepdims=True)

    head = model // HEADS
    first = lax.broadcasted_iota(jnp.int32, (1, 2 * head), 1) < head
    real = lax.broadcasted_iota(jnp.int32, (1, size), 1) < length
    scale = 1.0 / math.sqrt(head)
    grads = [[], [], []]
    for two in range(HEADS // 2):
        lanes = lambda start: slice(start + two * 2 * head, start + (two + 1) * 2 * head)
        q2, k2, v2 = (qkv[0, :, lanes(s * model)] for s in range(3))
        g2 = gatt[0, :, lanes(0)]
        zero = jnp.zeros_like(q2)
        stack = lambda t: jnp.concatenate([jnp.where(first, t, zero), jnp.where(first, zero, t)], axis=0)
        merge = lambda t: jnp.where(first, t[:size], t[size:])
        qs, gs = stack(q2), stack(g2)
        logs = jnp.concatenate([lse[0, :, 2 * two : 2 * two + 1], lse[0, :, 2 * two + 1 : 2 * two + 2]], axis=0)
        weights = jnp.where(real, jnp.exp(dot_nt(qs, k2) * scale - logs), 0.0)
        grad_weights = dot_nt(gs, v2)
        grad_scores = weights * (grad_weights - jnp.sum(grad_weights * weights, axis=-1, keepdims=True))
        grad_scores = grad_scores.astype(BF16)
        grads[0].append((merge(dot_nn(grad_scores, k2)) * scale).astype(BF16))
        grads[1].append((dot_tn(grad_scores, qs) * scale).astype(BF16))
        grads[2].append(dot_tn(weights.astype(BF16), gs).astype(BF16))
    grad_projected = jnp.concatenate(grads[0] + grads[1] + grads[2], axis=1)
    rows[:length, :] = images[0].astype(F32)
    xhat1, rstd1 = norm_parts(rows[...])
    normed = (xhat1 * vector(4) + vector(5)).astype(BF16)
    acc_qkv[:, : 3 * model] += dot_tn(normed, grad_projected)
    grad_normed = dot_nt(grad_projected, full[:, : 3 * model])
    add_row(4, grad_normed * xhat1)
    add_row(5, grad_normed)
    add_row(32, grad_projected[:, :model].astype(F32))
    add_row(33, grad_projected[:, 2 * model :].astype(F32))
    input_grad[0] = (gres[0] + norm_back(grad_normed * vector(4), xhat1, rstd1))[:length]

    @pl.when(b == pl.num_programs(0) - 1)
    def _():
        for part in range(parts):
            for k in range(2):
                start = (part * 2 + k) * 128
                source = 32 + start // model
                acc_small[9 + k : 10 + k, part * 128 : part * 128 + 128] = acc_small[
                    source : source + 1, start % model : start % model + 128
                ]
        acc_small[32:34, :] = jnp.zeros((2, model), F32)
        acc_qkv[:, 3 * model :] = acc_small[...].T + late[:, model:].astype(F32)
        depth = keep.shape[2]
        for pos in range(PIECES):
            for d in range(parts):
                owner = jnp.bitwise_xor(place[0], d) * PIECES
                row = pl.multiple_of((owner + jnp.bitwise_xor(place[1], offset_of(pos))) * depth, depth)
                out = keep if pos < PIECES // 2 else send
                spot = pos % (PIECES // 2)
                out[spot, d, :, : 3 * model] = acc_qkv[pl.ds(row, depth), : 3 * model].astype(BF16)
                out[spot, d, :, 3 * model : 4 * model] = late[pl.ds(row, depth), :model]
                out[spot, d, :, 4 * model :] = acc_qkv[pl.ds(row, depth), 3 * model :].astype(BF16)


def backward_call(place, images, qkv, lse, gres, gatt, full, small, late, parts):
    count, length, model = images.shape
    size = qkv.shape[1]
    half = jax.ShapeDtypeStruct((PIECES // 2, parts, model // (parts * PIECES), 4 * model + SMALL), BF16)
    outs = (jax.ShapeDtypeStruct((count, length, model), F32), half, half)
    return pl.pallas_call(
        backward_kernel,
        out_shape=outs,
        grid_spec=pltpu.PrefetchScalarGridSpec(
            num_scalar_prefetch=1,
            grid=(count,),
            in_specs=[
                image(length, model), image(size, 3 * model), image(size, 128), image(size, model),
                image(size, model), whole(full), whole(small), whole(late),
            ],
            out_specs=[image(length, model), whole(half), whole(half)],
            scratch_shapes=[
                pltpu.VMEM((size, model), F32),
                pltpu.VMEM((model, 3 * model + SMALL), F32),
                pltpu.VMEM((SMALL, model), F32),
            ],
        ),
        compiler_params=params(),
        cost_estimate=cost(22, 14),
        name="attention_backward",
    )(place, images, qkv, lse, gres, gatt, full, small, late)


def finish_kernel(place, *refs, half):
    pieces = refs[: PIECES // 2]
    inner_out, outer_out, loaded, inner, outer, in_sems, out_sems = refs[-7:]
    block = outer.shape[1]
    loads = [pltpu.make_async_copy(p, loaded.at[k], in_sems.at[k]) for k, p in enumerate(pieces)]
    for copy in loads:
        copy.start()
    stores = []
    for k, copy in enumerate(loads):
        copy.wait()
        piece = jnp.bitwise_xor(place[1], offset_of(k + half * PIECES // 2))
        spot = pl.ds(pl.multiple_of(piece * block, block), block)
        inner[k] = loaded[k, 0].astype(F32).T
        outer[k] = loaded[k, 1].astype(F32)
        for side, (source, target) in enumerate(((inner.at[k], inner_out.at[0, :, spot]), (outer.at[k], outer_out.at[0, spot]))):
            stores.append(pltpu.make_async_copy(source, target, out_sems.at[k, side]))
            stores[-1].start()
    for copy in stores:
        copy.wait()


def finish_call(half, place, pieces, outs=()):
    _, block, model = pieces[0].shape
    count = len(pieces)
    anywhere = pl.BlockSpec(memory_space=pl.ANY)
    return pl.pallas_call(
        functools.partial(finish_kernel, half=half),
        out_shape=(
            jax.ShapeDtypeStruct((1, model, PIECES * block), F32),
            jax.ShapeDtypeStruct((1, PIECES * block, model), F32),
        ),
        in_specs=[pl.BlockSpec(memory_space=pltpu.SMEM)] + [anywhere] * (count + len(outs)),
        out_specs=(anywhere, anywhere),
        scratch_shapes=[
            pltpu.VMEM((count, 2, block, model), BF16),
            pltpu.VMEM((count, model, block), F32),
            pltpu.VMEM((count, block, model), F32),
            pltpu.SemaphoreType.DMA((count,)),
            pltpu.SemaphoreType.DMA((count, 2)),
        ],
        input_output_aliases={1 + count + k: k for k in range(len(outs))},
        compiler_params=params(),
        cost_estimate=cost(4, 6),
        name="finish_experts",
    )(place, *pieces, *outs)


def finish_dense_kernel(place, *refs):
    pieces = refs[:2]
    qkv_out, proj_out, router_out, inner_out, outer_out, *vector_outs, pair_out, table = refs[2:]
    model = proj_out.shape[1]
    depth = pieces[0].shape[1]
    for pos in range(PIECES):
        row = pl.multiple_of(jnp.bitwise_xor(place[1], offset_of(pos)) * depth, depth)
        block = pieces[pos // (PIECES // 2)][pos % (PIECES // 2)].astype(F32)
        qkv_out[pl.ds(row, depth), :] = block[:, : 3 * model]
        proj_out[pl.ds(row, depth), :] = block[:, 3 * model : 4 * model]
        table[pl.ds(row, depth), :] = block[:, 4 * model :]
    table[...] = table[...].T
    router_out[...] = table[: router_out.shape[0], :]
    for k, out in enumerate(vector_outs):
        out[...] = table[4 + k, :]
    for k in range(2):
        pair_out[pl.ds(k * 128, 128)] = table[9 + k, :]
    for c in range(inner_out.shape[1] // 128):
        inner_out[:, c * 128 : (c + 1) * 128] = table[12 + c : 13 + c, :]
    for c in range(outer_out.shape[1] // 128):
        outer_out[:, c * 128 : (c + 1) * 128] = table[28 + c : 29 + c, :]


def finish_dense_call(place, pieces, model, parts, hidden):
    rows = pieces[0].shape[1] * PIECES
    vmem = pl.BlockSpec(memory_space=pltpu.VMEM)
    return pl.pallas_call(
        finish_dense_kernel,
        out_shape=(
            jax.ShapeDtypeStruct((rows, 3 * model), F32),
            jax.ShapeDtypeStruct((rows, model), F32),
            jax.ShapeDtypeStruct((parts, rows), F32),
            jax.ShapeDtypeStruct((1, hidden), F32),
            jax.ShapeDtypeStruct((1, model), F32),
        )
        + tuple(jax.ShapeDtypeStruct((n,), F32) for n in (rows, rows, rows, rows, rows, 2 * rows)),
        in_specs=[pl.BlockSpec(memory_space=pltpu.SMEM)] + [vmem] * 2,
        scratch_shapes=[pltpu.VMEM((rows, SMALL), F32)],
        cost_estimate=cost(2, 2),
        name="finish_dense",
    )(place, *pieces)


def join(*values):
    return lax.optimization_barrier(values)


def local(
    images, attn_norm_gain, attn_norm_bias, qkv_weight, query_value_bias, proj_weight, proj_bias,
    moe_norm_gain, moe_norm_bias, router_weight, expert_inner, expert_inner_bias, expert_outer,
    expert_outer_bias, live_count, routes, slot_ids, cotangent, *, n_replica, n_group,
):
    count, length, model = images.shape
    shard = qkv_weight.shape[0]
    hidden = expert_inner.shape[2]
    size = padded(length)
    z = lax.axis_index("group").astype(jnp.int32)
    r = lax.axis_index("replica").astype(jnp.int32) & (PIECES - 1)
    place = jnp.stack([z, r, live_count[0].astype(jnp.int32), jnp.int32(n_group)])

    def across(value, bit):
        return lax.ppermute(value, "replica", [(i, i ^ bit) for i in range(n_replica)])

    def along(value, shift):
        return lax.ppermute(value, "group", [(i, (i + shift) % n_group) for i in range(n_group)])

    def between(value, bit):
        return lax.ppermute(value, "group", [(i, i ^ bit) for i in range(n_group)])

    def plus(*values):
        return sum(v.astype(F32) for v in values).astype(BF16)

    def both(value, bit):
        return jnp.concatenate([value, across(value, bit)], axis=0)

    def spread(value):
        return [value] + [across(value, offset_of(pos)) for pos in range(1, PIECES // 2)]

    def rest_of_replicas(value):
        bit = PIECES
        while bit < n_replica:
            value = plus(value, across(value, bit))
            bit *= 2
        return value

    shifts = list(range(1, n_group))

    vectors = (attn_norm_gain, attn_norm_bias, proj_bias, moe_norm_gain, moe_norm_bias, query_value_bias)
    mine, own_table = pack_call(
        place, qkv_weight, proj_weight, router_weight, vectors + (expert_inner_bias, expert_outer_bias)
    )
    dense_z = {d: along(mine, d) for d in shifts}

    piece = cut_call(place, expert_inner, expert_outer)
    piece, dense_z = join(piece, dense_z)
    expert_z = {1: along(piece, 1)}
    dense = spread(jnp.stack([dense_z[d] for d in shifts]))
    dense = dense + [across(v, 1) for v in dense]

    experts = (z + n_group - jnp.arange(n_group, dtype=jnp.int32)) % n_group
    chosen = routes[:, None] == experts[None, :, None, None]
    seats = jnp.max(jnp.where(chosen, slot_ids[:, None], -1), axis=-1)
    slots_lane = jnp.pad(seats, ((0, 0), (0, 8 - n_group), (0, PAD - length)), constant_values=-1)
    slots_row = jnp.pad(
        seats.transpose(0, 2, 1), ((0, 0), (0, size - length), (0, 8 - n_group)), constant_values=-1
    )

    def sources(pos, side):
        return pos // (PIECES // 2), (pos % (PIECES // 2), side)

    outs, cores, chips, shards = {}, {}, {}, {}
    places = ((1, 0), (0, 1), (1, 1))

    def quarters(k):
        return [("sum", [(outs[k][0], at), (cores[k], at)]) for at in places]

    def own_quarter(k):
        return ("sum", [(outs[k][0], (0, 0)), (cores[k], (0, 0))] + [(v, ()) for v in chips[k]])

    def send_chips(values):
        return [across(v, offset_of(pos)) for pos, v in zip(range(1, PIECES // 2), values)]

    def send_shard(k, value):
        value = rest_of_replicas(value)
        return along(value, -k) if k else value

    spread_1 = spread(expert_z[1])
    piece, expert_z[1] = join(piece, expert_z[1])
    expert_z[2] = along(piece, 2)
    images, slots_lane, slots_row = join(images, slots_lane, slots_row)
    qkv, att, res, lse, tok, gates, full, small = forward_call(place, images, cotangent, dense, own_table)
    tok, gates, small, piece, spread_1, expert_z = join(tok, gates, small, piece, spread_1, expert_z)
    tables = (slots_lane, gates, small)

    spread_2 = spread(expert_z[2])
    expert_z[3] = along(piece, 3)
    outs[0] = expert_call(0, place, tok, *tables, ((expert_inner, expert_outer), None), spread_1)
    outs, tok, spread_2, expert_z = join(outs, tok, spread_2, expert_z)

    weights = (outs[0][4], across(outs[0][4], 1))
    cores[0] = across(outs[0][1], 1)
    spread_3 = spread(expert_z[3])
    outs[1] = expert_call(1, place, tok, *tables, (weights, sources), spread_2)
    outs, tok, cores, spread_3 = join(outs, tok, cores, spread_3)

    weights = (outs[1][4], across(outs[1][4], 1))
    cores[1] = across(outs[1][1], 1)
    chips[0] = send_chips(blend_call(*quarters(0)))
    outs[2] = expert_call(2, place, tok, *tables, (weights, sources), spread_3)
    outs, tok, cores, chips = join(outs, tok, cores, chips)

    weights = (outs[2][4], across(outs[2][4], 1))
    cores[2] = across(outs[2][1], 1)
    chips[1] = send_chips(blend_call(*quarters(1)))
    outs[3] = expert_call(3, place, tok, *tables, (weights, sources))
    outs, cores, chips, shards = join(outs, cores, chips, shards)

    cores[3] = across(outs[3][1], 1)
    chips[2] = send_chips(blend_call(*quarters(2)))
    pairs = [outs[k][2] for k in range(n_group)]
    biases = [outs[k][3] for k in range(n_group)]
    block_out, gres, gatt, late, shards[0], shards[1], *parts = combine_call(
        (own_quarter(0), own_quarter(1), *quarters(3)), place, cotangent, att, res, tok, slots_row, full, small, pairs, biases
    )
    gres, gatt, late, cores, chips, shards, parts = join(gres, gatt, late, cores, chips, shards, parts)

    chips[3] = send_chips(parts)
    shards[2], = blend_call(own_quarter(2))
    passed = along(rest_of_replicas(shards.pop(2)), 1)
    for k in range(2):
        shards[k] = send_shard(k, shards[k])
    input_grad, keep, send = backward_call(place, images, qkv, lse, gres, gatt, full, small, late, n_group)
    keep, send, chips, shards, passed = join(keep, send, chips, shards, passed)
    if n_replica == PIECES:
        value, = blend_call(("sum", own_quarter(3)[1] + [(passed, ())]))
    else:
        value = plus(rest_of_replicas(*blend_call(own_quarter(3))), passed)
    shards[3] = along(value, 1)

    value = plus(keep, across(send, 1))
    value = plus(value[0], *(across(value[pos], offset_of(pos)) for pos in range(1, PIECES // 2)))
    value = rest_of_replicas(value)
    total, = blend_call(("sum", [(v, ()) for v in shards.values()]))
    value, total = join(value, total)
    own_half = spread(total)
    value = plus(value[:2], between(value[2:], 2))
    value = plus(value[0], between(value[1], 1))
    value = spread(value)
    other_half = [across(v, 1) for v in own_half]
    grads = finish_call(0, place, own_half)
    grad_inner, grad_outer = finish_call(1, place, other_half, grads)
    value, grad_inner, grad_outer = join(value, grad_inner, grad_outer)
    value = jnp.stack(value)
    value = (value, across(value, 1))
    grad_qkv, grad_proj, grad_router, grad_inner_bias, grad_outer_bias, *rest = finish_dense_call(
        place, value, model, n_group, hidden
    )
    return (
        block_out, input_grad, rest[0], rest[1], grad_qkv, rest[5], grad_proj, rest[2], rest[3], rest[4],
        grad_router.T, grad_inner, grad_inner_bias, grad_outer, grad_outer_bias,
    )


def solution(mesh):
    both = ("replica", "group")
    in_specs = (
        P(both, None, None), P("group"), P("group"), P("group", None), P("group"), P("group", None),
        P("group"), P("group"), P("group"), P("group", None), P("group", None, None), P("group", None),
        P("group", None, None), P("group", None), P(both), P(both, None, None), P(both, None, None),
        P(both, None, None),
    )
    out_specs = (
        P(both, None, None), P(both, None, None), P("group"), P("group"), P("group", None), P("group"),
        P("group", None), P("group"), P("group"), P("group"), P("group", None), P("group", None, None),
        P("group", None), P("group", None, None), P("group", None),
    )
    body = functools.partial(local, n_replica=mesh.shape["replica"], n_group=mesh.shape["group"])
    return jax.shard_map(body, mesh=mesh, in_specs=in_specs, out_specs=out_specs, check_vma=False)
```

```python
import functools
import math

import jax
import jax.numpy as jnp
from jax import lax
from jax.experimental import pallas as pl
from jax.experimental.pallas import tpu as pltpu
from jax.sharding import PartitionSpec as P

HEADS = 8
CAP = 640
NORM_EPS = 1e-06
F32 = jnp.float32
BF16 = jnp.bfloat16
PAD = 256
PIECES = 8
BITS = (2, 4, 1)
WIDE = 512
SMALL = 128
MIB = 1 << 20


def offset_of(position):
    total = 0
    for k, bit in enumerate(BITS):
        total = total + ((position >> k) & 1) * bit
    return total


def dot_nn(a, b):
    return lax.dot_general(a, b, (((1,), (0,)), ((), ())), preferred_element_type=F32)


def dot_nt(a, b):
    return lax.dot_general(a, b, (((1,), (1,)), ((), ())), preferred_element_type=F32)


def dot_tn(a, b):
    return lax.dot_general(a, b, (((0,), (0,)), ((), ())), preferred_element_type=F32)


def norm_parts(values):
    center = values - jnp.mean(values, axis=-1, keepdims=True)
    spread = jnp.mean(center * center, axis=-1, keepdims=True)
    rstd = lax.rsqrt(spread + NORM_EPS)
    return center * rstd, rstd


def gelu_parts(v):
    size = jnp.abs(v)
    density = jnp.exp(v * v * (-0.5)) * 0.3989422804014327
    t = 1.0 / (1.0 + 0.2316418882 * size)
    series = t * (
        0.319381530 + t * (-0.356563782 + t * (1.781477937 + t * (-1.821255978 + t * 1.330274429)))
    )
    tail = density * series
    phi = jnp.where(v < 0, tail, 1.0 - tail)
    return v * phi, phi + v * density


def params(megabytes=62):
    return pltpu.CompilerParams(vmem_limit_bytes=megabytes * MIB)


def cost(microseconds, megabytes):
    return pl.CostEstimate(flops=int(microseconds * 1.1e9), bytes_accessed=int(megabytes * MIB), transcendentals=0)


def padded(length):
    return -(-length // 16) * 16


def pack_kernel(place, qkv, proj, router, *refs):
    *vectors, out, table, lines, turned = refs
    depth = out.shape[0]
    row = pl.multiple_of(place[1] * depth, depth)
    width = qkv.shape[1] + proj.shape[1]
    lines[...] = jnp.zeros_like(lines)
    lines[: router.shape[0], :] = router[...].astype(F32)
    at = 4
    for vector in vectors:
        values = vector[...].astype(F32).reshape(1, -1)
        for c in range(values.shape[1] // 128):
            lines[at : at + 1, :] = values[:, c * 128 : (c + 1) * 128]
            at += 1
        if at == 11:
            at = 12
    turned[...] = lines[...].T
    out[:, : qkv.shape[1]] = qkv[pl.ds(row, depth), :]
    out[:, qkv.shape[1] : width] = proj[pl.ds(row, depth), :]
    out[:, width:] = turned[pl.ds(row, depth), :].astype(BF16)
    table[:, : qkv.shape[1]] = qkv[...]
    table[:, qkv.shape[1] : width] = proj[...]
    table[:, width:] = turned[...].astype(BF16)


def pack_call(place, qkv, proj, router, vectors):
    shard = qkv.shape[0]
    vmem = pl.BlockSpec(memory_space=pltpu.VMEM)
    return pl.pallas_call(
        pack_kernel,
        out_shape=tuple(
            jax.ShapeDtypeStruct((rows, qkv.shape[1] + proj.shape[1] + SMALL), BF16) for rows in (shard // PIECES, shard)
        ),
        in_specs=[pl.BlockSpec(memory_space=pltpu.SMEM)] + [vmem] * (3 + len(vectors)),
        out_specs=(vmem, vmem),
        scratch_shapes=[pltpu.VMEM((SMALL, shard), F32), pltpu.VMEM((shard, SMALL), F32)],
        cost_estimate=cost(2, 1),
        name="pack_dense",
    )(place, qkv, proj, router.T, *vectors)


def cut_kernel(place, inner, outer, out):
    out[0] = inner[0].T
    out[1] = outer[0]


def cut_call(place, inner, outer):
    _, model, hidden = inner.shape
    block = hidden // PIECES
    return pl.pallas_call(
        cut_kernel,
        out_shape=jax.ShapeDtypeStruct((2, block, model), BF16),
        grid_spec=pltpu.PrefetchScalarGridSpec(
            num_scalar_prefetch=1,
            grid=(1,),
            in_specs=[
                pl.BlockSpec((1, model, block), lambda i, s: (0, 0, s[1])),
                pl.BlockSpec((1, block, model), lambda i, s: (0, s[1], 0)),
            ],
            out_specs=pl.BlockSpec((2, block, model), lambda i, s: (0, 0, 0)),
        ),
        compiler_params=params(),
        cost_estimate=cost(2, 1),
        name="cut_own",
    )(place, inner, outer)


def forward_kernel(
    place, images, cot, *refs,
):
    dense = refs[:PIECES]
    own, qkv_out, att_out, res_out, lse_out, tok_out, gates_out, full_out, small_out, rows = refs[PIECES:]
    model = images.shape[2]
    length = images.shape[1]
    size = rows.shape[0]
    parts = dense[0].shape[0] + 1
    depth = dense[0].shape[1]

    @pl.when(pl.program_id(0) == 0)
    def _():
        z, r = place[0], place[1]
        for pos in range(PIECES):
            for d in range(1, parts):
                owner = lax.rem(z + parts - d, parts) * PIECES
                row = pl.multiple_of((owner + jnp.bitwise_xor(r, offset_of(pos))) * depth, depth)
                full_out[pl.ds(row, depth), :] = dense[pos][d - 1]
        full_out[pl.ds(pl.multiple_of(z * PIECES * depth, depth), PIECES * depth), :] = own[...]
        small_out[...] = full_out[:, 4 * model :].astype(F32).T
        rows[...] = jnp.zeros_like(rows)

    def vector(row):
        return small_out[row : row + 1, :]

    rows[:length, :] = images[0].astype(F32)
    x = rows[...]
    xhat, _ = norm_parts(x)
    normed = (xhat * vector(4) + vector(5)).astype(BF16)
    projected = dot_nn(normed, full_out[:, : 3 * model])
    bias_parts = []
    for part in range(parts):
        lanes = slice(part * 128, part * 128 + 128)
        bias_parts += [small_out[9:10, lanes], small_out[10:11, lanes]]
    pair = jnp.concatenate(bias_parts, axis=1)
    qkv_out[0, :, :model] = (projected[:, :model] + pair[:, :model]).astype(BF16)
    qkv_out[0, :, model : 2 * model] = projected[:, model : 2 * model].astype(BF16)
    qkv_out[0, :, 2 * model :] = (projected[:, 2 * model :] + pair[:, model:]).astype(BF16)
    qkv_out[0, length:, :] = jnp.zeros((size - length, 3 * model), BF16)

    head = model // HEADS
    first = lax.broadcasted_iota(jnp.int32, (1, 2 * head), 1) < head
    real = lax.broadcasted_iota(jnp.int32, (1, size), 1) < length
    column = lax.broadcasted_iota(jnp.int32, (size, 128), 1)
    scale = 1.0 / math.sqrt(head)
    lse = jnp.zeros((size, 128), F32)
    attended = []
    for two in range(HEADS // 2):
        lanes = lambda start: slice(start + two * 2 * head, start + (two + 1) * 2 * head)
        q2, k2, v2 = (qkv_out[0, :, lanes(s * model)] for s in range(3))
        zero = jnp.zeros_like(q2)
        stack = jnp.concatenate([jnp.where(first, q2, zero), jnp.where(first, zero, q2)], axis=0)
        scores = jnp.where(real, dot_nt(stack, k2) * scale, -1e30)
        peak = jnp.max(scores, axis=-1, keepdims=True)
        e = jnp.exp(scores - peak)
        total = jnp.sum(e, axis=-1, keepdims=True)
        probs = (e * (1.0 / total)).astype(BF16)
        both = dot_nn(probs, v2)
        attended.append(jnp.where(first, both[:size], both[size:]).astype(BF16))
        logs = peak + jnp.log(total)
        lse = jnp.where(column == 2 * two, logs[:size], lse)
        lse = jnp.where(column == 2 * two + 1, logs[size:], lse)
    lse_out[0] = lse
    attended = jnp.concatenate(attended, axis=1)
    att_out[0] = attended
    residual = x + (dot_nn(attended, full_out[:, 3 * model : 4 * model]) + vector(6))
    res_out[0] = residual
    xhat2, _ = norm_parts(residual)
    normed2 = (xhat2 * vector(7) + vector(8)).astype(BF16)
    tail = length // 16 * 16
    tok_out[tail:, :] = jnp.zeros((PAD - tail, 2 * model), BF16)
    tok_out[:size, :model] = normed2
    tok_out[:length, model:] = cot[0]
    logits = dot_nt(small_out[0:8, :].astype(BF16), tok_out[:, :model])
    experts = lax.broadcasted_iota(jnp.int32, logits.shape, 0) < parts
    logits = jnp.where(experts, logits, -jnp.inf)
    e = jnp.exp(logits - jnp.max(logits, axis=0, keepdims=True))
    gates_out[0] = e / jnp.sum(e, axis=0, keepdims=True)


def whole(a):
    return pl.BlockSpec(a.shape, lambda i, *_: (0,) * len(a.shape))


def image(*dims):
    return pl.BlockSpec((1,) + dims, lambda i, *_: (i, 0, 0))


def forward_call(place, images, cot, dense, own):
    count, length, model = images.shape
    size = padded(length)
    outs = (
        jax.ShapeDtypeStruct((count, size, 3 * model), BF16),
        jax.ShapeDtypeStruct((count, size, model), BF16),
        jax.ShapeDtypeStruct((count, size, model), F32),
        jax.ShapeDtypeStruct((count, size, 128), F32),
        jax.ShapeDtypeStruct((count * PAD, 2 * model), BF16),
        jax.ShapeDtypeStruct((count, 8, PAD), F32),
        jax.ShapeDtypeStruct((model, 4 * model + SMALL), BF16),
        jax.ShapeDtypeStruct((SMALL, model), F32),
    )
    return pl.pallas_call(
        forward_kernel,
        out_shape=outs,
        grid_spec=pltpu.PrefetchScalarGridSpec(
            num_scalar_prefetch=1,
            grid=(count,),
            in_specs=[image(length, model), image(length, model)] + [whole(d) for d in (*dense, own)],
            out_specs=[
                image(size, 3 * model), image(size, model), image(size, model), image(size, 128),
                pl.BlockSpec((PAD, 2 * model), lambda i, *_: (i, 0)),
                image(8, PAD), whole(outs[6]), whole(outs[7]),
            ],
            scratch_shapes=[pltpu.VMEM((size, model), F32)],
        ),
        compiler_params=params(),
        cost_estimate=cost(12, 12),
        name="attention_forward",
    )(place, images, cot, *dense, own)


def blend_loads(jobs, arrays, loaded, sems):
    copies = []
    for _, terms in jobs:
        for which, index in terms:
            spot = len(copies)
            source = arrays[which].at[index] if index else arrays[which]
            copies.append(pltpu.make_async_copy(source, loaded.at[spot], sems.at[spot]))
    return copies


def blend_stores(jobs, outs, loaded, summed, sems):
    copies, spot, sums = [], 0, 0
    for out, (kind, terms) in zip(outs, jobs):
        if kind == "collect":
            pairs = [(loaded.at[spot + k], out.at[k]) for k in range(len(terms))]
        else:
            pairs = [(summed.at[sums], out)]
            sums += 1
        spot += len(terms)
        copies.append([pltpu.make_async_copy(a, b, sems.at[sum(map(len, copies)) + k]) for k, (a, b) in enumerate(pairs)])
    return copies


def blend_work(jobs, loads, stores, loaded, summed):
    spot = sums = 0
    for (kind, terms), copies in zip(jobs, stores):
        total = None
        for k in range(len(terms)):
            loads[spot].wait()
            if kind == "collect":
                copies[k].start()
            else:
                value = loaded[spot].astype(F32)
                total = value if total is None else total + value
            spot += 1
        if kind == "sum":
            summed[sums] = total.astype(BF16)
            copies[0].start()
            sums += 1


def blend_kernel(*refs, jobs, count_in):
    arrays = refs[:count_in]
    outs = refs[count_in : count_in + len(jobs)]
    loaded, summed, in_sems, out_sems = refs[count_in + len(jobs) :]
    loads = blend_loads(jobs, arrays, loaded, in_sems)
    for copy in loads:
        copy.start()
    stores = blend_stores(jobs, outs, loaded, summed, out_sems)
    blend_work(jobs, loads, stores, loaded, summed)
    for copies in stores:
        for copy in copies:
            copy.wait()


def blend_plan(jobs):
    arrays, plan, shapes = [], [], []
    for kind, terms in jobs:
        listed = []
        for array, index in terms:
            known = [k for k, a in enumerate(arrays) if a is array]
            if not known:
                arrays.append(array)
                known = [len(arrays) - 1]
            listed.append((known[0], index))
        unit = terms[0][0].shape[len(terms[0][1]) :]
        shapes.append(jax.ShapeDtypeStruct(((len(terms),) if kind == "collect" else ()) + unit, BF16))
        plan.append((kind, tuple(listed)))
    units = sum(len(terms) for _, terms in plan)
    sums = sum(kind == "sum" for kind, _ in plan)
    stores = sums + sum(len(terms) for kind, terms in plan if kind == "collect")
    scratch = [
        pltpu.VMEM((units,) + unit, BF16),
        pltpu.VMEM((max(sums, 1),) + unit, BF16),
        pltpu.SemaphoreType.DMA((units,)),
        pltpu.SemaphoreType.DMA((stores,)),
    ]
    return arrays, tuple(plan), shapes, scratch


def blend_call(*jobs):
    arrays, plan, shapes, scratch = blend_plan(jobs)
    anywhere = pl.BlockSpec(memory_space=pl.ANY)
    return pl.pallas_call(
        functools.partial(blend_kernel, jobs=plan, count_in=len(arrays)),
        out_shape=tuple(shapes),
        in_specs=[anywhere] * len(arrays),
        out_specs=(anywhere,) * len(shapes),
        scratch_shapes=scratch,
        compiler_params=params(),
        cost_estimate=cost(3, 3),
        name="blend",
    )(*arrays)


def expert_kernel(place, slots, gates, small, tok, *refs, turn, sources, count_in, count_side):
    arrays = refs[:count_in]
    beside = refs[count_in : count_in + count_side]
    count_in += count_side
    keep, send, pair_out, bias_out = refs[count_in : count_in + 4]
    if count_side:
        collected, passing, side_sems = refs[count_in + 4], refs[-2], refs[-1]
        refs = refs[: count_in + 4] + refs[count_in + 5 : -2]
    tokens, onehot, buffer, grad_slots, rows, back, mine, inners, outers, staged, token_sem, in_sems, out_sems = (
        refs[count_in + 4 :]
    )
    local = sources is None
    count = slots.shape[0]
    model = buffer.shape[1]
    block = outers.shape[1]
    per = staged.shape[1]
    steps = staged.shape[0]

    token_copy = pltpu.make_async_copy(tok, tokens, token_sem)
    token_copy.start()
    loads = []
    for pos in range(PIECES):
        for side, matrices in enumerate((inners, outers)):
            if local:
                start = pl.multiple_of(jnp.bitwise_xor(place[1], offset_of(pos)) * block, block)
                source = arrays[1].at[0, pl.ds(start, block)] if side else arrays[0].at[0, :, pl.ds(start, block)]
            else:
                which, at = sources(pos, side)
                source = arrays[which].at[at]
            loads.append(pltpu.make_async_copy(source, matrices.at[pos], in_sems.at[pos, side]))

    expert = lax.rem(place[0] + place[3] - turn, place[3])
    lanes = pl.ds(pl.multiple_of(expert * 128, 128), 128)
    mine[...] = small[:, lanes]
    where = lax.broadcasted_iota(jnp.int32, (CAP, PAD), 0)
    gate = jnp.zeros((CAP, 128), F32)
    for b in range(count):
        mask = where == slots[b, turn : turn + 1, :]
        onehot[:, b * PAD : (b + 1) * PAD] = mask.astype(F32).astype(BF16)
        weighted = jnp.where(mask, gates[b, pl.ds(expert, 1), :], 0.0)
        gate = gate + weighted[:, :128] + weighted[:, 128:]
    gate = jnp.sum(gate, axis=1, keepdims=True)
    outer_bias = jnp.concatenate([mine[28 + c : 29 + c, :] for c in range(model // 128)], axis=1)
    token_copy.wait()
    for copy in loads:
        copy.start()
    side_loads = [pltpu.make_async_copy(b, passing.at[k], side_sems.at[0, k]) for k, b in enumerate(beside)]
    side_stores = [pltpu.make_async_copy(passing.at[k], collected.at[k], side_sems.at[1, k]) for k in range(count_side)]
    for copy in side_loads:
        copy.start()
    buffer[...] = dot_nn(onehot[...], tokens[:, :model]).astype(BF16)
    grads = (dot_nn(onehot[...], tokens[:, model:]) * gate).astype(BF16)
    grad_slots[...] = grads
    sums = jnp.sum(grads.astype(F32), axis=0, keepdims=True)
    for c in range(model // 128):
        bias_out[16 + c : 17 + c, :] = sums[:, c * 128 : (c + 1) * 128]
    bias_out[20:32, :] = jnp.zeros((12, 128), F32)

    def first_products(i):
        for copy in loads[2 * i * per : 2 * (i + 1) * per]:
            copy.wait()
        buf, gs = buffer[...], grad_slots[...]
        here = slice(i * per, (i + 1) * per)
        lines = [
            jnp.bitwise_xor(place[1], offset_of(pos)) * (block // 128) + c
            for pos in range(here.start, here.stop)
            for c in range(block // 128)
        ]
        bias = jnp.concatenate([mine[pl.ds(12 + line, 1), :] for line in lines], axis=1)
        if local:
            hidden = jnp.concatenate([dot_nn(buf, inners[pos]) for pos in range(here.start, here.stop)], axis=1)
        else:
            hidden = dot_nt(buf, inners[here].reshape(per * block, model))
        return hidden + bias, dot_nt(gs, outers[here].reshape(per * block, model)), lines

    stores = []
    for i in range(steps):
        hidden, grad_active, lines = first_products(i)
        if i == 1:
            for load, store in zip(side_loads, side_stores):
                load.wait()
                store.start()
        here = slice(i * per, (i + 1) * per)
        active, slope = gelu_parts(hidden)
        active = active.astype(BF16)
        grad_low = (grad_active * slope).astype(BF16)
        sums = jnp.sum(grad_low.astype(F32), axis=0, keepdims=True)
        for k, line in enumerate(lines):
            bias_out[pl.ds(line, 1), :] = sums[:, k * 128 : (k + 1) * 128]
        staged[i, :, 0] = dot_tn(grad_low, buffer[...]).astype(BF16).reshape(per, block, model)
        staged[i, :, 1] = dot_tn(active, grad_slots[...]).astype(BF16).reshape(per, block, model)
        out = keep if i < steps // 2 else send
        stores.append(pltpu.make_async_copy(staged.at[i], out.at[:, i % (steps // 2)], out_sems.at[i]))
        stores[-1].start()
        new_rows = dot_nn(active, outers[here].reshape(per * block, model))
        if local:
            new_back = sum(
                dot_nt(grad_low[:, j * block : (j + 1) * block], inners[i * per + j]) for j in range(per)
            )
        else:
            new_back = dot_nn(grad_low, inners[here].reshape(per * block, model))
        rows[...] = new_rows + (outer_bias if i == 0 else rows[...])
        back[...] = new_back if i == 0 else new_back + back[...]
    pair_out[:, :model] = rows[...].astype(BF16)
    pair_out[:, model:] = back[...].astype(BF16)
    for copy in stores + side_stores:
        copy.wait()


def expert_call(turn, place, tok, slots, gates, small, weights, beside=()):
    arrays, sources = weights
    model = tok.shape[1] // 2
    count = slots.shape[0]
    block = arrays[1].shape[1] // PIECES if sources is None else arrays[0].shape[-2]
    per = WIDE // block
    steps = PIECES // per
    vmem = pl.BlockSpec(memory_space=pltpu.VMEM)
    anywhere = pl.BlockSpec(memory_space=pl.ANY)
    half = jax.ShapeDtypeStruct((2, 2, 2, block, model), BF16)
    return pl.pallas_call(
        functools.partial(expert_kernel, turn=turn, sources=sources, count_in=len(arrays), count_side=len(beside)),
        out_shape=(
            half,
            half,
            jax.ShapeDtypeStruct((CAP, 2 * model), BF16),
            jax.ShapeDtypeStruct((32, 128), F32),
        )
        + tuple(jax.ShapeDtypeStruct((len(beside),) + b.shape, BF16) for b in beside[:1]),
        in_specs=[pl.BlockSpec(memory_space=pltpu.SMEM), vmem, vmem, vmem, anywhere]
        + [anywhere] * (len(arrays) + len(beside)),
        out_specs=[anywhere, anywhere, vmem, vmem] + [anywhere] * len(beside[:1]),
        scratch_shapes=[
            pltpu.VMEM(tok.shape, BF16),
            pltpu.VMEM((CAP, count * PAD), BF16),
            pltpu.VMEM((CAP, model), BF16),
            pltpu.VMEM((CAP, model), BF16),
            pltpu.VMEM((CAP, model), F32),
            pltpu.VMEM((CAP, model), F32),
            pltpu.VMEM((SMALL, 128), F32),
            pltpu.VMEM((PIECES, model, block) if sources is None else (PIECES, block, model), BF16),
            pltpu.VMEM((PIECES, block, model), BF16),
            pltpu.VMEM((steps, per, 2, block, model), BF16),
            pltpu.SemaphoreType.DMA(()),
            pltpu.SemaphoreType.DMA((PIECES, 2)),
            pltpu.SemaphoreType.DMA((steps,)),
        ]
        + [pltpu.VMEM((len(beside),) + b.shape, BF16) for b in beside[:1]]
        + [pltpu.SemaphoreType.DMA((2, len(beside))) for _ in beside[:1]],
        compiler_params=params(),
        cost_estimate=cost(18, 14),
        name="expert",
    )(place, slots, gates, small, tok, *arrays, *beside)


def norm_back(inner, xhat, rstd):
    return rstd * (
        inner - jnp.mean(inner, axis=-1, keepdims=True) - xhat * jnp.mean(inner * xhat, axis=-1, keepdims=True)
    )


def combine_kernel(place, *refs, turns, jobs, count_in):
    cot, att, res, tok, slots, full, small = refs[:7]
    pairs = refs[7 : 7 + turns]
    biases = refs[7 + turns : 7 + 2 * turns]
    arrays = refs[7 + 2 * turns : 7 + 2 * turns + count_in]
    block_out, gres_out, gatt_out, late_out, *side_outs = refs[7 + 2 * turns + count_in : -8]
    cots, acc_proj, acc_router, acc_small, loaded, summed, in_sems, out_sems = refs[-8:]
    b = pl.program_id(0)
    loads = blend_loads(jobs, arrays, loaded, in_sems)
    stores = blend_stores(jobs, side_outs, loaded, summed, out_sems)

    @pl.when(b == 0)
    def _():
        for copy in loads:
            copy.start()

    @pl.when(b == 1)
    def _():
        blend_work(jobs, loads, stores, loaded, summed)

    length, model = cot.shape[1:]
    size = cots.shape[0]
    parts = turns

    @pl.when(b == 0)
    def _():
        cots[...] = jnp.zeros_like(cots)
        for acc in (acc_proj, acc_router, acc_small):
            acc[...] = jnp.zeros_like(acc)

    def vector(row):
        return small[row : row + 1, :]

    def add_row(row, values):
        acc_small[row : row + 1, :] += jnp.sum(values, axis=0, keepdims=True)

    live = (b < place[2]).astype(F32)
    cots[:length, :] = cot[0].astype(F32) * live
    grad_out = cots[...]
    residual = res[0]
    xhat2, rstd2 = norm_parts(residual)
    normed2 = tok[:size, :model]
    router = full[:, 4 * model :]

    logits = dot_nn(normed2, router)
    lane = lax.broadcasted_iota(jnp.int32, logits.shape, 1)
    logits = jnp.where(lane < parts, logits, -jnp.inf)
    e = jnp.exp(logits - jnp.max(logits, axis=-1, keepdims=True))
    probs = e / jnp.sum(e, axis=-1, keepdims=True)

    seat = lax.broadcasted_iota(jnp.int32, (size, CAP), 1)
    mixture = None
    grad_n2 = None
    grad_probs = jnp.zeros_like(probs)
    for j in range(turns):
        expert = lax.rem(place[0] + parts - j, parts)
        mask = (slots[0][:, j : j + 1] == seat).astype(F32).astype(BF16)
        both = dot_nn(mask, pairs[j][...])
        picked = both[:, :model]
        gate = jnp.sum(jnp.where(lane == expert, probs, 0.0), axis=-1, keepdims=True)
        mixture = gate * picked if mixture is None else mixture + gate * picked
        grad_gate = jnp.sum(grad_out * picked, axis=-1, keepdims=True)
        grad_probs = jnp.where(lane == expert, grad_gate, grad_probs)
        grad_n2 = both[:, model:] if grad_n2 is None else grad_n2 + both[:, model:]
    block_out[0] = ((residual + mixture) * live).astype(BF16)[:length]
    grad_logits = probs * (grad_probs - jnp.sum(probs * grad_probs, axis=-1, keepdims=True))
    grad_logits = grad_logits.astype(BF16)
    grad_n2 = grad_n2 + dot_nt(grad_logits, router)
    acc_router[...] += dot_tn(normed2, grad_logits)

    add_row(7, grad_n2 * xhat2)
    add_row(8, grad_n2)
    grad_res = grad_out + norm_back(grad_n2 * vector(7), xhat2, rstd2)
    gres_out[0] = grad_res
    branch = grad_res.astype(BF16)
    add_row(6, branch.astype(F32))
    acc_proj[...] += dot_tn(att[0], branch)
    gatt_out[0] = dot_nt(branch, full[:, 3 * model : 4 * model]).astype(BF16)

    @pl.when(b == pl.num_programs(0) - 1)
    def _():
        for copies in stores:
            for copy in copies:
                copy.wait()
        for j in range(turns):
            expert = lax.rem(place[0] + parts - j, parts)
            acc_small[12:32, pl.ds(pl.multiple_of(expert * 128, 128), 128)] = biases[j][0:20, :]
        late_out[:, :model] = acc_proj[...].astype(BF16)
        late_out[:, model:] = (acc_router[...] + acc_small[...].T).astype(BF16)


def combine_call(jobs, place, cot, att, res, tok, slots, full, small, pairs, biases):
    count, length, model = cot.shape
    size = att.shape[1]
    turns = len(pairs)
    arrays, plan, shapes, scratch = blend_plan(jobs)
    anywhere = pl.BlockSpec(memory_space=pl.ANY)
    outs = (
        jax.ShapeDtypeStruct((count, length, model), BF16),
        jax.ShapeDtypeStruct((count, size, model), F32),
        jax.ShapeDtypeStruct((count, size, model), BF16),
        jax.ShapeDtypeStruct((model, model + SMALL), BF16),
    )
    return pl.pallas_call(
        functools.partial(combine_kernel, turns=turns, jobs=plan, count_in=len(arrays)),
        out_shape=outs + tuple(shapes),
        grid_spec=pltpu.PrefetchScalarGridSpec(
            num_scalar_prefetch=1,
            grid=(count,),
            in_specs=[
                image(length, model), image(size, model), image(size, model),
                pl.BlockSpec((PAD, 2 * model), lambda i, *_: (i, 0)),
                image(size, slots.shape[2]), whole(full), whole(small),
            ] + [whole(a) for a in (*pairs, *biases)] + [anywhere] * len(arrays),
            out_specs=[image(length, model), image(size, model), image(size, model), whole(outs[3])] + [anywhere] * len(shapes),
            scratch_shapes=[
                pltpu.VMEM((size, model), F32),
                pltpu.VMEM((model, model), F32),
                pltpu.VMEM((model, SMALL), F32),
                pltpu.VMEM((SMALL, model), F32),
            ] + scratch,
        ),
        compiler_params=params(),
        cost_estimate=cost(18, 14),
        name="combine",
    )(place, cot, att, res, tok, slots, full, small, *pairs, *biases, *arrays)


def backward_kernel(
    place, images, qkv, lse, gres, gatt, full, small, late, input_grad, keep, send, rows, acc_qkv, acc_small,
):
    parts = keep.shape[1]
    b = pl.program_id(0)
    length, model = images.shape[1:]
    size = rows.shape[0]

    @pl.when(b == 0)
    def _():
        rows[...] = jnp.zeros_like(rows)
        acc_qkv[...] = jnp.zeros_like(acc_qkv)
        acc_small[...] = jnp.zeros_like(acc_small)

    def vector(row):
        return small[row : row + 1, :]

    def add_row(row, values):
        acc_small[row : row + 1, :] += jnp.sum(values, axis=0, keepdims=True)

    head = model // HEADS
    first = lax.broadcasted_iota(jnp.int32, (1, 2 * head), 1) < head
    real = lax.broadcasted_iota(jnp.int32, (1, size), 1) < length
    scale = 1.0 / math.sqrt(head)
    grads = [[], [], []]
    for two in range(HEADS // 2):
        lanes = lambda start: slice(start + two * 2 * head, start + (two + 1) * 2 * head)
        q2, k2, v2 = (qkv[0, :, lanes(s * model)] for s in range(3))
        g2 = gatt[0, :, lanes(0)]
        zero = jnp.zeros_like(q2)
        stack = lambda t: jnp.concatenate([jnp.where(first, t, zero), jnp.where(first, zero, t)], axis=0)
        merge = lambda t: jnp.where(first, t[:size], t[size:])
        qs, gs = stack(q2), stack(g2)
        logs = jnp.concatenate([lse[0, :, 2 * two : 2 * two + 1], lse[0, :, 2 * two + 1 : 2 * two + 2]], axis=0)
        weights = jnp.where(real, jnp.exp(dot_nt(qs, k2) * scale - logs), 0.0)
        grad_weights = dot_nt(gs, v2)
        grad_scores = weights * (grad_weights - jnp.sum(grad_weights * weights, axis=-1, keepdims=True))
        grad_scores = grad_scores.astype(BF16)
        grads[0].append((merge(dot_nn(grad_scores, k2)) * scale).astype(BF16))
        grads[1].append((dot_tn(grad_scores, qs) * scale).astype(BF16))
        grads[2].append(dot_tn(weights.astype(BF16), gs).astype(BF16))
    grad_projected = jnp.concatenate(grads[0] + grads[1] + grads[2], axis=1)
    rows[:length, :] = images[0].astype(F32)
    xhat1, rstd1 = norm_parts(rows[...])
    normed = (xhat1 * vector(4) + vector(5)).astype(BF16)
    acc_qkv[:, : 3 * model] += dot_tn(normed, grad_projected)
    grad_normed = dot_nt(grad_projected, full[:, : 3 * model])
    add_row(4, grad_normed * xhat1)
    add_row(5, grad_normed)
    add_row(32, grad_projected[:, :model].astype(F32))
    add_row(33, grad_projected[:, 2 * model :].astype(F32))
    input_grad[0] = (gres[0] + norm_back(grad_normed * vector(4), xhat1, rstd1))[:length]

    @pl.when(b == pl.num_programs(0) - 1)
    def _():
        for part in range(parts):
            for k in range(2):
                start = (part * 2 + k) * 128
                source = 32 + start // model
                acc_small[9 + k : 10 + k, part * 128 : part * 128 + 128] = acc_small[
                    source : source + 1, start % model : start % model + 128
                ]
        acc_small[32:34, :] = jnp.zeros((2, model), F32)
        acc_qkv[:, 3 * model :] = acc_small[...].T + late[:, model:].astype(F32)
        depth = keep.shape[2]
        for pos in range(PIECES):
            for d in range(parts):
                owner = jnp.bitwise_xor(place[0], d) * PIECES
                row = pl.multiple_of((owner + jnp.bitwise_xor(place[1], offset_of(pos))) * depth, depth)
                out = keep if pos < PIECES // 2 else send
                spot = pos % (PIECES // 2)
                out[spot, d, :, : 3 * model] = acc_qkv[pl.ds(row, depth), : 3 * model].astype(BF16)
                out[spot, d, :, 3 * model : 4 * model] = late[pl.ds(row, depth), :model]
                out[spot, d, :, 4 * model :] = acc_qkv[pl.ds(row, depth), 3 * model :].astype(BF16)


def backward_call(place, images, qkv, lse, gres, gatt, full, small, late, parts):
    count, length, model = images.shape
    size = qkv.shape[1]
    half = jax.ShapeDtypeStruct((PIECES // 2, parts, model // (parts * PIECES), 4 * model + SMALL), BF16)
    outs = (jax.ShapeDtypeStruct((count, length, model), F32), half, half)
    return pl.pallas_call(
        backward_kernel,
        out_shape=outs,
        grid_spec=pltpu.PrefetchScalarGridSpec(
            num_scalar_prefetch=1,
            grid=(count,),
            in_specs=[
                image(length, model), image(size, 3 * model), image(size, 128), image(size, model),
                image(size, model), whole(full), whole(small), whole(late),
            ],
            out_specs=[image(length, model), whole(half), whole(half)],
            scratch_shapes=[
                pltpu.VMEM((size, model), F32),
                pltpu.VMEM((model, 3 * model + SMALL), F32),
                pltpu.VMEM((SMALL, model), F32),
            ],
        ),
        compiler_params=params(),
        cost_estimate=cost(22, 14),
        name="attention_backward",
    )(place, images, qkv, lse, gres, gatt, full, small, late)


def finish_kernel(place, *refs, half):
    pieces = refs[: PIECES // 2]
    inner_out, outer_out, loaded, inner, outer, in_sems, out_sems = refs[-7:]
    block = outer.shape[1]
    loads = [pltpu.make_async_copy(p, loaded.at[k], in_sems.at[k]) for k, p in enumerate(pieces)]
    for copy in loads:
        copy.start()
    stores = []
    for k, copy in enumerate(loads):
        copy.wait()
        piece = jnp.bitwise_xor(place[1], offset_of(k + half * PIECES // 2))
        spot = pl.ds(pl.multiple_of(piece * block, block), block)
        inner[k] = loaded[k, 0].astype(F32).T
        outer[k] = loaded[k, 1].astype(F32)
        for side, (source, target) in enumerate(((inner.at[k], inner_out.at[0, :, spot]), (outer.at[k], outer_out.at[0, spot]))):
            stores.append(pltpu.make_async_copy(source, target, out_sems.at[k, side]))
            stores[-1].start()
    for copy in stores:
        copy.wait()


def finish_call(half, place, pieces, outs=()):
    _, block, model = pieces[0].shape
    count = len(pieces)
    anywhere = pl.BlockSpec(memory_space=pl.ANY)
    return pl.pallas_call(
        functools.partial(finish_kernel, half=half),
        out_shape=(
            jax.ShapeDtypeStruct((1, model, PIECES * block), F32),
            jax.ShapeDtypeStruct((1, PIECES * block, model), F32),
        ),
        in_specs=[pl.BlockSpec(memory_space=pltpu.SMEM)] + [anywhere] * (count + len(outs)),
        out_specs=(anywhere, anywhere),
        scratch_shapes=[
            pltpu.VMEM((count, 2, block, model), BF16),
            pltpu.VMEM((count, model, block), F32),
            pltpu.VMEM((count, block, model), F32),
            pltpu.SemaphoreType.DMA((count,)),
            pltpu.SemaphoreType.DMA((count, 2)),
        ],
        input_output_aliases={1 + count + k: k for k in range(len(outs))},
        compiler_params=params(),
        cost_estimate=cost(4, 6),
        name="finish_experts",
    )(place, *pieces, *outs)


def finish_dense_kernel(place, *refs):
    pieces = refs[:2]
    qkv_out, proj_out, router_out, inner_out, outer_out, *vector_outs, pair_out, table = refs[2:]
    model = proj_out.shape[1]
    depth = pieces[0].shape[1]
    for pos in range(PIECES):
        row = pl.multiple_of(jnp.bitwise_xor(place[1], offset_of(pos)) * depth, depth)
        block = pieces[pos // (PIECES // 2)][pos % (PIECES // 2)].astype(F32)
        qkv_out[pl.ds(row, depth), :] = block[:, : 3 * model]
        proj_out[pl.ds(row, depth), :] = block[:, 3 * model : 4 * model]
        table[pl.ds(row, depth), :] = block[:, 4 * model :]
    table[...] = table[...].T
    router_out[...] = table[: router_out.shape[0], :]
    for k, out in enumerate(vector_outs):
        out[...] = table[4 + k, :]
    for k in range(2):
        pair_out[pl.ds(k * 128, 128)] = table[9 + k, :]
    for c in range(inner_out.shape[1] // 128):
        inner_out[:, c * 128 : (c + 1) * 128] = table[12 + c : 13 + c, :]
    for c in range(outer_out.shape[1] // 128):
        outer_out[:, c * 128 : (c + 1) * 128] = table[28 + c : 29 + c, :]


def finish_dense_call(place, pieces, model, parts, hidden):
    rows = pieces[0].shape[1] * PIECES
    vmem = pl.BlockSpec(memory_space=pltpu.VMEM)
    return pl.pallas_call(
        finish_dense_kernel,
        out_shape=(
            jax.ShapeDtypeStruct((rows, 3 * model), F32),
            jax.ShapeDtypeStruct((rows, model), F32),
            jax.ShapeDtypeStruct((parts, rows), F32),
            jax.ShapeDtypeStruct((1, hidden), F32),
            jax.ShapeDtypeStruct((1, model), F32),
        )
        + tuple(jax.ShapeDtypeStruct((n,), F32) for n in (rows, rows, rows, rows, rows, 2 * rows)),
        in_specs=[pl.BlockSpec(memory_space=pltpu.SMEM)] + [vmem] * 2,
        scratch_shapes=[pltpu.VMEM((rows, SMALL), F32)],
        cost_estimate=cost(2, 2),
        name="finish_dense",
    )(place, *pieces)


def join(*values):
    return lax.optimization_barrier(values)


def local(
    images, attn_norm_gain, attn_norm_bias, qkv_weight, query_value_bias, proj_weight, proj_bias,
    moe_norm_gain, moe_norm_bias, router_weight, expert_inner, expert_inner_bias, expert_outer,
    expert_outer_bias, live_count, routes, slot_ids, cotangent, *, n_replica, n_group,
):
    count, length, model = images.shape
    shard = qkv_weight.shape[0]
    hidden = expert_inner.shape[2]
    size = padded(length)
    z = lax.axis_index("group").astype(jnp.int32)
    r = lax.axis_index("replica").astype(jnp.int32) & (PIECES - 1)
    place = jnp.stack([z, r, live_count[0].astype(jnp.int32), jnp.int32(n_group)])

    def across(value, bit):
        return lax.ppermute(value, "replica", [(i, i ^ bit) for i in range(n_replica)])

    def along(value, shift):
        return lax.ppermute(value, "group", [(i, (i + shift) % n_group) for i in range(n_group)])

    def between(value, bit):
        return lax.ppermute(value, "group", [(i, i ^ bit) for i in range(n_group)])

    def plus(*values):
        return sum(v.astype(F32) for v in values).astype(BF16)

    def both(value, bit):
        return jnp.concatenate([value, across(value, bit)], axis=0)

    def spread(value):
        return [value] + [across(value, offset_of(pos)) for pos in range(1, PIECES // 2)]

    def rest_of_replicas(value):
        bit = PIECES
        while bit < n_replica:
            value = plus(value, across(value, bit))
            bit *= 2
        return value

    shifts = list(range(1, n_group))

    vectors = (attn_norm_gain, attn_norm_bias, proj_bias, moe_norm_gain, moe_norm_bias, query_value_bias)
    mine, own_table = pack_call(
        place, qkv_weight, proj_weight, router_weight, vectors + (expert_inner_bias, expert_outer_bias)
    )
    dense_z = {d: along(mine, d) for d in shifts}

    piece = cut_call(place, expert_inner, expert_outer)
    piece, dense_z = join(piece, dense_z)
    expert_z = {1: along(piece, 1)}
    dense = spread(jnp.stack([dense_z[d] for d in shifts]))
    dense = dense + [across(v, 1) for v in dense]

    experts = (z + n_group - jnp.arange(n_group, dtype=jnp.int32)) % n_group
    chosen = routes[:, None] == experts[None, :, None, None]
    seats = jnp.max(jnp.where(chosen, slot_ids[:, None], -1), axis=-1)
    slots_lane = jnp.pad(seats, ((0, 0), (0, 8 - n_group), (0, PAD - length)), constant_values=-1)
    slots_row = jnp.pad(
        seats.transpose(0, 2, 1), ((0, 0), (0, size - length), (0, 8 - n_group)), constant_values=-1
    )

    def sources(pos, side):
        return pos // (PIECES // 2), (pos % (PIECES // 2), side)

    outs, cores, chips, shards = {}, {}, {}, {}
    places = ((1, 0), (0, 1), (1, 1))

    def quarters(k):
        return [("sum", [(outs[k][0], at), (cores[k], at)]) for at in places]

    def own_quarter(k):
        return ("sum", [(outs[k][0], (0, 0)), (cores[k], (0, 0))] + [(v, ()) for v in chips[k]])

    def send_chips(values):
        return [across(v, offset_of(pos)) for pos, v in zip(range(1, PIECES // 2), values)]

    def send_shard(k, value):
        value = rest_of_replicas(value)
        return along(value, -k) if k else value

    spread_1 = spread(expert_z[1])
    piece, expert_z[1] = join(piece, expert_z[1])
    expert_z[2] = along(piece, 2)
    images, slots_lane, slots_row = join(images, slots_lane, slots_row)
    qkv, att, res, lse, tok, gates, full, small = forward_call(place, images, cotangent, dense, own_table)
    tok, gates, small, piece, spread_1, expert_z = join(tok, gates, small, piece, spread_1, expert_z)
    tables = (slots_lane, gates, small)

    spread_2 = spread(expert_z[2])
    expert_z[3] = along(piece, 3)
    outs[0] = expert_call(0, place, tok, *tables, ((expert_inner, expert_outer), None), spread_1)
    outs, tok, spread_2, expert_z = join(outs, tok, spread_2, expert_z)

    weights = (outs[0][4], across(outs[0][4], 1))
    cores[0] = across(outs[0][1], 1)
    spread_3 = spread(expert_z[3])
    outs[1] = expert_call(1, place, tok, *tables, (weights, sources), spread_2)
    outs, tok, cores, spread_3 = join(outs, tok, cores, spread_3)

    weights = (outs[1][4], across(outs[1][4], 1))
    cores[1] = across(outs[1][1], 1)
    chips[0] = send_chips(blend_call(*quarters(0)))
    outs[2] = expert_call(2, place, tok, *tables, (weights, sources), spread_3)
    outs, tok, cores, chips = join(outs, tok, cores, chips)

    weights = (outs[2][4], across(outs[2][4], 1))
    cores[2] = across(outs[2][1], 1)
    chips[1] = send_chips(blend_call(*quarters(1)))
    outs[3] = expert_call(3, place, tok, *tables, (weights, sources))
    outs, cores, chips, shards = join(outs, cores, chips, shards)

    cores[3] = across(outs[3][1], 1)
    chips[2] = send_chips(blend_call(*quarters(2)))
    pairs = [outs[k][2] for k in range(n_group)]
    biases = [outs[k][3] for k in range(n_group)]
    block_out, gres, gatt, late, shards[0], shards[1], *parts = combine_call(
        (own_quarter(0), own_quarter(1), *quarters(3)), place, cotangent, att, res, tok, slots_row, full, small, pairs, biases
    )
    gres, gatt, late, cores, chips, shards, parts = join(gres, gatt, late, cores, chips, shards, parts)

    chips[3] = send_chips(parts)
    shards[2], = blend_call(own_quarter(2))
    passed = along(rest_of_replicas(shards.pop(2)), 1)
    for k in range(2):
        shards[k] = send_shard(k, shards[k])
    input_grad, keep, send = backward_call(place, images, qkv, lse, gres, gatt, full, small, late, n_group)
    keep, send, chips, shards, passed = join(keep, send, chips, shards, passed)
    if n_replica == PIECES:
        value, = blend_call(("sum", own_quarter(3)[1] + [(passed, ())]))
    else:
        value = plus(rest_of_replicas(*blend_call(own_quarter(3))), passed)
    shards[3] = along(value, 1)

    value = plus(keep, across(send, 1))
    value = plus(value[0], *(across(value[pos], offset_of(pos)) for pos in range(1, PIECES // 2)))
    value = rest_of_replicas(value)
    total, = blend_call(("sum", [(v, ()) for v in shards.values()]))
    value, total = join(value, total)
    own_half = spread(total)
    value = value.reshape((2, 2) + value.shape[1:])
    value = plus(value[:, 0], between(value[:, 1], 1))
    value = plus(value[0], between(value[1], 2))
    value = spread(value)
    other_half = [across(v, 1) for v in own_half]
    grads = finish_call(0, place, own_half)
    grad_inner, grad_outer = finish_call(1, place, other_half, grads)
    value, grad_inner, grad_outer = join(value, grad_inner, grad_outer)
    value = jnp.stack(value)
    value = (value, across(value, 1))
    grad_qkv, grad_proj, grad_router, grad_inner_bias, grad_outer_bias, *rest = finish_dense_call(
        place, value, model, n_group, hidden
    )
    return (
        block_out, input_grad, rest[0], rest[1], grad_qkv, rest[5], grad_proj, rest[2], rest[3], rest[4],
        grad_router.T, grad_inner, grad_inner_bias, grad_outer, grad_outer_bias,
    )


def solution(mesh):
    both = ("replica", "group")
    in_specs = (
        P(both, None, None), P("group"), P("group"), P("group", None), P("group"), P("group", None),
        P("group"), P("group"), P("group"), P("group", None), P("group", None, None), P("group", None),
        P("group", None, None), P("group", None), P(both), P(both, None, None), P(both, None, None),
        P(both, None, None),
    )
    out_specs = (
        P(both, None, None), P(both, None, None), P("group"), P("group"), P("group", None), P("group"),
        P("group", None), P("group"), P("group"), P("group"), P("group", None), P("group", None, None),
        P("group", None), P("group", None, None), P("group", None),
    )
    body = functools.partial(local, n_replica=mesh.shape["replica"], n_group=mesh.shape["group"])
    return jax.shard_map(body, mesh=mesh, in_specs=in_specs, out_specs=out_specs, check_vma=False)
```

```python
import functools
import math

import jax
import jax.numpy as jnp
from jax import lax
from jax.experimental import pallas as pl
from jax.experimental.pallas import tpu as pltpu
from jax.sharding import PartitionSpec as P

HEADS = 8
CAP = 640
NORM_EPS = 1e-06
F32 = jnp.float32
BF16 = jnp.bfloat16
PAD = 256
PIECES = 8
BITS = (2, 4, 1)
WIDE = 512
SMALL = 128
MIB = 1 << 20


def offset_of(position):
    total = 0
    for k, bit in enumerate(BITS):
        total = total + ((position >> k) & 1) * bit
    return total


def dot_nn(a, b):
    return lax.dot_general(a, b, (((1,), (0,)), ((), ())), preferred_element_type=F32)


def dot_nt(a, b):
    return lax.dot_general(a, b, (((1,), (1,)), ((), ())), preferred_element_type=F32)


def dot_tn(a, b):
    return lax.dot_general(a, b, (((0,), (0,)), ((), ())), preferred_element_type=F32)


def norm_parts(values):
    center = values - jnp.mean(values, axis=-1, keepdims=True)
    spread = jnp.mean(center * center, axis=-1, keepdims=True)
    rstd = lax.rsqrt(spread + NORM_EPS)
    return center * rstd, rstd


def gelu_parts(v):
    size = jnp.abs(v)
    density = jnp.exp(v * v * (-0.5)) * 0.3989422804014327
    t = 1.0 / (1.0 + 0.2316418882 * size)
    series = t * (
        0.319381530 + t * (-0.356563782 + t * (1.781477937 + t * (-1.821255978 + t * 1.330274429)))
    )
    tail = density * series
    phi = jnp.where(v < 0, tail, 1.0 - tail)
    return v * phi, phi + v * density


def params(megabytes=62):
    return pltpu.CompilerParams(vmem_limit_bytes=megabytes * MIB)


def cost(microseconds, megabytes):
    return pl.CostEstimate(flops=int(microseconds * 1.1e9), bytes_accessed=int(megabytes * MIB), transcendentals=0)


def padded(length):
    return -(-length // 16) * 16


def pack_kernel(place, qkv, proj, router, *refs):
    *vectors, out, table, lines, turned = refs
    depth = out.shape[0]
    row = pl.multiple_of(place[1] * depth, depth)
    width = qkv.shape[1] + proj.shape[1]
    lines[...] = jnp.zeros_like(lines)
    lines[: router.shape[0], :] = router[...].astype(F32)
    at = 4
    for vector in vectors:
        values = vector[...].astype(F32).reshape(1, -1)
        for c in range(values.shape[1] // 128):
            lines[at : at + 1, :] = values[:, c * 128 : (c + 1) * 128]
            at += 1
        if at == 11:
            at = 12
    turned[...] = lines[...].T
    out[:, : qkv.shape[1]] = qkv[pl.ds(row, depth), :]
    out[:, qkv.shape[1] : width] = proj[pl.ds(row, depth), :]
    out[:, width:] = turned[pl.ds(row, depth), :].astype(BF16)
    table[:, : qkv.shape[1]] = qkv[...]
    table[:, qkv.shape[1] : width] = proj[...]
    table[:, width:] = turned[...].astype(BF16)


def pack_call(place, qkv, proj, router, vectors):
    shard = qkv.shape[0]
    vmem = pl.BlockSpec(memory_space=pltpu.VMEM)
    return pl.pallas_call(
        pack_kernel,
        out_shape=tuple(
            jax.ShapeDtypeStruct((rows, qkv.shape[1] + proj.shape[1] + SMALL), BF16) for rows in (shard // PIECES, shard)
        ),
        in_specs=[pl.BlockSpec(memory_space=pltpu.SMEM)] + [vmem] * (3 + len(vectors)),
        out_specs=(vmem, vmem),
        scratch_shapes=[pltpu.VMEM((SMALL, shard), F32), pltpu.VMEM((shard, SMALL), F32)],
        cost_estimate=cost(2, 1),
        name="pack_dense",
    )(place, qkv, proj, router.T, *vectors)


def cut_kernel(place, inner, outer, out):
    out[0] = inner[0].T
    out[1] = outer[0]


def cut_call(place, inner, outer):
    _, model, hidden = inner.shape
    block = hidden // PIECES
    return pl.pallas_call(
        cut_kernel,
        out_shape=jax.ShapeDtypeStruct((2, block, model), BF16),
        grid_spec=pltpu.PrefetchScalarGridSpec(
            num_scalar_prefetch=1,
            grid=(1,),
            in_specs=[
                pl.BlockSpec((1, model, block), lambda i, s: (0, 0, s[1])),
                pl.BlockSpec((1, block, model), lambda i, s: (0, s[1], 0)),
            ],
            out_specs=pl.BlockSpec((2, block, model), lambda i, s: (0, 0, 0)),
        ),
        compiler_params=params(),
        cost_estimate=cost(2, 1),
        name="cut_own",
    )(place, inner, outer)


def forward_kernel(
    place, images, cot, *refs,
):
    dense = refs[:PIECES]
    own, qkv_out, att_out, res_out, lse_out, tok_out, gates_out, full_out, small_out, rows = refs[PIECES:]
    model = images.shape[2]
    length = images.shape[1]
    size = rows.shape[0]
    parts = dense[0].shape[0] + 1
    depth = dense[0].shape[1]

    @pl.when(pl.program_id(0) == 0)
    def _():
        z, r = place[0], place[1]
        for pos in range(PIECES):
            for d in range(1, parts):
                owner = lax.rem(z + parts - d, parts) * PIECES
                row = pl.multiple_of((owner + jnp.bitwise_xor(r, offset_of(pos))) * depth, depth)
                full_out[pl.ds(row, depth), :] = dense[pos][d - 1]
        full_out[pl.ds(pl.multiple_of(z * PIECES * depth, depth), PIECES * depth), :] = own[...]
        small_out[...] = full_out[:, 4 * model :].astype(F32).T
        rows[...] = jnp.zeros_like(rows)

    def vector(row):
        return small_out[row : row + 1, :]

    rows[:length, :] = images[0].astype(F32)
    x = rows[...]
    xhat, _ = norm_parts(x)
    normed = (xhat * vector(4) + vector(5)).astype(BF16)
    projected = dot_nn(normed, full_out[:, : 3 * model])
    bias_parts = []
    for part in range(parts):
        lanes = slice(part * 128, part * 128 + 128)
        bias_parts += [small_out[9:10, lanes], small_out[10:11, lanes]]
    pair = jnp.concatenate(bias_parts, axis=1)
    qkv_out[0, :, :model] = (projected[:, :model] + pair[:, :model]).astype(BF16)
    qkv_out[0, :, model : 2 * model] = projected[:, model : 2 * model].astype(BF16)
    qkv_out[0, :, 2 * model :] = (projected[:, 2 * model :] + pair[:, model:]).astype(BF16)
    qkv_out[0, length:, :] = jnp.zeros((size - length, 3 * model), BF16)

    head = model // HEADS
    first = lax.broadcasted_iota(jnp.int32, (1, 2 * head), 1) < head
    real = lax.broadcasted_iota(jnp.int32, (1, size), 1) < length
    column = lax.broadcasted_iota(jnp.int32, (size, 128), 1)
    scale = 1.0 / math.sqrt(head)
    lse = jnp.zeros((size, 128), F32)
    attended = []
    for two in range(HEADS // 2):
        lanes = lambda start: slice(start + two * 2 * head, start + (two + 1) * 2 * head)
        q2, k2, v2 = (qkv_out[0, :, lanes(s * model)] for s in range(3))
        zero = jnp.zeros_like(q2)
        stack = jnp.concatenate([jnp.where(first, q2, zero), jnp.where(first, zero, q2)], axis=0)
        scores = jnp.where(real, dot_nt(stack, k2) * scale, -1e30)
        peak = jnp.max(scores, axis=-1, keepdims=True)
        e = jnp.exp(scores - peak)
        total = jnp.sum(e, axis=-1, keepdims=True)
        probs = (e * (1.0 / total)).astype(BF16)
        both = dot_nn(probs, v2)
        attended.append(jnp.where(first, both[:size], both[size:]).astype(BF16))
        logs = peak + jnp.log(total)
        lse = jnp.where(column == 2 * two, logs[:size], lse)
        lse = jnp.where(column == 2 * two + 1, logs[size:], lse)
    lse_out[0] = lse
    attended = jnp.concatenate(attended, axis=1)
    att_out[0] = attended
    residual = x + (dot_nn(attended, full_out[:, 3 * model : 4 * model]) + vector(6))
    res_out[0] = residual
    xhat2, _ = norm_parts(residual)
    normed2 = (xhat2 * vector(7) + vector(8)).astype(BF16)
    tail = length // 16 * 16
    tok_out[tail:, :] = jnp.zeros((PAD - tail, 2 * model), BF16)
    tok_out[:size, :model] = normed2
    tok_out[:length, model:] = cot[0]
    logits = dot_nt(small_out[0:8, :].astype(BF16), tok_out[:, :model])
    experts = lax.broadcasted_iota(jnp.int32, logits.shape, 0) < parts
    logits = jnp.where(experts, logits, -jnp.inf)
    e = jnp.exp(logits - jnp.max(logits, axis=0, keepdims=True))
    gates_out[0] = e / jnp.sum(e, axis=0, keepdims=True)


def whole(a):
    return pl.BlockSpec(a.shape, lambda i, *_: (0,) * len(a.shape))


def image(*dims):
    return pl.BlockSpec((1,) + dims, lambda i, *_: (i, 0, 0))


def forward_call(place, images, cot, dense, own):
    count, length, model = images.shape
    size = padded(length)
    outs = (
        jax.ShapeDtypeStruct((count, size, 3 * model), BF16),
        jax.ShapeDtypeStruct((count, size, model), BF16),
        jax.ShapeDtypeStruct((count, size, model), F32),
        jax.ShapeDtypeStruct((count, size, 128), F32),
        jax.ShapeDtypeStruct((count * PAD, 2 * model), BF16),
        jax.ShapeDtypeStruct((count, 8, PAD), F32),
        jax.ShapeDtypeStruct((model, 4 * model + SMALL), BF16),
        jax.ShapeDtypeStruct((SMALL, model), F32),
    )
    return pl.pallas_call(
        forward_kernel,
        out_shape=outs,
        grid_spec=pltpu.PrefetchScalarGridSpec(
            num_scalar_prefetch=1,
            grid=(count,),
            in_specs=[image(length, model), image(length, model)] + [whole(d) for d in (*dense, own)],
            out_specs=[
                image(size, 3 * model), image(size, model), image(size, model), image(size, 128),
                pl.BlockSpec((PAD, 2 * model), lambda i, *_: (i, 0)),
                image(8, PAD), whole(outs[6]), whole(outs[7]),
            ],
            scratch_shapes=[pltpu.VMEM((size, model), F32)],
        ),
        compiler_params=params(),
        cost_estimate=cost(12, 12),
        name="attention_forward",
    )(place, images, cot, *dense, own)


def blend_loads(jobs, arrays, loaded, sems):
    copies = []
    for _, terms in jobs:
        for which, index in terms:
            spot = len(copies)
            source = arrays[which].at[index] if index else arrays[which]
            copies.append(pltpu.make_async_copy(source, loaded.at[spot], sems.at[spot]))
    return copies


def blend_stores(jobs, outs, loaded, summed, sems):
    copies, spot, sums = [], 0, 0
    for out, (kind, terms) in zip(outs, jobs):
        if kind == "collect":
            pairs = [(loaded.at[spot + k], out.at[k]) for k in range(len(terms))]
        else:
            pairs = [(summed.at[sums], out)]
            sums += 1
        spot += len(terms)
        copies.append([pltpu.make_async_copy(a, b, sems.at[sum(map(len, copies)) + k]) for k, (a, b) in enumerate(pairs)])
    return copies


def blend_work(jobs, loads, stores, loaded, summed):
    spot = sums = 0
    for (kind, terms), copies in zip(jobs, stores):
        total = None
        for k in range(len(terms)):
            loads[spot].wait()
            if kind == "collect":
                copies[k].start()
            else:
                value = loaded[spot].astype(F32)
                total = value if total is None else total + value
            spot += 1
        if kind == "sum":
            summed[sums] = total.astype(BF16)
            copies[0].start()
            sums += 1


def blend_kernel(*refs, jobs, count_in):
    arrays = refs[:count_in]
    outs = refs[count_in : count_in + len(jobs)]
    loaded, summed, in_sems, out_sems = refs[count_in + len(jobs) :]
    loads = blend_loads(jobs, arrays, loaded, in_sems)
    for copy in loads:
        copy.start()
    stores = blend_stores(jobs, outs, loaded, summed, out_sems)
    blend_work(jobs, loads, stores, loaded, summed)
    for copies in stores:
        for copy in copies:
            copy.wait()


def blend_plan(jobs):
    arrays, plan, shapes = [], [], []
    for kind, terms in jobs:
        listed = []
        for array, index in terms:
            known = [k for k, a in enumerate(arrays) if a is array]
            if not known:
                arrays.append(array)
                known = [len(arrays) - 1]
            listed.append((known[0], index))
        unit = terms[0][0].shape[len(terms[0][1]) :]
        shapes.append(jax.ShapeDtypeStruct(((len(terms),) if kind == "collect" else ()) + unit, BF16))
        plan.append((kind, tuple(listed)))
    units = sum(len(terms) for _, terms in plan)
    sums = sum(kind == "sum" for kind, _ in plan)
    stores = sums + sum(len(terms) for kind, terms in plan if kind == "collect")
    scratch = [
        pltpu.VMEM((units,) + unit, BF16),
        pltpu.VMEM((max(sums, 1),) + unit, BF16),
        pltpu.SemaphoreType.DMA((units,)),
        pltpu.SemaphoreType.DMA((stores,)),
    ]
    return arrays, tuple(plan), shapes, scratch


def blend_call(*jobs):
    arrays, plan, shapes, scratch = blend_plan(jobs)
    anywhere = pl.BlockSpec(memory_space=pl.ANY)
    return pl.pallas_call(
        functools.partial(blend_kernel, jobs=plan, count_in=len(arrays)),
        out_shape=tuple(shapes),
        in_specs=[anywhere] * len(arrays),
        out_specs=(anywhere,) * len(shapes),
        scratch_shapes=scratch,
        compiler_params=params(),
        cost_estimate=cost(3, 3),
        name="blend",
    )(*arrays)


def expert_kernel(place, slots, gates, small, tok, *refs, turn, sources, count_in, count_side):
    arrays = refs[:count_in]
    beside = refs[count_in : count_in + count_side]
    count_in += count_side
    keep, send, pair_out, bias_out = refs[count_in : count_in + 4]
    if count_side:
        collected, passing, side_sems = refs[count_in + 4], refs[-2], refs[-1]
        refs = refs[: count_in + 4] + refs[count_in + 5 : -2]
    tokens, onehot, buffer, grad_slots, rows, back, mine, inners, outers, staged, token_sem, in_sems, out_sems = (
        refs[count_in + 4 :]
    )
    local = sources is None
    count = slots.shape[0]
    model = buffer.shape[1]
    block = outers.shape[1]
    per = staged.shape[1]
    steps = staged.shape[0]

    token_copy = pltpu.make_async_copy(tok, tokens, token_sem)
    token_copy.start()
    loads = []
    for pos in range(PIECES):
        for side, matrices in enumerate((inners, outers)):
            if local:
                start = pl.multiple_of(jnp.bitwise_xor(place[1], offset_of(pos)) * block, block)
                source = arrays[1].at[0, pl.ds(start, block)] if side else arrays[0].at[0, :, pl.ds(start, block)]
            else:
                which, at = sources(pos, side)
                source = arrays[which].at[at]
            loads.append(pltpu.make_async_copy(source, matrices.at[pos], in_sems.at[pos, side]))

    expert = lax.rem(place[0] + place[3] - turn, place[3])
    lanes = pl.ds(pl.multiple_of(expert * 128, 128), 128)
    mine[...] = small[:, lanes]
    where = lax.broadcasted_iota(jnp.int32, (CAP, PAD), 0)
    gate = jnp.zeros((CAP, 128), F32)
    for b in range(count):
        mask = where == slots[b, turn : turn + 1, :]
        onehot[:, b * PAD : (b + 1) * PAD] = mask.astype(F32).astype(BF16)
        weighted = jnp.where(mask, gates[b, pl.ds(expert, 1), :], 0.0)
        gate = gate + weighted[:, :128] + weighted[:, 128:]
    gate = jnp.sum(gate, axis=1, keepdims=True)
    outer_bias = jnp.concatenate([mine[28 + c : 29 + c, :] for c in range(model // 128)], axis=1)
    token_copy.wait()
    for copy in loads:
        copy.start()
    side_loads = [pltpu.make_async_copy(b, passing.at[k], side_sems.at[0, k]) for k, b in enumerate(beside)]
    side_stores = [pltpu.make_async_copy(passing.at[k], collected.at[k], side_sems.at[1, k]) for k in range(count_side)]
    for copy in side_loads:
        copy.start()
    buffer[...] = dot_nn(onehot[...], tokens[:, :model]).astype(BF16)
    grads = (dot_nn(onehot[...], tokens[:, model:]) * gate).astype(BF16)
    grad_slots[...] = grads
    sums = jnp.sum(grads.astype(F32), axis=0, keepdims=True)
    for c in range(model // 128):
        bias_out[16 + c : 17 + c, :] = sums[:, c * 128 : (c + 1) * 128]
    bias_out[20:32, :] = jnp.zeros((12, 128), F32)

    def first_products(i):
        for copy in loads[2 * i * per : 2 * (i + 1) * per]:
            copy.wait()
        buf, gs = buffer[...], grad_slots[...]
        here = slice(i * per, (i + 1) * per)
        lines = [
            jnp.bitwise_xor(place[1], offset_of(pos)) * (block // 128) + c
            for pos in range(here.start, here.stop)
            for c in range(block // 128)
        ]
        bias = jnp.concatenate([mine[pl.ds(12 + line, 1), :] for line in lines], axis=1)
        if local:
            hidden = jnp.concatenate([dot_nn(buf, inners[pos]) for pos in range(here.start, here.stop)], axis=1)
        else:
            hidden = dot_nt(buf, inners[here].reshape(per * block, model))
        return hidden + bias, dot_nt(gs, outers[here].reshape(per * block, model)), lines

    stores = []
    for i in range(steps):
        hidden, grad_active, lines = first_products(i)
        if i == 1:
            for load, store in zip(side_loads, side_stores):
                load.wait()
                store.start()
        here = slice(i * per, (i + 1) * per)
        active, slope = gelu_parts(hidden)
        active = active.astype(BF16)
        grad_low = (grad_active * slope).astype(BF16)
        sums = jnp.sum(grad_low.astype(F32), axis=0, keepdims=True)
        for k, line in enumerate(lines):
            bias_out[pl.ds(line, 1), :] = sums[:, k * 128 : (k + 1) * 128]
        staged[i, :, 0] = dot_tn(grad_low, buffer[...]).astype(BF16).reshape(per, block, model)
        staged[i, :, 1] = dot_tn(active, grad_slots[...]).astype(BF16).reshape(per, block, model)
        out = keep if i < steps // 2 else send
        stores.append(pltpu.make_async_copy(staged.at[i], out.at[:, i % (steps // 2)], out_sems.at[i]))
        stores[-1].start()
        new_rows = dot_nn(active, outers[here].reshape(per * block, model))
        if local:
            new_back = sum(
                dot_nt(grad_low[:, j * block : (j + 1) * block], inners[i * per + j]) for j in range(per)
            )
        else:
            new_back = dot_nn(grad_low, inners[here].reshape(per * block, model))
        rows[...] = new_rows + (outer_bias if i == 0 else rows[...])
        back[...] = new_back if i == 0 else new_back + back[...]
    pair_out[:, :model] = rows[...].astype(BF16)
    pair_out[:, model:] = back[...].astype(BF16)
    for copy in stores + side_stores:
        copy.wait()


def expert_call(turn, place, tok, slots, gates, small, weights, beside=()):
    arrays, sources = weights
    model = tok.shape[1] // 2
    count = slots.shape[0]
    block = arrays[1].shape[1] // PIECES if sources is None else arrays[0].shape[-2]
    per = WIDE // block
    steps = PIECES // per
    vmem = pl.BlockSpec(memory_space=pltpu.VMEM)
    anywhere = pl.BlockSpec(memory_space=pl.ANY)
    half = jax.ShapeDtypeStruct((2, 2, 2, block, model), BF16)
    return pl.pallas_call(
        functools.partial(expert_kernel, turn=turn, sources=sources, count_in=len(arrays), count_side=len(beside)),
        out_shape=(
            half,
            half,
            jax.ShapeDtypeStruct((CAP, 2 * model), BF16),
            jax.ShapeDtypeStruct((32, 128), F32),
        )
        + tuple(jax.ShapeDtypeStruct((len(beside),) + b.shape, BF16) for b in beside[:1]),
        in_specs=[pl.BlockSpec(memory_space=pltpu.SMEM), vmem, vmem, vmem, anywhere]
        + [anywhere] * (len(arrays) + len(beside)),
        out_specs=[anywhere, anywhere, vmem, vmem] + [anywhere] * len(beside[:1]),
        scratch_shapes=[
            pltpu.VMEM(tok.shape, BF16),
            pltpu.VMEM((CAP, count * PAD), BF16),
            pltpu.VMEM((CAP, model), BF16),
            pltpu.VMEM((CAP, model), BF16),
            pltpu.VMEM((CAP, model), F32),
            pltpu.VMEM((CAP, model), F32),
            pltpu.VMEM((SMALL, 128), F32),
            pltpu.VMEM((PIECES, model, block) if sources is None else (PIECES, block, model), BF16),
            pltpu.VMEM((PIECES, block, model), BF16),
            pltpu.VMEM((steps, per, 2, block, model), BF16),
            pltpu.SemaphoreType.DMA(()),
            pltpu.SemaphoreType.DMA((PIECES, 2)),
            pltpu.SemaphoreType.DMA((steps,)),
        ]
        + [pltpu.VMEM((len(beside),) + b.shape, BF16) for b in beside[:1]]
        + [pltpu.SemaphoreType.DMA((2, len(beside))) for _ in beside[:1]],
        compiler_params=params(),
        cost_estimate=cost(18, 14),
        name="expert",
    )(place, slots, gates, small, tok, *arrays, *beside)


def norm_back(inner, xhat, rstd):
    return rstd * (
        inner - jnp.mean(inner, axis=-1, keepdims=True) - xhat * jnp.mean(inner * xhat, axis=-1, keepdims=True)
    )


def combine_kernel(place, *refs, turns, jobs, count_in):
    cot, att, res, tok, slots, full, small = refs[:7]
    pairs = refs[7 : 7 + turns]
    biases = refs[7 + turns : 7 + 2 * turns]
    arrays = refs[7 + 2 * turns : 7 + 2 * turns + count_in]
    block_out, gres_out, gatt_out, late_out, *side_outs = refs[7 + 2 * turns + count_in : -8]
    cots, acc_proj, acc_router, acc_small, loaded, summed, in_sems, out_sems = refs[-8:]
    b = pl.program_id(0)
    loads = blend_loads(jobs, arrays, loaded, in_sems)
    stores = blend_stores(jobs, side_outs, loaded, summed, out_sems)

    @pl.when(b == 0)
    def _():
        for copy in loads:
            copy.start()

    @pl.when(b == 1)
    def _():
        blend_work(jobs, loads, stores, loaded, summed)

    length, model = cot.shape[1:]
    size = cots.shape[0]
    parts = turns

    @pl.when(b == 0)
    def _():
        cots[...] = jnp.zeros_like(cots)
        for acc in (acc_proj, acc_router, acc_small):
            acc[...] = jnp.zeros_like(acc)

    def vector(row):
        return small[row : row + 1, :]

    def add_row(row, values):
        acc_small[row : row + 1, :] += jnp.sum(values, axis=0, keepdims=True)

    live = (b < place[2]).astype(F32)
    cots[:length, :] = cot[0].astype(F32) * live
    grad_out = cots[...]
    residual = res[0]
    xhat2, rstd2 = norm_parts(residual)
    normed2 = tok[:size, :model]
    router = full[:, 4 * model :]

    logits = dot_nn(normed2, router)
    lane = lax.broadcasted_iota(jnp.int32, logits.shape, 1)
    logits = jnp.where(lane < parts, logits, -jnp.inf)
    e = jnp.exp(logits - jnp.max(logits, axis=-1, keepdims=True))
    probs = e / jnp.sum(e, axis=-1, keepdims=True)

    seat = lax.broadcasted_iota(jnp.int32, (size, CAP), 1)
    mixture = None
    grad_n2 = None
    grad_probs = jnp.zeros_like(probs)
    for j in range(turns):
        expert = lax.rem(place[0] + parts - j, parts)
        mask = (slots[0][:, j : j + 1] == seat).astype(F32).astype(BF16)
        both = dot_nn(mask, pairs[j][...])
        picked = both[:, :model]
        gate = jnp.sum(jnp.where(lane == expert, probs, 0.0), axis=-1, keepdims=True)
        mixture = gate * picked if mixture is None else mixture + gate * picked
        grad_gate = jnp.sum(grad_out * picked, axis=-1, keepdims=True)
        grad_probs = jnp.where(lane == expert, grad_gate, grad_probs)
        grad_n2 = both[:, model:] if grad_n2 is None else grad_n2 + both[:, model:]
    block_out[0] = ((residual + mixture) * live).astype(BF16)[:length]
    grad_logits = probs * (grad_probs - jnp.sum(probs * grad_probs, axis=-1, keepdims=True))
    grad_logits = grad_logits.astype(BF16)
    grad_n2 = grad_n2 + dot_nt(grad_logits, router)
    acc_router[...] += dot_tn(normed2, grad_logits)

    add_row(7, grad_n2 * xhat2)
    add_row(8, grad_n2)
    grad_res = grad_out + norm_back(grad_n2 * vector(7), xhat2, rstd2)
    gres_out[0] = grad_res
    branch = grad_res.astype(BF16)
    add_row(6, branch.astype(F32))
    acc_proj[...] += dot_tn(att[0], branch)
    gatt_out[0] = dot_nt(branch, full[:, 3 * model : 4 * model]).astype(BF16)

    @pl.when(b == pl.num_programs(0) - 1)
    def _():
        for copies in stores:
            for copy in copies:
                copy.wait()
        for j in range(turns):
            expert = lax.rem(place[0] + parts - j, parts)
            acc_small[12:32, pl.ds(pl.multiple_of(expert * 128, 128), 128)] = biases[j][0:20, :]
        late_out[:, :model] = acc_proj[...].astype(BF16)
        late_out[:, model:] = (acc_router[...] + acc_small[...].T).astype(BF16)


def combine_call(jobs, place, cot, att, res, tok, slots, full, small, pairs, biases):
    count, length, model = cot.shape
    size = att.shape[1]
    turns = len(pairs)
    arrays, plan, shapes, scratch = blend_plan(jobs)
    anywhere = pl.BlockSpec(memory_space=pl.ANY)
    outs = (
        jax.ShapeDtypeStruct((count, length, model), BF16),
        jax.ShapeDtypeStruct((count, size, model), F32),
        jax.ShapeDtypeStruct((count, size, model), BF16),
        jax.ShapeDtypeStruct((model, model + SMALL), BF16),
    )
    return pl.pallas_call(
        functools.partial(combine_kernel, turns=turns, jobs=plan, count_in=len(arrays)),
        out_shape=outs + tuple(shapes),
        grid_spec=pltpu.PrefetchScalarGridSpec(
            num_scalar_prefetch=1,
            grid=(count,),
            in_specs=[
                image(length, model), image(size, model), image(size, model),
                pl.BlockSpec((PAD, 2 * model), lambda i, *_: (i, 0)),
                image(size, slots.shape[2]), whole(full), whole(small),
            ] + [whole(a) for a in (*pairs, *biases)] + [anywhere] * len(arrays),
            out_specs=[image(length, model), image(size, model), image(size, model), whole(outs[3])] + [anywhere] * len(shapes),
            scratch_shapes=[
                pltpu.VMEM((size, model), F32),
                pltpu.VMEM((model, model), F32),
                pltpu.VMEM((model, SMALL), F32),
                pltpu.VMEM((SMALL, model), F32),
            ] + scratch,
        ),
        compiler_params=params(),
        cost_estimate=cost(18, 14),
        name="combine",
    )(place, cot, att, res, tok, slots, full, small, *pairs, *biases, *arrays)


def backward_kernel(
    place, images, qkv, lse, gres, gatt, full, small, late, input_grad, keep, send, rows, acc_qkv, acc_small,
):
    parts = keep.shape[1]
    b = pl.program_id(0)
    length, model = images.shape[1:]
    size = rows.shape[0]

    @pl.when(b == 0)
    def _():
        rows[...] = jnp.zeros_like(rows)
        acc_qkv[...] = jnp.zeros_like(acc_qkv)
        acc_small[...] = jnp.zeros_like(acc_small)

    def vector(row):
        return small[row : row + 1, :]

    def add_row(row, values):
        acc_small[row : row + 1, :] += jnp.sum(values, axis=0, keepdims=True)

    head = model // HEADS
    first = lax.broadcasted_iota(jnp.int32, (1, 2 * head), 1) < head
    real = lax.broadcasted_iota(jnp.int32, (1, size), 1) < length
    scale = 1.0 / math.sqrt(head)
    grads = [[], [], []]
    for two in range(HEADS // 2):
        lanes = lambda start: slice(start + two * 2 * head, start + (two + 1) * 2 * head)
        q2, k2, v2 = (qkv[0, :, lanes(s * model)] for s in range(3))
        g2 = gatt[0, :, lanes(0)]
        zero = jnp.zeros_like(q2)
        stack = lambda t: jnp.concatenate([jnp.where(first, t, zero), jnp.where(first, zero, t)], axis=0)
        merge = lambda t: jnp.where(first, t[:size], t[size:])
        qs, gs = stack(q2), stack(g2)
        logs = jnp.concatenate([lse[0, :, 2 * two : 2 * two + 1], lse[0, :, 2 * two + 1 : 2 * two + 2]], axis=0)
        weights = jnp.where(real, jnp.exp(dot_nt(qs, k2) * scale - logs), 0.0)
        grad_weights = dot_nt(gs, v2)
        grad_scores = weights * (grad_weights - jnp.sum(grad_weights * weights, axis=-1, keepdims=True))
        grad_scores = grad_scores.astype(BF16)
        grads[0].append((merge(dot_nn(grad_scores, k2)) * scale).astype(BF16))
        grads[1].append((dot_tn(grad_scores, qs) * scale).astype(BF16))
        grads[2].append(dot_tn(weights.astype(BF16), gs).astype(BF16))
    grad_projected = jnp.concatenate(grads[0] + grads[1] + grads[2], axis=1)
    rows[:length, :] = images[0].astype(F32)
    xhat1, rstd1 = norm_parts(rows[...])
    normed = (xhat1 * vector(4) + vector(5)).astype(BF16)
    acc_qkv[:, : 3 * model] += dot_tn(normed, grad_projected)
    grad_normed = dot_nt(grad_projected, full[:, : 3 * model])
    add_row(4, grad_normed * xhat1)
    add_row(5, grad_normed)
    add_row(32, grad_projected[:, :model].astype(F32))
    add_row(33, grad_projected[:, 2 * model :].astype(F32))
    input_grad[0] = (gres[0] + norm_back(grad_normed * vector(4), xhat1, rstd1))[:length]

    @pl.when(b == pl.num_programs(0) - 1)
    def _():
        for part in range(parts):
            for k in range(2):
                start = (part * 2 + k) * 128
                source = 32 + start // model
                acc_small[9 + k : 10 + k, part * 128 : part * 128 + 128] = acc_small[
                    source : source + 1, start % model : start % model + 128
                ]
        acc_small[32:34, :] = jnp.zeros((2, model), F32)
        acc_qkv[:, 3 * model :] = acc_small[...].T + late[:, model:].astype(F32)
        depth = keep.shape[2]
        for pos in range(PIECES):
            for d in range(parts):
                owner = jnp.bitwise_xor(place[0], d) * PIECES
                row = pl.multiple_of((owner + jnp.bitwise_xor(place[1], offset_of(pos))) * depth, depth)
                out = keep if pos < PIECES // 2 else send
                spot = pos % (PIECES // 2)
                out[spot, d, :, : 3 * model] = acc_qkv[pl.ds(row, depth), : 3 * model].astype(BF16)
                out[spot, d, :, 3 * model : 4 * model] = late[pl.ds(row, depth), :model]
                out[spot, d, :, 4 * model :] = acc_qkv[pl.ds(row, depth), 3 * model :].astype(BF16)


def backward_call(place, images, qkv, lse, gres, gatt, full, small, late, parts):
    count, length, model = images.shape
    size = qkv.shape[1]
    half = jax.ShapeDtypeStruct((PIECES // 2, parts, model // (parts * PIECES), 4 * model + SMALL), BF16)
    outs = (jax.ShapeDtypeStruct((count, length, model), F32), half, half)
    return pl.pallas_call(
        backward_kernel,
        out_shape=outs,
        grid_spec=pltpu.PrefetchScalarGridSpec(
            num_scalar_prefetch=1,
            grid=(count,),
            in_specs=[
                image(length, model), image(size, 3 * model), image(size, 128), image(size, model),
                image(size, model), whole(full), whole(small), whole(late),
            ],
            out_specs=[image(length, model), whole(half), whole(half)],
            scratch_shapes=[
                pltpu.VMEM((size, model), F32),
                pltpu.VMEM((model, 3 * model + SMALL), F32),
                pltpu.VMEM((SMALL, model), F32),
            ],
        ),
        compiler_params=params(),
        cost_estimate=cost(22, 14),
        name="attention_backward",
    )(place, images, qkv, lse, gres, gatt, full, small, late)


def finish_kernel(place, *refs, half):
    pieces = refs[: PIECES // 2]
    inner_out, outer_out, loaded, inner, outer, in_sems, out_sems = refs[-7:]
    block = outer.shape[1]
    loads = [pltpu.make_async_copy(p, loaded.at[k], in_sems.at[k]) for k, p in enumerate(pieces)]
    for copy in loads:
        copy.start()
    stores = []
    for k, copy in enumerate(loads):
        copy.wait()
        piece = jnp.bitwise_xor(place[1], offset_of(k + half * PIECES // 2))
        spot = pl.ds(pl.multiple_of(piece * block, block), block)
        inner[k] = loaded[k, 0].astype(F32).T
        outer[k] = loaded[k, 1].astype(F32)
        for side, (source, target) in enumerate(((inner.at[k], inner_out.at[0, :, spot]), (outer.at[k], outer_out.at[0, spot]))):
            stores.append(pltpu.make_async_copy(source, target, out_sems.at[k, side]))
            stores[-1].start()
    for copy in stores:
        copy.wait()


def finish_call(half, place, pieces, outs=()):
    _, block, model = pieces[0].shape
    count = len(pieces)
    anywhere = pl.BlockSpec(memory_space=pl.ANY)
    return pl.pallas_call(
        functools.partial(finish_kernel, half=half),
        out_shape=(
            jax.ShapeDtypeStruct((1, model, PIECES * block), F32),
            jax.ShapeDtypeStruct((1, PIECES * block, model), F32),
        ),
        in_specs=[pl.BlockSpec(memory_space=pltpu.SMEM)] + [anywhere] * (count + len(outs)),
        out_specs=(anywhere, anywhere),
        scratch_shapes=[
            pltpu.VMEM((count, 2, block, model), BF16),
            pltpu.VMEM((count, model, block), F32),
            pltpu.VMEM((count, block, model), F32),
            pltpu.SemaphoreType.DMA((count,)),
            pltpu.SemaphoreType.DMA((count, 2)),
        ],
        input_output_aliases={1 + count + k: k for k in range(len(outs))},
        compiler_params=params(),
        cost_estimate=cost(4, 6),
        name="finish_experts",
    )(place, *pieces, *outs)


def finish_dense_kernel(place, *refs):
    pieces = refs[:2]
    qkv_out, proj_out, router_out, inner_out, outer_out, *vector_outs, pair_out, table = refs[2:]
    model = proj_out.shape[1]
    depth = pieces[0].shape[1]
    for pos in range(PIECES):
        row = pl.multiple_of(jnp.bitwise_xor(place[1], offset_of(pos)) * depth, depth)
        block = pieces[pos // (PIECES // 2)][pos % (PIECES // 2)].astype(F32)
        qkv_out[pl.ds(row, depth), :] = block[:, : 3 * model]
        proj_out[pl.ds(row, depth), :] = block[:, 3 * model : 4 * model]
        table[pl.ds(row, depth), :] = block[:, 4 * model :]
    table[...] = table[...].T
    router_out[...] = table[: router_out.shape[0], :]
    for k, out in enumerate(vector_outs):
        out[...] = table[4 + k, :]
    for k in range(2):
        pair_out[pl.ds(k * 128, 128)] = table[9 + k, :]
    for c in range(inner_out.shape[1] // 128):
        inner_out[:, c * 128 : (c + 1) * 128] = table[12 + c : 13 + c, :]
    for c in range(outer_out.shape[1] // 128):
        outer_out[:, c * 128 : (c + 1) * 128] = table[28 + c : 29 + c, :]


def finish_dense_call(place, pieces, model, parts, hidden):
    rows = pieces[0].shape[1] * PIECES
    vmem = pl.BlockSpec(memory_space=pltpu.VMEM)
    return pl.pallas_call(
        finish_dense_kernel,
        out_shape=(
            jax.ShapeDtypeStruct((rows, 3 * model), F32),
            jax.ShapeDtypeStruct((rows, model), F32),
            jax.ShapeDtypeStruct((parts, rows), F32),
            jax.ShapeDtypeStruct((1, hidden), F32),
            jax.ShapeDtypeStruct((1, model), F32),
        )
        + tuple(jax.ShapeDtypeStruct((n,), F32) for n in (rows, rows, rows, rows, rows, 2 * rows)),
        in_specs=[pl.BlockSpec(memory_space=pltpu.SMEM)] + [vmem] * 2,
        scratch_shapes=[pltpu.VMEM((rows, SMALL), F32)],
        cost_estimate=cost(2, 2),
        name="finish_dense",
    )(place, *pieces)


def join(*values):
    return lax.optimization_barrier(values)


def local(
    images, attn_norm_gain, attn_norm_bias, qkv_weight, query_value_bias, proj_weight, proj_bias,
    moe_norm_gain, moe_norm_bias, router_weight, expert_inner, expert_inner_bias, expert_outer,
    expert_outer_bias, live_count, routes, slot_ids, cotangent, *, n_replica, n_group,
):
    count, length, model = images.shape
    shard = qkv_weight.shape[0]
    hidden = expert_inner.shape[2]
    size = padded(length)
    z = lax.axis_index("group").astype(jnp.int32)
    r = lax.axis_index("replica").astype(jnp.int32) & (PIECES - 1)
    place = jnp.stack([z, r, live_count[0].astype(jnp.int32), jnp.int32(n_group)])

    def across(value, bit):
        return lax.ppermute(value, "replica", [(i, i ^ bit) for i in range(n_replica)])

    def along(value, shift):
        return lax.ppermute(value, "group", [(i, (i + shift) % n_group) for i in range(n_group)])

    def between(value, bit):
        return lax.ppermute(value, "group", [(i, i ^ bit) for i in range(n_group)])

    def plus(*values):
        return sum(v.astype(F32) for v in values).astype(BF16)

    def both(value, bit):
        return jnp.concatenate([value, across(value, bit)], axis=0)

    def spread(value):
        return [value] + [across(value, offset_of(pos)) for pos in range(1, PIECES // 2)]

    def rest_of_replicas(value):
        bit = PIECES
        while bit < n_replica:
            value = plus(value, across(value, bit))
            bit *= 2
        return value

    shifts = list(range(1, n_group))

    vectors = (attn_norm_gain, attn_norm_bias, proj_bias, moe_norm_gain, moe_norm_bias, query_value_bias)
    mine, own_table = pack_call(
        place, qkv_weight, proj_weight, router_weight, vectors + (expert_inner_bias, expert_outer_bias)
    )
    dense_z = {d: along(mine, d) for d in shifts}

    piece = cut_call(place, expert_inner, expert_outer)
    piece, dense_z = join(piece, dense_z)
    expert_z = {1: along(piece, 1)}
    dense = spread(jnp.stack([dense_z[d] for d in shifts]))
    dense = dense + [across(v, 1) for v in dense]

    experts = (z + n_group - jnp.arange(n_group, dtype=jnp.int32)) % n_group
    chosen = routes[:, None] == experts[None, :, None, None]
    seats = jnp.max(jnp.where(chosen, slot_ids[:, None], -1), axis=-1)
    slots_lane = jnp.pad(seats, ((0, 0), (0, 8 - n_group), (0, PAD - length)), constant_values=-1)
    slots_row = jnp.pad(
        seats.transpose(0, 2, 1), ((0, 0), (0, size - length), (0, 8 - n_group)), constant_values=-1
    )

    def sources(pos, side):
        return pos // (PIECES // 2), (pos % (PIECES // 2), side)

    outs, cores, chips, shards = {}, {}, {}, {}
    places = ((1, 0), (0, 1), (1, 1))

    def quarters(k):
        return [("sum", [(outs[k][0], at), (cores[k], at)]) for at in places]

    def own_quarter(k):
        return ("sum", [(outs[k][0], (0, 0)), (cores[k], (0, 0))] + [(v, ()) for v in chips[k]])

    def send_chips(values):
        return [across(v, offset_of(pos)) for pos, v in zip(range(1, PIECES // 2), values)]

    def send_shard(k, value):
        value = rest_of_replicas(value)
        return along(value, -k) if k else value

    spread_1 = spread(expert_z[1])
    piece, expert_z[1] = join(piece, expert_z[1])
    expert_z[2] = along(piece, 2)
    images, slots_lane, slots_row = join(images, slots_lane, slots_row)
    qkv, att, res, lse, tok, gates, full, small = forward_call(place, images, cotangent, dense, own_table)
    tok, gates, small, piece, spread_1, expert_z = join(tok, gates, small, piece, spread_1, expert_z)
    tables = (slots_lane, gates, small)

    spread_2 = spread(expert_z[2])
    expert_z[3] = along(piece, 3)
    outs[0] = expert_call(0, place, tok, *tables, ((expert_inner, expert_outer), None), spread_1)
    outs, tok, spread_2, expert_z = join(outs, tok, spread_2, expert_z)

    weights = (outs[0][4], across(outs[0][4], 1))
    cores[0] = across(outs[0][1], 1)
    spread_3 = spread(expert_z[3])
    outs[1] = expert_call(1, place, tok, *tables, (weights, sources), spread_2)
    outs, tok, cores, spread_3 = join(outs, tok, cores, spread_3)

    weights = (outs[1][4], across(outs[1][4], 1))
    cores[1] = across(outs[1][1], 1)
    chips[0] = send_chips(blend_call(*quarters(0)))
    outs[2] = expert_call(2, place, tok, *tables, (weights, sources), spread_3)
    outs, tok, cores, chips = join(outs, tok, cores, chips)

    weights = (outs[2][4], across(outs[2][4], 1))
    cores[2] = across(outs[2][1], 1)
    chips[1] = send_chips(blend_call(*quarters(1)))
    outs[3] = expert_call(3, place, tok, *tables, (weights, sources))
    outs, cores, chips, shards = join(outs, cores, chips, shards)

    cores[3] = across(outs[3][1], 1)
    chips[2] = send_chips(blend_call(*quarters(2)))
    pairs = [outs[k][2] for k in range(n_group)]
    biases = [outs[k][3] for k in range(n_group)]
    block_out, gres, gatt, late, shards[0], shards[1], *parts = combine_call(
        (own_quarter(0), own_quarter(1), *quarters(3), ("sum", [(outs[3][0], (0, 0)), (cores[3], (0, 0))])), place, cotangent, att, res, tok, slots_row, full, small, pairs, biases
    )
    gres, gatt, late, cores, chips, shards, parts = join(gres, gatt, late, cores, chips, shards, parts)

    *parts, local_3 = parts
    chips[3] = send_chips(parts)
    shards[2], = blend_call(own_quarter(2))
    passed = along(rest_of_replicas(shards.pop(2)), 1)
    for k in range(2):
        shards[k] = send_shard(k, shards[k])
    input_grad, keep, send = backward_call(place, images, qkv, lse, gres, gatt, full, small, late, n_group)
    keep, send, chips, shards, passed, local_3 = join(keep, send, chips, shards, passed, local_3)
    local_3 = [(local_3, ())] + [(v, ()) for v in chips[3]]
    if n_replica == PIECES:
        value, = blend_call(("sum", local_3 + [(passed, ())]))
    else:
        value = plus(rest_of_replicas(*blend_call(("sum", local_3))), passed)
    shards[3] = along(value, 1)

    value = plus(keep, across(send, 1))
    value = plus(value[0], *(across(value[pos], offset_of(pos)) for pos in range(1, PIECES // 2)))
    value = rest_of_replicas(value)
    total, = blend_call(("sum", [(v, ()) for v in shards.values()]))
    value, total = join(value, total)
    own_half = spread(total)
    value = value.reshape((2, 2) + value.shape[1:])
    value = plus(value[:, 0], between(value[:, 1], 1))
    value = plus(value[0], between(value[1], 2))
    value = spread(value)
    other_half = [across(v, 1) for v in own_half]
    grads = finish_call(0, place, own_half)
    grad_inner, grad_outer = finish_call(1, place, other_half, grads)
    value, grad_inner, grad_outer = join(value, grad_inner, grad_outer)
    value = jnp.stack(value)
    value = (value, across(value, 1))
    grad_qkv, grad_proj, grad_router, grad_inner_bias, grad_outer_bias, *rest = finish_dense_call(
        place, value, model, n_group, hidden
    )
    return (
        block_out, input_grad, rest[0], rest[1], grad_qkv, rest[5], grad_proj, rest[2], rest[3], rest[4],
        grad_router.T, grad_inner, grad_inner_bias, grad_outer, grad_outer_bias,
    )


def solution(mesh):
    both = ("replica", "group")
    in_specs = (
        P(both, None, None), P("group"), P("group"), P("group", None), P("group"), P("group", None),
        P("group"), P("group"), P("group"), P("group", None), P("group", None, None), P("group", None),
        P("group", None, None), P("group", None), P(both), P(both, None, None), P(both, None, None),
        P(both, None, None),
    )
    out_specs = (
        P(both, None, None), P(both, None, None), P("group"), P("group"), P("group", None), P("group"),
        P("group", None), P("group"), P("group"), P("group"), P("group", None), P("group", None, None),
        P("group", None), P("group", None, None), P("group", None),
    )
    body = functools.partial(local, n_replica=mesh.shape["replica"], n_group=mesh.shape["group"])
    return jax.shard_map(body, mesh=mesh, in_specs=in_specs, out_specs=out_specs, check_vma=False)
```
